32 devices in a mesh: gx: 2 (over x), gy: 4 (over y, core), gz: 4 (over z).
Axes of the slice: x: 2, y: 2, z: 4, core: 2. Of those that a mesh axis runs over, the one named last changes fastest.
Arguments:
- features: bfloat16 [32, 8, 256, 512], P(None, 'gz', 'gx', 'gy'), may hold values from -6 to 6
- conv_weight: bfloat16 [27, 32, 32], replicated, may hold values from -0.21875 to 0.21875
- conv_bias: float32 [32], replicated, may hold values from -3 to 3
- head_weight: bfloat16 [3, 32], replicated, may hold values from -3 to 3
- head_bias: float32 [3], replicated, may hold values from -3 to 3
- fragments: int32 [8, 256, 512], P('gz', 'gx', 'gy'), may hold values from 0 to 63
- edge_cells: int32 [2, 32768], P(None, ('gx', 'gy', 'gz')), may hold values from 0 to 16384, as said below
- edge_owner: int32 [32768, 1], P(('gx', 'gy', 'gz')), may hold values from 0 to 31; in each aligned block of 1024 rows (0 to 1023, 1024 to 2047, ...) at most 48 rows name the same one
- edge_count: int32 [32], P(('gx', 'gy', 'gz')), may hold values from 1 to 1024, 24576 in all
- recv_slot: int32 [32, 1536], P(('gx', 'gy', 'gz')), may hold values from 0 to 383
Outputs:
- affinity: bfloat16 [3, 8, 256, 512], P(None, 'gz', 'gx', 'gy')
- edge_mean: float32 [32, 384], P(('gx', 'gy', 'gz'))
The draws below stay inside these ranges and needn't reach their ends.
Inputs may be any that keep to these rules, and one draw needn't show every extreme that they name: `edge_cells`: each code is a 256 + c with a < 64 and c < 256, or 16384, which names the zero entry. `edge_owner`: at most 48 slots of one device name the same owner; some device has exactly 48 for one owner.
All inputs are finite; a program needn't handle non-finite values. No bound on the sum of `edge_count` on one device may be relied on, other than what follows from the above.
Results may differ from the reference program's by a relative error of at most 0.0041.
Values may be sent and summed in bfloat16 or wider, within the bound.
No kernel may reach another device: no remote copies, remote signals or barrier semaphores. Data moves between devices by JAX's collectives and lax.ppermute only.
A program may use at most 128 MiB of HBM per device.

```python
import math
import jax
import jax.numpy as jnp
import numpy as np
from jax import lax

C = 32
BZ = 2
BX = 128
BY = 128
F = 64
E_DEV = 1024
NZ = 8
NX = 256
NY = 512
EDGES = 32768
CAP = 48
OWN = 384
N_GX = 2
N_GY = 4
N_GZ = 4
DEVICES = 32


def draw_fragments(key, part):
    key = jax.random.fold_in(key, 5)
    keys = jax.random.split(key, 3)
    coarse = jax.random.randint(keys[0], (NZ, NX // 2, NY // 2), 0, F)
    blobs = jnp.repeat(jnp.repeat(coarse, 2, axis=1), 2, axis=2)
    scattered = jax.random.randint(keys[1], (NZ, NX, NY), 0, F)
    picked = jax.random.randint(keys[2], (NZ, NX, NY), 0, 5) < 2
    return jnp.where(picked, scattered, blobs).astype(jnp.int32)


def draw_edge_cells(key, part):
    key = jax.random.fold_in(key, 11)
    keys = jax.random.split(key, 5)
    first = jax.random.randint(keys[0], (EDGES,), 0, F)
    offset = jax.random.randint(keys[1], (EDGES,), 1, F)
    kinds = jax.random.randint(keys[2], (EDGES,), 0, 8)
    other = jax.random.randint(keys[3], (EDGES,), 0, F)
    sideways = jax.random.randint(keys[4], (EDGES,), 1, 3)
    second = (first + offset) % F
    along = jnp.where(kinds == 6, 0, sideways)
    inner = kinds < 6
    code_one = jnp.where(inner, first * (4 * F) + second, first * (4 * F) + F * (1 + along) + other)
    code_two = jnp.where(inner, second * (4 * F) + first, 4 * F * F)
    return jnp.stack([code_one, code_two]).astype(jnp.int32)


def with_ends(array, key, least, top_value):
    spot = [jax.random.randint(jax.random.fold_in(key, axis), (), 0, length) for axis, length in enumerate(array.shape)]
    longest = array.shape.index(max(array.shape))
    next_to = spot[:longest] + [(spot[longest] + 1) % array.shape[longest]] + spot[longest + 1:]
    return array.at[tuple(spot)].set(least).at[tuple(next_to)].set(top_value)


def block_scale(stream_key, shape, pieces, low, top_value):
    gain, own = 1.0, jax.random.fold_in(stream_key, 6)
    for dim, shards_of in pieces:
        draws = jnp.exp(jax.random.uniform(jax.random.fold_in(own, dim), (shards_of,), jnp.float32, low / len(pieces), top_value / len(pieces)))
        gain = gain * jnp.repeat(draws, shape[dim] // shards_of).reshape([-1 if axis == dim else 1 for axis in range(len(shape))])
    return gain


def profile(count, total, bound, lean):
    portions = [(1 << 20) // math.isqrt(rank ** lean) + 1 for rank in range(2, count + 1)]
    surplus, given = total - bound - (count - 1), [1] * (count - 1)
    while surplus > 0:
        movable = [i for i in range(count - 1) if given[i] < bound]
        mass, remaining = sum([portions[i] for i in movable]), surplus
        for i in movable:
            addition = min(bound - given[i], max(1, remaining * portions[i] // mass), surplus)
            given[i] = given[i] + addition
            surplus = surplus - addition
    return np.array([bound] + given)


def uneven_parts(own_key, number_of, total, most, lean):
    if number_of == 2:
        one = jax.random.randint(own_key, (), max(1, total - most), min(most, total - 1) + 1)
        return jnp.stack([one, total - one])
    lengths = jnp.asarray(profile(number_of, total, most, lean), jnp.int32)
    pairs = (number_of - 1) // 2
    giver, receiver = lengths[1:1 + 2 * pairs:2], lengths[2:2 + 2 * pairs:2]
    slack = jnp.minimum(giver - 1, most - receiver)
    moved = jax.random.randint(jax.random.fold_in(own_key, 1), (pairs,), 0, 1 << 20) % (slack + 1)
    lengths = lengths.at[1:1 + 2 * pairs:2].set(giver - moved).at[2:2 + 2 * pairs:2].set(receiver + moved)
    return lengths[jax.random.permutation(jax.random.fold_in(own_key, 2), number_of)]


def assign_block(rng, own, number, rows, count, top, most, lean):
    sequence = jax.random.permutation(rng, count)
    packed, ordinary = shares(count, rows * top, most, lean, True), shares(count, rows * top, most, lean, False)
    places = jnp.arange(count)

    def named(lengths, turn):
        used = int((lengths > 0).sum())
        fixed = max(1, used // 4)
        moved = fixed + (places - fixed + turn * (used - fixed)) % max(1, count - fixed)
        return jnp.zeros((count,), jnp.int32).at[sequence[jnp.where(places < fixed, places, moved)]].set(jnp.asarray(lengths, jnp.int32))

    lengths = jnp.where(number % 4 == 0, named(packed, number // 4), named(ordinary, number - number // 4 - 1))
    mixed = jax.random.permutation(jax.random.fold_in(own, 3), count)
    donor, sink = mixed[0:count // 2 * 2:2], mixed[1:count // 2 * 2:2]
    margin = jnp.minimum(lengths[donor] - 1, most - lengths[sink]) // 2
    margin = jnp.where((donor == sequence[0]) | (sink == sequence[0]) | (lengths[sink] == 0), 0, jnp.maximum(margin, 0))
    moved = jax.random.randint(jax.random.fold_in(own, 4), (count // 2,), 0, 1 << 20) % (margin + 1)
    lengths = lengths.at[donor].add(-moved).at[sink].add(moved)
    labels = jnp.searchsorted(jnp.cumsum(lengths), jnp.arange(rows * top), side="right").astype(jnp.int32)
    grid = labels.reshape(top, rows).T
    grid = grid[jax.random.permutation(jax.random.fold_in(own, 1), rows)]
    turn = jax.random.randint(jax.random.fold_in(own, 2), (rows, 1), 0, top)
    return jnp.take_along_axis(grid, (jnp.arange(top)[None, :] + turn) % top, axis=1)


def shares(count, total, limit, slope, full):
    weights = [(1 << 20) // math.isqrt(standing ** slope) + 1 for standing in range(1, count + 1)]
    largest = limit if full else min(limit, max(-(-total // count), total * weights[0] // sum(weights)))
    least = 1 if total - largest >= count - 1 else 0
    holding, spare = [largest] + [least] * (count - 1), total - largest - least * (count - 1)
    while spare > 0:
        candidates = [i for i in range(1, count) if holding[i] < largest] or [i for i in range(1, count) if holding[i] < limit]
        mass, budget = sum([weights[i] for i in candidates]), spare
        for i in candidates:
            addition = min(limit - holding[i], max(1, budget * weights[i] // mass), spare)
            holding[i] = holding[i] + addition
            spare = spare - addition
    return np.array(holding)


def centred(key, extent, spread, limit, cuts=(), kind=jnp.bfloat16):
    level = block_scale(key, extent, cuts, -0.22, 0.18) if cuts else 1.0
    drawn = jax.random.normal(key, extent, jnp.float32) * spread * level
    return jnp.minimum(jnp.maximum(drawn, -limit), limit).astype(kind)


def setup_inputs(seed: int = 0) -> dict:
    key_of = jax.random.split(jax.random.key(seed), 11)
    features = centred(key_of[0], (C, NZ, NX, NY), 1.0, 6.0, ((1, 4), (2, 2), (3, 4)))
    conv_weight = centred(key_of[1], (27, C, C), (27 * C) ** -0.5, 0.21875)
    conv_bias = centred(key_of[2], (C,), 0.5, 3.0, (), jnp.float32)
    head_weight = centred(key_of[3], (3, C), 0.5, 3.0)
    head_bias = centred(key_of[4], (3,), 1.0, 3.0, (), jnp.float32)
    fragments = draw_fragments(jax.random.fold_in(key_of[10], 71), 0)
    edge_cells = draw_edge_cells(jax.random.fold_in(key_of[10], 71), 0)
    edge_owner_keys = jax.random.split(jax.random.fold_in(key_of[7], 1), EDGES // E_DEV)
    edge_owner_turns = jax.random.permutation(jax.random.fold_in(key_of[7], 3), EDGES // E_DEV)
    edge_owner = jax.vmap(lambda own, number: assign_block(jax.random.fold_in(key_of[7], 2), own, number, E_DEV, DEVICES, 1, CAP, 1))(edge_owner_keys, edge_owner_turns).reshape((EDGES, 1))
    edge_count = uneven_parts(key_of[8], DEVICES, DEVICES * E_DEV * 3 // 4, E_DEV, 2).astype(jnp.int32)
    recv_slot = with_ends(jax.random.randint(key_of[9], (DEVICES, DEVICES * CAP), 0, OWN), jax.random.fold_in(key_of[9], 1), 0, OWN - 1).astype(jnp.int32)
    return dict(features=features, conv_weight=conv_weight, conv_bias=conv_bias, head_weight=head_weight, head_bias=head_bias, fragments=fragments, edge_cells=edge_cells, edge_owner=edge_owner, edge_count=edge_count, recv_slot=recv_slot)


def pair_table(own_frag, codes, values):
    valid = codes >= 0
    index = jnp.where(valid, own_frag * (4 * F) + codes, 4 * F * F).reshape(-1)
    sums = jax.ops.segment_sum(jnp.where(valid, values, 0.0).reshape(-1), index, num_segments=4 * F * F + 1)
    counts = jax.ops.segment_sum(valid.astype(jnp.float32).reshape(-1), index, num_segments=4 * F * F + 1)
    return sums.at[4 * F * F].set(0.0), counts.at[4 * F * F].set(0.0)


def code_of(partner, along, axis_code):
    line = lax.broadcasted_iota(jnp.int32, partner.shape, along)
    outer = jnp.where(partner >= 0, F * (1 + axis_code) + partner, -1)
    return jnp.where(line >= 1, partner, outer).astype(jnp.int32)


def reference(features, conv_weight, conv_bias, head_weight, head_bias, fragments, edge_cells, edge_owner, edge_count, recv_slot):
    kernel = conv_weight.astype(jnp.float32).reshape(3, 3, 3, C, C).transpose(3, 4, 0, 1, 2)
    padded = jnp.pad(features, ((0, 0), (1, 1), (1, 1), (1, 1)))
    frag_pad = jnp.pad(fragments, ((1, 0), (1, 0), (1, 0)), constant_values=-1)
    zero = jnp.zeros((), jnp.int32)
    owners_all = edge_owner[:, 0]

    def device_block(device):
        index_z = device % N_GZ
        index_y = (device // N_GZ) % N_GY
        index_x = device // (N_GZ * N_GY)
        start_z = (index_z * BZ).astype(jnp.int32)
        start_x = (index_x * BX).astype(jnp.int32)
        start_y = (index_y * BY).astype(jnp.int32)
        window = lax.dynamic_slice(padded, (zero, start_z, start_x, start_y), (C, BZ + 2, BX + 2, BY + 2)).astype(jnp.float32)
        pre_act = lax.conv_general_dilated(window[None], kernel, (1, 1, 1), "VALID", dimension_numbers=("NCDHW", "OIDHW", "NCDHW"), precision=lax.Precision.HIGHEST)[0]
        hidden = jnp.maximum(pre_act + conv_bias[:, None, None, None], 0.0).astype(jnp.bfloat16)
        logits = jnp.einsum("oc,czxy->ozxy", head_weight.astype(jnp.float32), hidden.astype(jnp.float32), precision=lax.Precision.HIGHEST) + head_bias[:, None, None, None]
        affinity = jax.nn.sigmoid(logits).astype(jnp.bfloat16)
        own_frag = lax.dynamic_slice(fragments, (start_z, start_x, start_y), (BZ, BX, BY))
        lower_frag = lax.dynamic_slice(frag_pad, (start_z, start_x, start_y), (BZ + 1, BX + 1, BY + 1))
        partners = (lower_frag[:BZ, 1:, 1:], lower_frag[1:, :BX, 1:], lower_frag[1:, 1:, :BY])
        table_sum = jnp.zeros((4 * F * F + 1,), jnp.float32)
        table_count = jnp.zeros((4 * F * F + 1,), jnp.float32)
        for along in range(3):
            codes = code_of(partners[along], along, along)
            sums, counts = pair_table(own_frag, codes, affinity[along].astype(jnp.float32))
            table_sum = table_sum + sums
            table_count = table_count + counts
        cells = lax.dynamic_slice(edge_cells, (zero, (device * E_DEV).astype(jnp.int32)), (2, E_DEV))
        live_mask = (jnp.arange(E_DEV, dtype=jnp.int32) < edge_count[device]).astype(jnp.float32)
        part_sum = (table_sum[cells[0]] + table_sum[cells[1]]) * live_mask
        part_count = (table_count[cells[0]] + table_count[cells[1]]) * live_mask
        owners = lax.dynamic_slice(owners_all, ((device * E_DEV).astype(jnp.int32),), (E_DEV,))
        owner_hot = (owners[:, None] == jnp.arange(DEVICES, dtype=jnp.int32)[None, :]).astype(jnp.int32)
        owner_rank = jnp.sum(jnp.cumsum(owner_hot, axis=0) * owner_hot, axis=1) - 1
        position = (owners * CAP + owner_rank).astype(jnp.int32)
        outgoing = jnp.zeros((2, DEVICES * CAP), jnp.float32).at[:, position].add(jnp.stack([part_sum, part_count]))
        return affinity, outgoing

    affinity_all, outgoing_all = lax.map(device_block, jnp.arange(DEVICES, dtype=jnp.int32))
    affinity_whole = affinity_all.reshape(N_GX, N_GY, N_GZ, 3, BZ, BX, BY).transpose(3, 2, 4, 0, 5, 1, 6).reshape(3, NZ, NX, NY)
    received = outgoing_all.reshape(DEVICES, 2, DEVICES, CAP).transpose(2, 1, 0, 3).reshape(DEVICES, 2, DEVICES * CAP)

    def settle(incoming, slots):
        totals = jax.ops.segment_sum(incoming.T, slots, num_segments=OWN)
        return totals[:, 0] / jnp.maximum(totals[:, 1], 1.0)

    edge_mean = jax.vmap(settle)(received, recv_slot)
    return affinity_whole, edge_mean
```

```python
import jax
import jax.numpy as jnp
from jax import lax
from jax.experimental import pallas as pl
from jax.experimental.pallas import tpu as pltpu
from jax.sharding import PartitionSpec as P

F = 64
LANES = 128
BF = jnp.bfloat16
F32 = jnp.float32
VMEM = pl.BlockSpec(memory_space=pltpu.VMEM)
SMEM = pl.BlockSpec(memory_space=pltpu.SMEM)


def params():
    return pltpu.CompilerParams(vmem_limit_bytes=48 << 20)


def cost(flops, nbytes):
    return pl.CostEstimate(flops=flops, bytes_accessed=nbytes, transcendentals=0)


def exchange(up, down, axis):
    n = lax.axis_size(axis)
    if n == 1:
        return jnp.zeros_like(up), jnp.zeros_like(down)
    if n == 2 and up.shape == down.shape:
        first = lax.axis_index(axis) == 0
        got = lax.ppermute(jnp.where(first, up, down), axis, [(0, 1), (1, 0)])
        none = jnp.zeros_like(got)
        return jnp.where(first, none, got), jnp.where(first, got, none)
    forward = [(i, i + 1) for i in range(n - 1)]
    backward = [(i + 1, i) for i in range(n - 1)]
    return lax.ppermute(up, axis, forward), lax.ppermute(down, axis, backward)


def spread(stage, zi, src, row_low, row_high, col_low, col_high):
    lane = lax.broadcasted_iota(jnp.int32, (32, LANES), 1)
    is_first = lane == 0
    is_last = lane == LANES - 1

    def put(x, centre, low, high):
        stage[1, zi, x] = centre
        stage[0, zi, x] = jnp.where(is_first, low, pltpu.roll(centre, 1, 1))
        stage[2, zi, x] = jnp.where(is_last, high, pltpu.roll(centre, LANES - 1, 1))

    put(0, row_low, col_low[:, LANES:], pltpu.roll(col_high[:, LANES:], LANES - 1, 1))
    put(
        LANES + 1,
        row_high,
        pltpu.roll(col_low[:, LANES:], LANES - 1, 1),
        pltpu.roll(col_high[:, LANES:], LANES - 2, 1),
    )
    low0 = col_low[:, :LANES]
    high0 = pltpu.roll(col_high[:, :LANES], LANES - 1, 1)

    def body(t, carry):
        low, high = carry
        block = jnp.swapaxes(src[:, pl.ds(pl.multiple_of(16 * t, 16), 16), :], 0, 1)
        for j in range(16):
            put(16 * t + j + 1, block[j], low, high)
            low = pltpu.roll(low, LANES - 1, 1)
            high = pltpu.roll(high, LANES - 1, 1)
        return low, high

    lax.fori_loop(0, 8, body, (low0, high0))


def toeplitz(weight_ref, out_ref, planes):
    quarter = lax.broadcasted_iota(jnp.int32, (32, LANES), 1) // 32
    zero = jnp.zeros((32, LANES), BF)
    for zo in range(2):
        for xo in range(4):
            row = 32 * (4 * zo + xo)
            for chunk in range(9):
                tile = zero
                for q in range(4):
                    place = 4 * chunk + q
                    dy, rest = divmod(place, 12)
                    plane, xi = divmod(rest, 6)
                    dz, dx = planes[plane] - zo, xi - 1 - xo
                    if abs(dz) <= 1 and abs(dx) <= 1:
                        weight = weight_ref[9 * (dz + 1) + 3 * (dx + 1) + dy]
                        tile = jnp.where(quarter == q, weight, tile)
                out_ref[row : row + 32, LANES * chunk : LANES * (chunk + 1)] = tile


def window(stage, x):
    return jnp.concatenate(
        [
            stage[:, :, pl.ds(x, 6)].reshape(1152, LANES),
            stage[:, :, pl.ds(x + 4, 6)].reshape(1152, LANES),
        ],
        axis=1,
    )


def own_planes_kernel(feat, rows, cols, weight, bias, acc, outer_weight, stage, inner_weight):
    toeplitz(weight, inner_weight, (0, 1))
    toeplitz(weight, outer_weight, (-1, 2))
    for z in range(2):
        spread(
            stage,
            z,
            feat.at[:, z],
            rows[0, 32 * z : 32 * z + 32],
            rows[1, 32 * z : 32 * z + 32],
            cols[0, 32 * z : 32 * z + 32],
            cols[1, 32 * z : 32 * z + 32],
        )
    bias_block = jnp.broadcast_to(bias[...], (256, 2 * LANES))

    def body(p, _):
        acc[p] = bias_block + jnp.dot(
            inner_weight[...], window(stage, 8 * p), preferred_element_type=F32
        )
        return 0

    lax.fori_loop(0, 16, body, 0)


def row_of(ref, z, x, copies):
    one = jnp.broadcast_to(ref[z, pl.ds(x, 1), :], (16, LANES)).astype(BF)
    return jnp.concatenate([one] * copies, axis=0)


def outer_product(left, right):
    return lax.dot_general(left, right, (((1,), (1,)), ((), ())), preferred_element_type=F32)


def table_rows(t, frag, ycode, weight_row, own_hot, pair_hot, extra):
    one = jnp.ones((F, LANES), BF)
    none = jnp.zeros((F, LANES), BF)
    iota = lax.broadcasted_iota(jnp.int32, (F, LANES), 0).astype(F32).astype(BF)
    iota2 = lax.broadcasted_iota(jnp.int32, (2 * F, LANES), 0).astype(F32).astype(BF)
    none2 = jnp.zeros((2 * F, LANES), BF)
    for j in range(16):
        x = 16 * t + j
        spot = slice(LANES * j, LANES * (j + 1))
        before = jnp.maximum(x - 1, 0)
        live = jnp.where(x > 0, 0.0, -1.0).astype(F32)
        hot = [row_of(frag, z, x, 4) == iota for z in range(2)]
        for z in range(2):
            own_hot[z, :, spot] = jnp.where(hot[z], one, none)
            earlier = jnp.broadcast_to(
                jnp.where(live < 0, live, frag[z, pl.ds(before, 1), :]), (16, LANES)
            ).astype(BF)
            earlier = jnp.concatenate([earlier] * 4, axis=0) == iota
            pair_hot[z, 0:F, spot] = jnp.where(earlier, weight_row(1, z, x, 4), none)
            pair_hot[z, F : 3 * F, spot] = jnp.where(
                row_of(ycode, z, x, 8) == iota2, weight_row(2, z, x, 8), none2
            )
        pair_hot[1, 3 * F : 4 * F, spot] = jnp.where(hot[0], weight_row(0, 1, x, 4), none)
        extra(x, spot, iota, none)


def first_line(frag, xcode, weight_row):
    none = jnp.zeros((F, LANES), BF)
    iota = lax.broadcasted_iota(jnp.int32, (F, LANES), 0).astype(F32).astype(BF)
    one = jnp.ones((F, LANES), BF)
    left = [jnp.where(row_of(frag, z, 0, 4) == iota, one, none) for z in range(2)]
    right = [
        jnp.where(row_of(xcode, z, 0, 4) == iota, weight_row(1, z, 0, 4), none) for z in range(2)
    ]
    return outer_product(jnp.concatenate(left, axis=1), jnp.concatenate(right, axis=1))


def count_kernel(frag, ycode, xcode, out, own_hot, pair_hot):
    def ones(d, z, x, copies):
        return jnp.ones((16 * copies, LANES), BF)

    def body(t, carry):
        low, high = carry
        table_rows(t, frag, ycode, ones, own_hot, pair_hot, lambda *_: None)
        low = low + outer_product(own_hot[0], pair_hot[0, : 3 * F])
        high = high + outer_product(own_hot[1], pair_hot[1, : 4 * F])
        return low, high

    low, high = lax.fori_loop(
        0, 8, body, (jnp.zeros((F, 3 * F), F32), jnp.zeros((F, 4 * F), F32))
    )
    both = low + high[:, : 3 * F]
    own = both[:, :F] + both[:, F : 2 * F] + high[:, 3 * F :]
    out[...] = jnp.concatenate(
        [own, jnp.zeros((F, F), F32), first_line(frag, xcode, ones), both[:, 2 * F :]], axis=1
    )


def rank_kernel(owner, out):
    slots = owner.shape[1]
    devices = out.shape[0]
    hot = lax.broadcasted_iota(jnp.int32, (devices, slots), 0) == owner[...]
    before = (
        lax.broadcasted_iota(jnp.int32, (slots, slots), 0)
        < lax.broadcasted_iota(jnp.int32, (slots, slots), 1)
    )
    earlier = jnp.dot(
        jnp.where(hot, 1.0, 0.0).astype(BF),
        jnp.where(before, 1.0, 0.0).astype(BF),
        preferred_element_type=F32,
    )
    rank = jnp.sum(jnp.where(hot, earlier, 0.0), axis=0, keepdims=True)
    out[...] = jnp.broadcast_to(rank, out.shape)


def halves(value):
    high = value.astype(BF)
    return high, (value - high.astype(F32)).astype(BF)


def finish_kernel(
    acc,
    below,
    above,
    ring_low,
    ring_high,
    outer_weight,
    head,
    head_bias,
    frag,
    ycode,
    xcode,
    zlive,
    counts,
    cells,
    owner,
    rank,
    edge_count,
    affinity,
    outgoing,
    stage,
    kept,
    own_hot,
    pair_hot,
    zcode,
):
    for i, (plane, ring) in enumerate(((below, ring_low), (above, ring_high))):
        spread(
            stage,
            i,
            plane,
            ring[0:32],
            ring[32:64],
            jnp.concatenate([ring[64:96], ring[96:128]], axis=1),
            jnp.concatenate([ring[128:160], ring[160:192]], axis=1),
        )
    zcode[0] = jnp.where(zlive[...] > 0, ring_low[192:320].astype(F32), -1.0)
    bias_block = jnp.broadcast_to(head_bias[...], (48, LANES))
    top_half = (lax.broadcasted_iota(jnp.int32, (48, LANES), 0) % 8) < 4

    def weight_row(d, z, x, copies):
        return row_of(kept, 2 * d + z, x, copies)

    def z_outer(x, spot, iota, none):
        hot = row_of(zcode, 0, x, 4) == iota
        pair_hot[0, 3 * F : 4 * F, spot] = jnp.where(hot, weight_row(0, 0, x, 4), none)
        pair_hot[0, 4 * F :, spot] = jnp.where(hot, jnp.ones((F, LANES), BF), none)

    def body(t, carry):
        low, high = carry
        for half in range(2):
            p = 2 * t + half
            total = acc[p] + jnp.dot(
                outer_weight[...], window(stage, 8 * p), preferred_element_type=F32
            )
            hidden = jnp.maximum(total, 0.0).astype(BF)
            logits = jnp.dot(head[...], hidden, preferred_element_type=F32)
            logits = jnp.where(top_half, logits[:, :LANES], logits[:, LANES:]) + bias_block
            value = jax.nn.sigmoid(logits).astype(BF).astype(F32)
            for i in range(6):
                kept[i, pl.ds(pl.multiple_of(8 * p, 8), 8), :] = value[8 * i : 8 * i + 8]
        lines = pl.ds(pl.multiple_of(16 * t, 16), 16)
        for i in range(6):
            affinity[i // 2, i % 2, lines, :] = kept[i, lines, :].astype(BF)
        table_rows(t, frag, ycode, weight_row, own_hot, pair_hot, z_outer)
        low = low + outer_product(own_hot[0], pair_hot[0])
        high = high + outer_product(own_hot[1], pair_hot[1, : 4 * F])
        return low, high

    low, high = lax.fori_loop(
        0, 8, body, (jnp.zeros((F, 5 * F), F32), jnp.zeros((F, 4 * F), F32))
    )
    both = low[:, : 3 * F] + high[:, : 3 * F]
    own = both[:, :F] + both[:, F : 2 * F] + high[:, 3 * F :]
    sums = jnp.concatenate(
        [own, low[:, 3 * F : 4 * F], first_line(frag, xcode, weight_row), both[:, 2 * F :]], axis=1
    )
    tally = counts[...] + jnp.concatenate(
        [jnp.zeros((F, F), F32), low[:, 4 * F :], jnp.zeros((F, 2 * F), F32)], axis=1
    )
    slots = cells.shape[1]
    code = jnp.concatenate([cells[0:1, :], cells[1:2, :]], axis=1)
    column = (code & (4 * F - 1)).astype(F32)
    line = code >> 8
    column_hot = jnp.where(
        lax.broadcasted_iota(jnp.int32, (4 * F, 2 * slots), 0).astype(F32) == column, 1.0, 0.0
    ).astype(BF)
    picked = jnp.dot(
        jnp.concatenate(halves(sums) + halves(tally), axis=0),
        column_hot,
        preferred_element_type=F32,
    )
    line_hot = lax.broadcasted_iota(jnp.int32, (F, 2 * slots), 0) == line
    alive = lax.broadcasted_iota(jnp.int32, (1, slots), 1) < edge_count[0]

    def part(value):
        total = jnp.sum(jnp.where(line_hot, value, 0.0), axis=0, keepdims=True)
        return jnp.where(alive, total[:, :slots] + total[:, slots:], 0.0)

    part_sum = part(picked[:F] + picked[F : 2 * F])
    part_count = part(picked[2 * F : 3 * F] + picked[3 * F :])
    devices = outgoing.shape[0]
    to_owner = lax.broadcasted_iota(jnp.int32, (devices, slots), 0) == owner[...]
    lanes = lax.broadcasted_iota(jnp.int32, (LANES, slots), 0)
    place = rank[0:1, :].astype(jnp.int32)
    low_hot = jnp.where(lanes == place, 1.0, 0.0).astype(BF)
    high_hot = jnp.where(lanes == place + F, 1.0, 0.0).astype(BF)
    left = [
        jnp.where(to_owner, piece.astype(F32), 0.0).astype(BF)
        for piece in halves(part_sum) + halves(part_count)
    ]
    sent = outer_product(
        jnp.concatenate(left, axis=1),
        jnp.concatenate([low_hot, low_hot, high_hot, high_hot], axis=1),
    )
    outgoing[...] = sent.reshape(outgoing.shape)


def settle_kernel(received, slot, out, left, right):
    devices = received.shape[0]
    groups = out.shape[1] // LANES
    iota = lax.broadcasted_iota(jnp.int32, (LANES, LANES), 0)
    row = lax.broadcasted_iota(jnp.int32, (16, LANES), 0)
    lane = lax.broadcasted_iota(jnp.int32, (16, LANES), 1)
    of_count = row >= 2 * groups
    inner = jnp.where(of_count, row - 2 * groups, row)
    is_low = inner >= groups
    group = jnp.where(is_low, inner - groups, inner)
    group = jnp.where((lane >= F) == of_count, group, -1)
    group = jnp.where(row < 4 * groups, group, -1)

    def body(p, _):
        spot = pl.ds(pl.multiple_of(p * LANES, LANES), LANES)
        code = slot[pl.ds(p, 1), :]
        value = received[p]
        high = value.astype(BF).astype(F32)
        piece = jnp.where(is_low, value - high, high)
        left[:, spot] = jnp.where((code >> 7) == group, piece, 0.0).astype(BF)
        right[:, spot] = jnp.where((code & (LANES - 1)) == iota, 1.0, 0.0).astype(BF)
        return 0

    lax.fori_loop(0, devices, body, 0, unroll=8)
    total = outer_product(left[...], right[...])
    for g in range(groups):
        total_sum = total[g : g + 1] + total[groups + g : groups + g + 1]
        total_count = total[2 * groups + g : 2 * groups + g + 1] + total[3 * groups + g : 3 * groups + g + 1]
        out[:, LANES * g : LANES * (g + 1)] = total_sum / jnp.maximum(total_count, 1.0)


def shards(
    features,
    conv_weight,
    conv_bias,
    head_weight,
    head_bias,
    fragments,
    edge_cells,
    edge_owner,
    edge_count,
    recv_slot,
):
    axes = ("gx", "gy", "gz")
    devices = lax.axis_size("gx") * lax.axis_size("gy") * lax.axis_size("gz")
    capacity = recv_slot.shape[1] // devices
    slots = edge_cells.shape[1]
    own_slots = devices * capacity // 4
    frag_bf = fragments.astype(BF)
    frag = fragments.astype(F32)

    below, above = exchange(features[:, 1], features[:, 0], "gz")

    def packed(value):
        return value.transpose(1, 0, 2).reshape(64, LANES)

    def rows16(value):
        return jnp.pad(value, ((0, 16 - value.shape[0]), (0, 0)))

    x_up = jnp.concatenate([packed(features[:, :, -1, :]), rows16(frag_bf[:, -1, :])], 0)
    x_down = jnp.concatenate([packed(features[:, :, 0, :]), jnp.zeros((16, LANES), BF)], 0)
    x_low, x_high = exchange(x_up, x_down, "gx")
    rows = jnp.stack([x_low[:64], x_high[:64]])

    def columns(at, last):
        main = jnp.concatenate([packed(features[:, :, :, at]), last], 0)
        ends = jnp.concatenate([rows[0, :, at, None], rows[1, :, at, None]], 1)
        return jnp.concatenate([main, jnp.pad(ends, ((0, 16), (0, LANES - 2)))], 1)

    y_low, y_high = exchange(
        columns(-1, rows16(frag_bf[:, :, -1])), columns(0, jnp.zeros((16, LANES), BF)), "gy"
    )
    cols = jnp.stack([y_low[:64], y_high[:64]])

    def ring(z):
        lines = slice(32 * z, 32 * z + 32)
        return [
            rows[0, lines],
            rows[1, lines],
            cols[0, lines, :LANES],
            cols[0, lines, LANES:],
            cols[1, lines, :LANES],
            cols[1, lines, LANES:],
        ]

    ring_low, ring_high = exchange(
        jnp.concatenate(ring(1) + [frag_bf[1]], 0), jnp.concatenate(ring(0), 0), "gz"
    )

    first_x = lax.axis_index("gx") > 0
    first_y = lax.axis_index("gy") > 0
    first_z = lax.axis_index("gz") > 0
    xcode = jnp.where(first_x, x_low[64:66].astype(F32), -1.0)[:, None, :]
    y_outer = jnp.where(first_y, y_low[64:66, :LANES].astype(F32) + F, -1.0)[:, :, None]
    ycode = jnp.concatenate([y_outer, frag[:, :, :-1]], 2)
    zlive = jnp.broadcast_to(first_z.astype(F32), (1, LANES))

    weight4 = jnp.tile(conv_weight, (1, 1, 4))
    bias_col = jnp.tile(conv_bias, 8)[:, None]
    line = jnp.arange(48)
    step = jnp.arange(256)
    match = ((line[:, None] // 8) % 2 == step[None, :] // 128) & (
        line[:, None] % 4 == (step[None, :] // 32) % 4
    )
    head = jnp.where(match, jnp.tile(jnp.repeat(head_weight, 16, axis=0), (1, 8)), 0).astype(BF)
    head_col = jnp.repeat(head_bias, 16)[:, None]

    acc, outer_weight = pl.pallas_call(
        own_planes_kernel,
        out_shape=(
            jax.ShapeDtypeStruct((16, 256, 256), F32),
            jax.ShapeDtypeStruct((256, 1152), BF),
        ),
        in_specs=[VMEM] * 5,
        out_specs=(VMEM, VMEM),
        scratch_shapes=[pltpu.VMEM((3, 2, 130, 32, LANES), BF), pltpu.VMEM((256, 1152), BF)],
        compiler_params=params(),
        cost_estimate=cost(10_000_000_000, 8 << 20),
        name="own_planes",
    )(features, rows, cols, weight4, bias_col)

    counts = pl.pallas_call(
        count_kernel,
        out_shape=jax.ShapeDtypeStruct((F, 4 * F), F32),
        in_specs=[VMEM] * 3,
        out_specs=VMEM,
        scratch_shapes=[pltpu.VMEM((2, F, 2048), BF), pltpu.VMEM((2, 4 * F, 2048), BF)],
        compiler_params=params(),
        cost_estimate=cost(5_000_000_000, 1 << 20),
        name="pair_counts",
    )(frag, ycode, xcode)

    owner = edge_owner.reshape(1, slots)
    rank = pl.pallas_call(
        rank_kernel,
        out_shape=jax.ShapeDtypeStruct((devices, slots), F32),
        in_specs=[VMEM],
        out_specs=VMEM,
        compiler_params=params(),
        cost_estimate=cost(1_000_000_000, 1 << 20),
        name="owner_rank",
    )(owner)

    affinity, outgoing = pl.pallas_call(
        finish_kernel,
        out_shape=(
            jax.ShapeDtypeStruct((3, 2, LANES, LANES), BF),
            jax.ShapeDtypeStruct((devices, 1, LANES), F32),
        ),
        in_specs=[VMEM] * 16 + [SMEM],
        out_specs=(VMEM, VMEM),
        scratch_shapes=[
            pltpu.VMEM((3, 2, 130, 32, LANES), BF),
            pltpu.VMEM((6, LANES, LANES), F32),
            pltpu.VMEM((2, F, 2048), BF),
            pltpu.VMEM((2, 5 * F, 2048), BF),
            pltpu.VMEM((1, LANES, LANES), F32),
        ],
        compiler_params=params(),
        cost_estimate=cost(10_000_000_000, 8 << 20),
        name="finish",
    )(
        acc,
        below,
        above,
        ring_low,
        ring_high,
        outer_weight,
        head,
        head_col,
        frag,
        ycode,
        xcode,
        zlive,
        counts,
        edge_cells,
        owner,
        rank,
        edge_count,
    )

    received = lax.all_to_all(outgoing, axes, split_axis=0, concat_axis=0, tiled=True)

    slot = recv_slot.reshape(devices, capacity)
    slot = jnp.pad(slot, ((0, 0), (0, F - capacity)), constant_values=-256)
    slot = jnp.concatenate([slot, slot], 1)
    edge_mean = pl.pallas_call(
        settle_kernel,
        out_shape=jax.ShapeDtypeStruct((1, own_slots), F32),
        in_specs=[VMEM] * 2,
        out_specs=VMEM,
        scratch_shapes=[
            pltpu.VMEM((16, devices * LANES), BF),
            pltpu.VMEM((LANES, devices * LANES), BF),
        ],
        compiler_params=params(),
        name="settle",
    )(received, slot)
    return affinity, edge_mean


def solution(mesh):
    in_specs = (
        P(None, "gz", "gx", "gy"),
        P(),
        P(),
        P(),
        P(),
        P("gz", "gx", "gy"),
        P(None, ("gx", "gy", "gz")),
        P(("gx", "gy", "gz"), None),
        P(("gx", "gy", "gz")),
        P(("gx", "gy", "gz"), None),
    )
    out_specs = (P(None, "gz", "gx", "gy"), P(("gx", "gy", "gz"), None))
    return jax.shard_map(shards, mesh=mesh, in_specs=in_specs, out_specs=out_specs, check_vma=False)
```

```python
import jax
import jax.numpy as jnp
from jax import lax
from jax.experimental import pallas as pl
from jax.experimental.pallas import tpu as pltpu
from jax.sharding import PartitionSpec as P

F = 64
LANES = 128
GROUPS = 32
TILES = GROUPS + 1
WIDE = TILES * LANES
STACK = 8
STEP = LANES + 8
EDGE = 48
BF = jnp.bfloat16
F32 = jnp.float32
VMEM = pl.BlockSpec(memory_space=pltpu.VMEM)
SMEM = pl.BlockSpec(memory_space=pltpu.SMEM)


def call(kernel, name, out_shape, args, smem, scratch=(), flops=1_000_000):
    return pl.pallas_call(
        kernel,
        out_shape=out_shape,
        in_specs=[VMEM] * (len(args) - smem) + [SMEM] * smem,
        out_specs=jax.tree.map(lambda _: VMEM, out_shape),
        scratch_shapes=list(scratch),
        compiler_params=pltpu.CompilerParams(vmem_limit_bytes=48 << 20),
        cost_estimate=pl.CostEstimate(flops=flops, bytes_accessed=1 << 20, transcendentals=0),
        name=name,
    )(*args)


def shape(dims, dtype):
    return jax.ShapeDtypeStruct(dims, dtype)


def iota(dims, axis):
    return lax.broadcasted_iota(jnp.int32, dims, axis)


def outer_product(left, right):
    return lax.dot_general(left, right, (((1,), (1,)), ((), ())), preferred_element_type=F32)


def halves(value):
    high = value.astype(BF)
    return high, (value - high.astype(F32)).astype(BF)


def layout_kernel(feat, frag, flags, low, high, x_up, x_down, edge, first_col, rows):
    first = flags[0] == 0
    zero = jnp.zeros((32, LANES), BF)
    for z, plane in ((1, high), (0, low)):
        last = zero
        for t in range(8):
            block = jnp.swapaxes(feat[:, z, 16 * t : 16 * t + 16, :], 0, 1).reshape(512, LANES)
            turned = jnp.concatenate([last, block[:480]], axis=0).T
            last = block[480:]
            plane[:, 512 * t : 512 * t + 512] = turned
            for side, line in ((0, turned[112:128].astype(F32)[15:16]), (1, turned[0:16].astype(F32)[0:1])):
                for q in range(4):
                    spot = 4 * t + q
                    rows[2 * side + z, spot : spot + 1, :] = line[:, LANES * q : LANES * (q + 1)]
            if t == 0:
                tile_zero = turned[:, :LANES]
        end = jnp.concatenate([last, zero, zero, zero], axis=0).T
        plane[:, WIDE - LANES : WIDE] = end
        rows[z, TILES - 1 : TILES, :] = end[112:128].astype(F32)[15:16]
        rows[2 + z, TILES - 1 : TILES, :] = end[0:16].astype(F32)[0:1]
        x_up[LANES * z : LANES * (z + 1), :] = jnp.where(first, end, tile_zero)
        x_down[LANES * z : LANES * (z + 1), :] = tile_zero
        turned = frag[z].astype(F32).T
        first_col[z : z + 1, :] = turned[0:1]
        for side in range(2):
            rows[2 * side + z, TILES:EDGE, :] = jnp.broadcast_to(turned[127:128], (EDGE - TILES, LANES))
            edge[2 * side + z] = rows[2 * side + z].astype(BF)
    high[:, WIDE:] = frag[1].astype(F32).astype(BF)
    lines = [jnp.broadcast_to(frag[z, 127:128, :], (8, LANES)).astype(F32) for z in range(2)]
    x_up[2 * LANES :, :] = jnp.concatenate(lines, axis=0).astype(BF)
    x_down[2 * LANES :, :] = jnp.zeros((16, LANES), BF)


def x_face_kernel(low, high, edge, flags, face, x_code, y_up, y_down):
    has_low, has_high = flags[0] > 0, flags[1] > 0
    lane = iota((LANES, LANES), 1)
    is_low = (lane < 32) & has_low
    is_high = (lane >= 32) & (lane < 64) & has_high
    none = jnp.zeros((LANES, LANES), BF)
    for z in range(2):
        lines = slice(LANES * z, LANES * (z + 1))
        tile = jnp.where(is_low, low[lines, :], jnp.where(is_high, high[lines, :], none))
        face[z] = tile
        for side, out in ((0, y_up), (1, y_down)):
            near = (tile[112:128].astype(F32)[15:16], tile[0:16].astype(F32)[0:1])[side]
            line = edge[2 * side + z].astype(F32)
            row, place = iota((EDGE, LANES), 0), iota((EDGE, LANES), 1)
            ends = ((row == 0) & (place < 32)) | ((row == TILES - 1) & (place >= 32) & (place < 64))
            out[z] = jnp.where(ends, jnp.broadcast_to(near, (EDGE, LANES)), line).astype(BF)
        other = low[2 * LANES :, :].astype(F32)[8 * z : 8 * z + 1]
        x_code[z] = jnp.where(has_low, other, -1.0)


def ring_kernel(face, y_low, y_high, up, down):
    for z, out in ((1, up), (0, down)):
        out[:LANES, :] = face[z]
        out[LANES : LANES + EDGE, :] = y_low[z]
        out[LANES + EDGE :, :] = y_high[z]


def banded(weight, z_off, dy, slot, quarter):
    tile = jnp.zeros((32, LANES), BF)
    if abs(z_off) <= 1:
        for q in range(4):
            dx = slot - 1 - q
            if abs(dx) <= 1:
                tile = jnp.where(quarter == q, weight[9 * (z_off + 1) + 3 * (dx + 1) + dy], tile)
    return tile


def own_kernel(low, high, conv_weight, conv_bias, acc, inner, outer, weight, scr):
    quarter = iota((32, LANES), 1) // 32
    for k in range(27):
        one = conv_weight[k].astype(F32).T.astype(BF)
        weight[k] = jnp.concatenate([one] * 4, axis=1)
    for dy in range(3):
        for slot in range(8):
            for z in range(2):
                line = slice(256 * z + 32 * slot, 256 * z + 32 * slot + 32)
                for zo in range(2):
                    inner[dy, line, LANES * zo : LANES * (zo + 1)] = banded(weight, z - zo, dy, slot, quarter)
                outer[z, 32 * slot : 32 * slot + 32, LANES * dy : LANES * (dy + 1)] = banded(
                    weight, 2 * z - 1, dy, slot, quarter
                )
    bias = jnp.concatenate([conv_bias[...]] * 8, axis=1)
    for g in range(STACK):
        scr[STEP * g + 7 : STEP * g + 8, :] = jnp.zeros((1, 768), F32)
        scr[STEP * g + STEP : STEP * g + STEP + 1, :] = jnp.zeros((1, 768), F32)

    def body(s, _):
        base = s * STACK
        left = jnp.concatenate(
            [
                jnp.concatenate(
                    [plane[:, pl.ds(pl.multiple_of((base + g) * LANES, LANES), 2 * LANES)] for g in range(STACK)],
                    axis=0,
                )
                for plane in (low, high)
            ],
            axis=1,
        )
        for dy in range(3):
            part = jnp.dot(left, inner[dy], preferred_element_type=F32)
            for g in range(STACK):
                scr[STEP * g + 8 : STEP * g + STEP, 256 * dy : 256 * dy + 256] = part[LANES * g : LANES * (g + 1)]
        for g in range(STACK):
            o = STEP * g
            acc[base + g] = (
                scr[o + 7 : o + 135, 0:256] + scr[o + 8 : o + 136, 256:512] + scr[o + 9 : o + 137, 512:768] + bias
            )
        return 0

    lax.fori_loop(0, GROUPS // STACK, body, 0)


def line_windows(chunks):
    wide = chunks.astype(F32)
    return jnp.concatenate([wide[:GROUPS], wide[1:TILES]], axis=1).astype(BF)


def edge_kernel(face, y_low, y_high, inner, lines, ends):
    for side, (dy, source) in enumerate(((0, y_low), (2, y_high))):
        left = jnp.concatenate([line_windows(source[z]) for z in range(2)], axis=1)
        lines[side] = jnp.dot(left, inner[dy], preferred_element_type=F32)
    row = iota((LANES, 256), 0)
    lane = iota((LANES, LANES), 1)
    none = jnp.zeros((LANES, LANES), BF)
    for end in range(2):
        keep = lane < 32 if end == 0 else lane >= 32
        tiles = [jnp.where(keep, face[z], none) for z in range(2)]
        parts = []
        for dy in range(3):
            right = [inner[dy, 256 * z + LANES * end : 256 * z + LANES * end + LANES, :] for z in range(2)]
            parts.append(
                jnp.dot(
                    jnp.concatenate(tiles, axis=1), jnp.concatenate(right, axis=0), preferred_element_type=F32
                )
            )
        ends[end] = (
            jnp.where(row == 0, 0.0, pltpu.roll(parts[0], 1, 0))
            + parts[1]
            + jnp.where(row == LANES - 1, 0.0, pltpu.roll(parts[2], LANES - 1, 0))
        )


def spread(row, copies):
    one = jnp.broadcast_to(row, (16, LANES)).astype(BF)
    return jnp.concatenate([one] * copies, axis=0)


def numbers(rows):
    return iota((rows, LANES), 0).astype(F32).astype(BF)


def table_rows(t, frag, y_code, weight_row, own_hot, pair_hot, outer_z):
    one = jnp.ones((F, LANES), BF)
    none = jnp.zeros((F, LANES), BF)
    names = numbers(F)
    for j in range(16):
        x = 16 * t + j
        line = pl.ds(x, 1)
        before = pl.ds(jnp.maximum(x - 1, 0), 1)
        hot = [spread(frag[z, line, :], 4) == names for z in range(2)]
        spot = slice(LANES * j, LANES * (j + 1))
        for z in range(2):
            own_hot[z, :, spot] = jnp.where(hot[z], one, none)
            earlier = frag[z, before, :] + (jnp.where(x > 0, 0.0, -128.0) if j == 0 else 0.0)
            pair_hot[z, 0:F, spot] = jnp.where(spread(earlier, 4) == names, weight_row(1, z, x), none)
            pair_hot[z, F : 2 * F, spot] = jnp.where(
                spread(y_code[z, line, :], 4) == names, weight_row(2, z, x), none
            )
        pair_hot[1, 2 * F : 3 * F, spot] = jnp.where(hot[0], weight_row(0, 1, x), none)
        outer_z(line, x, spot, names, one, none)


def faces_product(own, partner, weight):
    names = numbers(F)
    one, none = jnp.ones((F, LANES), BF), jnp.zeros((F, LANES), BF)
    left = [jnp.where(spread(row, 4) == names, one, none) for row in own]
    right = [jnp.where(spread(row, 4) == names, spread(value, 4), none) for row, value in zip(partner, weight)]
    return outer_product(jnp.concatenate(left, axis=1), jnp.concatenate(right, axis=1))


def load_numbers(frag, plain, y_code):
    lane = iota((LANES, LANES), 1)
    for z in range(2):
        value = frag[z].astype(F32)
        plain[z] = value
        y_code[z] = jnp.where(lane == 0, -1.0, pltpu.roll(value, 1, 1))


def y_partner(y_low, z, has_low):
    return jnp.where(has_low, y_low[z, TILES - 1 :, :].astype(F32)[8:9], -1.0)


def count_kernel(frag, x_code, y_low, first_col, flags, out, own_hot, pair_hot, plain, y_code):
    load_numbers(frag, plain, y_code)
    unit = jnp.ones((F, LANES), BF)

    def body(t, carry):
        low, high = carry
        table_rows(t, plain, y_code, lambda *_: unit, own_hot, pair_hot, lambda *_: None)
        low = low + outer_product(own_hot[0], pair_hot[0, : 2 * F])
        high = high + outer_product(own_hot[1], pair_hot[1])
        return low, high

    low, high = lax.fori_loop(0, 8, body, (jnp.zeros((F, 2 * F), F32), jnp.zeros((F, 3 * F), F32)))
    own = low[:, :F] + low[:, F:] + high[:, :F] + high[:, F : 2 * F] + high[:, 2 * F :]
    ones = [jnp.ones((1, LANES), F32)] * 2
    x_outer = faces_product([plain[z, 0:1, :] for z in range(2)], [x_code[z] for z in range(2)], ones)
    y_outer = faces_product(
        [first_col[z : z + 1, :] for z in range(2)], [y_partner(y_low, z, flags[2] > 0) for z in range(2)], ones
    )
    out[...] = jnp.concatenate([own, jnp.zeros((F, F), F32), x_outer, y_outer], axis=1)


def slots_kernel(owner, recv, rank, place):
    slots = owner.shape[1]
    devices = place.shape[0]
    capacity = recv.shape[1] // devices
    hot = iota((devices, slots), 0) == owner[...]
    before = iota((slots, slots), 0) < iota((slots, slots), 1)
    earlier = jnp.dot(
        jnp.where(hot, 1.0, 0.0).astype(BF), jnp.where(before, 1.0, 0.0).astype(BF), preferred_element_type=F32
    )
    rank[...] = jnp.sum(jnp.where(hot, earlier, 0.0), axis=0, keepdims=True).astype(jnp.int32)
    place[...] = jnp.full(place.shape, -4 * LANES, jnp.int32)
    for p in range(devices):
        piece = recv[:, capacity * p : capacity * (p + 1)]
        place[p : p + 1, 0:capacity] = piece
        place[p : p + 1, F : F + capacity] = piece


def finish_kernel(
    acc,
    below,
    above,
    ring_low,
    ring_high,
    inner_lines,
    inner_ends,
    outer,
    head_weight,
    frag,
    x_code,
    y_low,
    first_col,
    counts,
    cells,
    owner,
    rank,
    head_bias,
    flags,
    edge_count,
    affinity,
    outgoing,
    planes,
    scr,
    lines,
    kept,
    own_hot,
    pair_hot,
    plain,
    y_code,
    z_code,
):
    load_numbers(frag, plain, y_code)
    z_code[...] = jnp.where(flags[3] > 0, below[:, WIDE:].astype(F32), -1.0)
    lane = iota((LANES, LANES), 1)
    for i, (plane, ring) in enumerate(((below, ring_low), (above, ring_high))):
        planes[i, :, LANES : WIDE - LANES] = plane[:, LANES : WIDE - LANES]
        face = ring[:LANES, :]
        planes[i, :, :LANES] = jnp.where(lane < 32, face, plane[:, :LANES])
        planes[i, :, WIDE - LANES :] = jnp.where(
            (lane >= 32) & (lane < 64), face, plane[:, WIDE - LANES : WIDE]
        )
        half = slice(LANES * i, LANES * (i + 1))
        for side, dy in ((0, 0), (1, 2)):
            chunks = ring[LANES + EDGE * side : LANES + EDGE * (side + 1), :]
            lines[side, :, half] = inner_lines[side, :, half] + jnp.dot(
                line_windows(chunks), outer[i, :, LANES * dy : LANES * (dy + 1)], preferred_element_type=F32
            )
    line, spot = iota((8, 256), 0), iota((8, 256), 1)
    head = []
    for d in range(3):
        weights = jnp.concatenate([head_weight[d : d + 1, :].astype(F32)] * 8, axis=1)
        for z in range(2):
            match = (spot // LANES == z) & ((spot // 32) % 4 == line % 4)
            head.append(jnp.where(match, jnp.broadcast_to(weights, (8, 256)), 0.0))
    head = jnp.concatenate(head, axis=0).astype(BF)
    top_half = iota((8, LANES), 0) < 4

    def weight_row(d, z, x):
        return spread(kept[2 * d + z, pl.ds(x, 1), :], 4)

    def outer_z(at, x, place, names, one, none):
        hot = spread(z_code[at, :], 4) == names
        pair_hot[0, 2 * F : 3 * F, place] = jnp.where(hot, weight_row(0, 0, x), none)
        pair_hot[0, 3 * F :, place] = jnp.where(hot, one, none)

    def body(s, carry):
        low, high = carry
        base = s * STACK
        for i in range(2):
            left = jnp.concatenate(
                [
                    planes[i, :, pl.ds(pl.multiple_of((base + g) * LANES, LANES), 2 * LANES)]
                    for g in range(STACK)
                ],
                axis=0,
            )
            part = jnp.dot(left, outer[i], preferred_element_type=F32)
            half = slice(LANES * i, LANES * (i + 1))
            ends = [lines[side, pl.ds(pl.multiple_of(base, 8), STACK), half] for side in range(2)]
            for g in range(STACK):
                o = STEP * g
                scr[i, o + 8 : o + STEP, :] = part[LANES * g : LANES * (g + 1)]
                scr[i, o + 7 : o + 8, 0:LANES] = ends[0][g : g + 1]
                scr[i, o + STEP : o + STEP + 1, 2 * LANES :] = ends[1][g : g + 1]
        hidden = []
        for g in range(STACK):
            o = STEP * g
            outside = [
                scr[i, o + 7 : o + 135, 0:LANES]
                + scr[i, o + 8 : o + 136, LANES : 2 * LANES]
                + scr[i, o + 9 : o + 137, 2 * LANES :]
                for i in range(2)
            ]
            total = acc[base + g] + jnp.concatenate(outside, axis=1)
            if g == 0:
                total = total + jnp.where(s == 0, inner_ends[0], 0.0)
            if g == STACK - 1:
                total = total + jnp.where(s == GROUPS // STACK - 1, inner_ends[1], 0.0)
            hidden.append(jnp.maximum(total, 0.0).astype(BF))
        logits = outer_product(head, jnp.concatenate(hidden, axis=0))
        for i in range(6):
            for pair in range(STACK // 2):
                at = 2 * LANES * pair
                both = logits[8 * i : 8 * i + 8]
                value = jnp.where(top_half, both[:, at : at + LANES], both[:, at + LANES : at + 2 * LANES])
                value = jax.nn.sigmoid(value + head_bias[i // 2]).astype(BF).astype(F32)
                kept[i, pl.ds(pl.multiple_of(4 * STACK * s + 8 * pair, 8), 8), :] = value
            all_lines = pl.ds(pl.multiple_of(4 * STACK * s, 16), 4 * STACK)
            affinity[i // 2, i % 2, all_lines, :] = kept[i, all_lines, :].astype(BF)
        for t in range(STACK // 4):
            table_rows(STACK // 4 * s + t, plain, y_code, weight_row, own_hot, pair_hot, outer_z)
            low = low + outer_product(own_hot[0], pair_hot[0])
            high = high + outer_product(own_hot[1], pair_hot[1, : 3 * F])
        return low, high

    low, high = lax.fori_loop(
        0, GROUPS // STACK, body, (jnp.zeros((F, 4 * F), F32), jnp.zeros((F, 3 * F), F32))
    )
    own = low[:, :F] + low[:, F : 2 * F] + high[:, :F] + high[:, F : 2 * F] + high[:, 2 * F :]
    x_outer = faces_product(
        [plain[z, 0:1, :] for z in range(2)],
        [x_code[z] for z in range(2)],
        [kept[2 + z, 0:1, :] for z in range(2)],
    )
    y_outer = faces_product(
        [first_col[z : z + 1, :] for z in range(2)],
        [y_partner(y_low, z, flags[2] > 0) for z in range(2)],
        [kept[4 + z].T[0:1, :] for z in range(2)],
    )
    sums = jnp.concatenate([own, low[:, 2 * F : 3 * F], x_outer, y_outer], axis=1)
    tally = counts[...] + jnp.concatenate(
        [jnp.zeros((F, F), F32), low[:, 3 * F :], jnp.zeros((F, 2 * F), F32)], axis=1
    )
    slots = cells.shape[1]
    code = jnp.concatenate([cells[0:1, :], cells[1:2, :]], axis=1)
    column_hot = jnp.where(iota((4 * F, 2 * slots), 0) == (code & (4 * F - 1)), 1.0, 0.0).astype(BF)
    picked = jnp.dot(
        jnp.concatenate(halves(sums) + halves(tally), axis=0), column_hot, preferred_element_type=F32
    )
    line_hot = iota((F, 2 * slots), 0) == (code >> 8)
    alive = iota((1, slots), 1) < edge_count[0]

    def part_of(value):
        total = jnp.sum(jnp.where(line_hot, value, 0.0), axis=0, keepdims=True)
        return jnp.where(alive, total[:, :slots] + total[:, slots:], 0.0)

    part_sum = part_of(picked[:F] + picked[F : 2 * F])
    part_count = part_of(picked[2 * F : 3 * F] + picked[3 * F :])
    to_owner = iota((outgoing.shape[0], slots), 0) == owner[...]
    lanes = iota((LANES, slots), 0)
    low_hot = jnp.where(lanes == rank[...], 1.0, 0.0).astype(BF)
    high_hot = jnp.where(lanes == rank[...] + F, 1.0, 0.0).astype(BF)
    left = [
        jnp.where(to_owner, piece.astype(F32), 0.0).astype(BF) for piece in halves(part_sum) + halves(part_count)
    ]
    sent = outer_product(
        jnp.concatenate(left, axis=1), jnp.concatenate([low_hot, low_hot, high_hot, high_hot], axis=1)
    )
    outgoing[...] = sent.reshape(outgoing.shape)


def settle_kernel(received, slot, out, left, right):
    devices = received.shape[0]
    groups = out.shape[1] // LANES
    names = iota((LANES, LANES), 0)
    row, lane = iota((16, LANES), 0), iota((16, LANES), 1)
    of_count = row >= 2 * groups
    inner = jnp.where(of_count, row - 2 * groups, row)
    is_low = inner >= groups
    group = jnp.where(is_low, inner - groups, inner)
    group = jnp.where((lane >= F) == of_count, group, -1)
    group = jnp.where(row < 4 * groups, group, -1)

    def body(p, _):
        spot = pl.ds(pl.multiple_of(p * LANES, LANES), LANES)
        code = slot[pl.ds(p, 1), :]
        value = received[p]
        high = value.astype(BF).astype(F32)
        piece = jnp.where(is_low, value - high, high)
        left[:, spot] = jnp.where((code >> 7) == group, piece, 0.0).astype(BF)
        right[:, spot] = jnp.where((code & (LANES - 1)) == names, 1.0, 0.0).astype(BF)
        return 0

    lax.fori_loop(0, devices, body, 0, unroll=8)
    total = outer_product(left[...], right[...])
    for g in range(groups):
        total_sum = total[g : g + 1] + total[groups + g : groups + g + 1]
        total_count = total[2 * groups + g : 2 * groups + g + 1] + total[3 * groups + g : 3 * groups + g + 1]
        out[:, LANES * g : LANES * (g + 1)] = total_sum / jnp.maximum(total_count, 1.0)


def exchange(up, down, axis):
    n = lax.axis_size(axis)
    if n == 1:
        return jnp.zeros_like(up), jnp.zeros_like(down)
    forward = [(i, i + 1) for i in range(n - 1)]
    backward = [(i + 1, i) for i in range(n - 1)]
    return lax.ppermute(up, axis, forward), lax.ppermute(down, axis, backward)


def shards(
    features,
    conv_weight,
    conv_bias,
    head_weight,
    head_bias,
    fragments,
    edge_cells,
    edge_owner,
    edge_count,
    recv_slot,
):
    axes = ("gx", "gy", "gz")
    size = {axis: lax.axis_size(axis) for axis in axes}
    at = {axis: lax.axis_index(axis) for axis in axes}
    devices = size["gx"] * size["gy"] * size["gz"]
    capacity = recv_slot.shape[1] // devices
    slots = edge_cells.shape[1]
    own_slots = devices * capacity // 4
    flags = jnp.stack([at["gx"], size["gx"] - 1 - at["gx"], at["gy"], at["gz"]]).astype(jnp.int32)
    pair = size["gx"] == 2
    send_up = flags if pair else jnp.zeros_like(flags)

    xt_low, xt_high, x_up, x_down, edge, first_col = call(
        layout_kernel,
        "layout",
        (
            shape((LANES, WIDE), BF),
            shape((LANES, WIDE + LANES), BF),
            shape((2 * LANES + 16, LANES), BF),
            shape((2 * LANES + 16, LANES), BF),
            shape((4, EDGE, LANES), BF),
            shape((2, LANES), F32),
        ),
        (features, fragments, send_up),
        1,
        [pltpu.VMEM((4, EDGE, LANES), F32)],
    )
    below, above = exchange(xt_high, xt_low, "gz")
    if pair:
        x_low = x_high = lax.ppermute(x_up, "gx", [(0, 1), (1, 0)])
    else:
        x_low, x_high = exchange(x_up, x_down, "gx")

    acc, inner, outer = call(
        own_kernel,
        "own_planes",
        (shape((GROUPS, LANES, 256), F32), shape((3, 512, 256), BF), shape((2, 256, 3 * LANES), BF)),
        (xt_low, xt_high, conv_weight, conv_bias.reshape(1, -1)),
        0,
        [pltpu.VMEM((27, 32, LANES), BF), pltpu.VMEM((STEP * STACK + 8, 768), F32)],
        flops=5_000_000_000,
    )
    owner = edge_owner.reshape(1, slots)
    rank, place = call(
        slots_kernel,
        "slots",
        (shape((1, slots), jnp.int32), shape((devices, LANES), jnp.int32)),
        (owner, recv_slot),
        0,
    )
    face, x_code, y_up, y_down = call(
        x_face_kernel,
        "x_face",
        (
            shape((2, LANES, LANES), BF),
            shape((2, 1, LANES), F32),
            shape((2, EDGE, LANES), BF),
            shape((2, EDGE, LANES), BF),
        ),
        (x_low, x_high, edge, flags),
        1,
    )
    y_low, y_high = exchange(y_up, y_down, "gy")
    ring_up, ring_down = call(
        ring_kernel, "ring", (shape((LANES + 2 * EDGE, LANES), BF),) * 2, (face, y_low, y_high), 0
    )
    ring_low, ring_high = exchange(ring_up, ring_down, "gz")

    lines, ends = call(
        edge_kernel,
        "edges",
        (shape((2, GROUPS, 256), F32), shape((2, LANES, 256), F32)),
        (face, y_low, y_high, inner),
        0,
        flops=500_000_000,
    )
    counts = call(
        count_kernel,
        "pair_counts",
        shape((F, 4 * F), F32),
        (fragments, x_code, y_low, first_col, flags),
        1,
        [
            pltpu.VMEM((2, F, 2048), BF),
            pltpu.VMEM((2, 3 * F, 2048), BF),
            pltpu.VMEM((2, LANES, LANES), F32),
            pltpu.VMEM((2, LANES, LANES), F32),
        ],
        flops=4_000_000_000,
    )
    affinity, outgoing = call(
        finish_kernel,
        "finish",
        (shape((3, 2, LANES, LANES), BF), shape((devices, 1, LANES), F32)),
        (
            acc,
            below,
            above,
            ring_low,
            ring_high,
            lines,
            ends,
            outer,
            head_weight,
            fragments,
            x_code,
            y_low,
            first_col,
            counts,
            edge_cells,
            owner,
            rank,
            head_bias,
            flags,
            edge_count,
        ),
        3,
        [
            pltpu.VMEM((2, LANES, WIDE), BF),
            pltpu.VMEM((2, STEP * STACK + 8, 3 * LANES), F32),
            pltpu.VMEM((2, GROUPS, 256), F32),
            pltpu.VMEM((6, LANES, LANES), F32),
            pltpu.VMEM((2, F, 2048), BF),
            pltpu.VMEM((2, 4 * F, 2048), BF),
            pltpu.VMEM((2, LANES, LANES), F32),
            pltpu.VMEM((2, LANES, LANES), F32),
            pltpu.VMEM((LANES, LANES), F32),
        ],
        flops=8_000_000_000,
    )
    received = lax.all_to_all(outgoing, axes, split_axis=0, concat_axis=0, tiled=True)
    edge_mean = call(
        settle_kernel,
        "settle",
        shape((1, own_slots), F32),
        (received, place),
        0,
        [pltpu.VMEM((16, devices * LANES), BF), pltpu.VMEM((LANES, devices * LANES), BF)],
    )
    return affinity, edge_mean


def solution(mesh):
    in_specs = (
        P(None, "gz", "gx", "gy"),
        P(),
        P(),
        P(),
        P(),
        P("gz", "gx", "gy"),
        P(None, ("gx", "gy", "gz")),
        P(("gx", "gy", "gz"), None),
        P(("gx", "gy", "gz")),
        P(("gx", "gy", "gz"), None),
    )
    out_specs = (P(None, "gz", "gx", "gy"), P(("gx", "gy", "gz"), None))
    return jax.shard_map(shards, mesh=mesh, in_specs=in_specs, out_specs=out_specs, check_vma=False)
```

```python
import jax
import jax.numpy as jnp
from jax import lax
from jax.experimental import pallas as pl
from jax.experimental.pallas import tpu as pltpu
from jax.sharding import PartitionSpec as P

F = 64
LANES = 128
GROUPS = 32
TILES = GROUPS + 1
WIDE = TILES * LANES
STACK = 8
STEP = LANES + 8
EDGE = 48
BF = jnp.bfloat16
F32 = jnp.float32
F8 = jnp.float8_e4m3fn
VMEM = pl.BlockSpec(memory_space=pltpu.VMEM)
SMEM = pl.BlockSpec(memory_space=pltpu.SMEM)


def call(kernel, name, out_shape, args, smem, scratch=(), flops=1_000_000):
    return pl.pallas_call(
        kernel,
        out_shape=out_shape,
        in_specs=[VMEM] * (len(args) - smem) + [SMEM] * smem,
        out_specs=jax.tree.map(lambda _: VMEM, out_shape),
        scratch_shapes=list(scratch),
        compiler_params=pltpu.CompilerParams(vmem_limit_bytes=28 << 20),
        cost_estimate=pl.CostEstimate(flops=flops, bytes_accessed=1 << 20, transcendentals=0),
        name=name,
    )(*args)


def shape(dims, dtype):
    return jax.ShapeDtypeStruct(dims, dtype)


def iota(dims, axis):
    return lax.broadcasted_iota(jnp.int32, dims, axis)


X_LOW, X_HIGH, X_ODD, Y_LOW, Y_HIGH, Y_ODD, Z_LOW, Z_HIGH, Z_ODD, LIVE = range(10)


def outer_product(left, right):
    return lax.dot_general(left, right, (((1,), (1,)), ((), ())), preferred_element_type=F32)


def halves(value):
    high = value.astype(BF)
    return high, (value - high.astype(F32)).astype(BF)


def layout_kernel(flags, feat_hbm, frag, low, high, z_one, z_two, x_one, x_two, edge, first_col, rows, feat, sems):
    copies = []
    for t in range(8):
        lines = slice(16 * t, 16 * t + 16)
        copies.append(pltpu.make_async_copy(feat_hbm.at[:, :, lines, :], feat.at[:, :, lines, :], sems.at[t]))
        copies[-1].start()
    x_odd, z_odd = flags[X_ODD] > 0, flags[Z_ODD] > 0
    zero = jnp.zeros((32, LANES), BF)
    last = [zero, zero]
    tile_zero = [None, None]
    for t in range(9):
        if t < 8:
            copies[t].wait()
        both = []
        for z, plane in ((0, low), (1, high)):
            if t < 8:
                block = jnp.swapaxes(feat[:, z, 16 * t : 16 * t + 16, :], 0, 1).reshape(512, LANES)
                turned = jnp.concatenate([last[z], block[:480]], axis=0).T
                last[z] = block[480:]
            else:
                turned = jnp.concatenate([last[z], zero, zero, zero], axis=0).T
            wide = turned.shape[1]
            plane[:, 512 * t : 512 * t + wide] = turned
            both.append(turned)
            for side, line in ((0, turned[112:128].astype(F32)[15:16]), (1, turned[0:16].astype(F32)[0:1])):
                for q in range(wide // LANES):
                    spot = 4 * t + q
                    rows[2 * side + z, spot : spot + 1, :] = line[:, LANES * q : LANES * (q + 1)]
            if t == 0:
                tile_zero[z] = turned[:, :LANES]
            if t == 8:
                lines = slice(LANES * z, LANES * (z + 1))
                x_one[lines, :] = jnp.where(x_odd, tile_zero[z], turned)
                x_two[lines, :] = jnp.where(x_odd, turned, tile_zero[z])
        z_one[:, 512 * t : 512 * t + wide] = jnp.where(z_odd, both[0], both[1])
        z_two[:, 512 * t : 512 * t + wide] = jnp.where(z_odd, both[1], both[0])
    for z in range(2):
        turned = frag[z].astype(F32).T
        first_col[z : z + 1, :] = turned[0:1]
        for side in range(2):
            rows[2 * side + z, TILES:EDGE, :] = jnp.broadcast_to(turned[127:128], (EDGE - TILES, LANES))
            edge[2 * side + z] = rows[2 * side + z].astype(BF)
    top = frag[1].astype(F32).astype(BF)
    lines = [jnp.broadcast_to(frag[z, 127:128, :], (8, LANES)).astype(F32) for z in range(2)]
    lines = jnp.concatenate(lines, axis=0).astype(BF)
    for out in (z_one, z_two):
        out[:, WIDE:] = top
    for out in (x_one, x_two):
        out[2 * LANES :, :] = lines


def x_face_kernel(got_one, got_two, edge, flags, face, x_code, y_one, y_two):
    has_low, has_high, odd = flags[X_LOW] > 0, flags[X_HIGH] > 0, flags[X_ODD] > 0
    y_odd = flags[Y_ODD] > 0
    lane = iota((LANES, LANES), 1)
    is_low = (lane < 32) & has_low
    is_high = (lane >= 32) & (lane < 64) & has_high
    none = jnp.zeros((LANES, LANES), BF)
    row, place = iota((EDGE, LANES), 0), iota((EDGE, LANES), 1)
    ends = ((row == 0) & (place < 32)) | ((row == TILES - 1) & (place >= 32) & (place < 64))
    other = jnp.where(odd, got_one[2 * LANES :, :], got_two[2 * LANES :, :]).astype(F32)
    for z in range(2):
        lines = slice(LANES * z, LANES * (z + 1))
        low = jnp.where(odd, got_one[lines, :], got_two[lines, :])
        high = jnp.where(odd, got_two[lines, :], got_one[lines, :])
        tile = jnp.where(is_low, low, jnp.where(is_high, high, none))
        face[z] = tile
        patched = []
        for side in range(2):
            near = (tile[112:128].astype(F32)[15:16], tile[0:16].astype(F32)[0:1])[side]
            line = edge[2 * side + z].astype(F32)
            patched.append(jnp.where(ends, jnp.broadcast_to(near, (EDGE, LANES)), line).astype(BF))
        y_one[z] = jnp.where(y_odd, patched[1], patched[0])
        y_two[z] = jnp.where(y_odd, patched[0], patched[1])
        x_code[z] = jnp.where(has_low, other[8 * z : 8 * z + 1], -1.0)


def ring_kernel(face, got_one, got_two, flags, y_low, y_high, z_one, z_two):
    odd, z_odd = flags[Y_ODD] > 0, flags[Z_ODD] > 0
    none = jnp.zeros((EDGE, LANES), BF)
    rings = []
    for z in range(2):
        low = jnp.where(flags[Y_LOW] > 0, jnp.where(odd, got_one[z], got_two[z]), none)
        high = jnp.where(flags[Y_HIGH] > 0, jnp.where(odd, got_two[z], got_one[z]), none)
        y_low[z] = low
        y_high[z] = high
        rings.append(jnp.concatenate([face[z], low, high], axis=0))
    z_one[...] = jnp.where(z_odd, rings[0], rings[1])
    z_two[...] = jnp.where(z_odd, rings[1], rings[0])


def banded(weight, z_off, dy, slot, quarter):
    tile = jnp.zeros((32, LANES), BF)
    if abs(z_off) <= 1:
        for q in range(4):
            dx = slot - 1 - q
            if abs(dx) <= 1:
                tile = jnp.where(quarter == q, weight[9 * (z_off + 1) + 3 * (dx + 1) + dy], tile)
    return tile


def own_kernel(low, high, conv_weight, conv_bias, acc, inner, outer, weight, scr):
    quarter = iota((32, LANES), 1) // 32
    for k in range(27):
        one = conv_weight[k].astype(F32).T.astype(BF)
        weight[k] = jnp.concatenate([one] * 4, axis=1)
    for dy in range(3):
        for slot in range(8):
            for z in range(2):
                line = slice(256 * z + 32 * slot, 256 * z + 32 * slot + 32)
                for zo in range(2):
                    inner[dy, line, LANES * zo : LANES * (zo + 1)] = banded(weight, z - zo, dy, slot, quarter)
                outer[z, 32 * slot : 32 * slot + 32, LANES * dy : LANES * (dy + 1)] = banded(
                    weight, 2 * z - 1, dy, slot, quarter
                )
    bias = jnp.concatenate([conv_bias[...]] * 8, axis=1)
    for g in range(STACK):
        scr[STEP * g + 7 : STEP * g + 8, :] = jnp.zeros((1, 768), F32)
        scr[STEP * g + STEP : STEP * g + STEP + 1, :] = jnp.zeros((1, 768), F32)

    def body(s, _):
        base = s * STACK
        left = jnp.concatenate(
            [
                jnp.concatenate(
                    [plane[:, pl.ds(pl.multiple_of((base + g) * LANES, LANES), 2 * LANES)] for g in range(STACK)],
                    axis=0,
                )
                for plane in (low, high)
            ],
            axis=1,
        )
        for dy in range(3):
            part = jnp.dot(left, inner[dy], preferred_element_type=F32)
            for g in range(STACK):
                scr[STEP * g + 8 : STEP * g + STEP, 256 * dy : 256 * dy + 256] = part[LANES * g : LANES * (g + 1)]
        for g in range(STACK):
            o = STEP * g
            acc[base + g] = (
                scr[o + 7 : o + 135, 0:256] + scr[o + 8 : o + 136, 256:512] + scr[o + 9 : o + 137, 512:768] + bias
            )
        return 0

    lax.fori_loop(0, GROUPS // STACK, body, 0)


def line_windows(chunks):
    wide = chunks.astype(F32)
    return jnp.concatenate([wide[:GROUPS], wide[1:TILES]], axis=1).astype(BF)


def edge_kernel(face, y_low, y_high, inner, lines, ends):
    for side, (dy, source) in enumerate(((0, y_low), (2, y_high))):
        left = jnp.concatenate([line_windows(source[z]) for z in range(2)], axis=1)
        lines[side] = jnp.dot(left, inner[dy], preferred_element_type=F32)
    row = iota((LANES, 256), 0)
    lane = iota((LANES, LANES), 1)
    none = jnp.zeros((LANES, LANES), BF)
    for end in range(2):
        keep = lane < 32 if end == 0 else lane >= 32
        tiles = [jnp.where(keep, face[z], none) for z in range(2)]
        parts = []
        for dy in range(3):
            right = [inner[dy, 256 * z + LANES * end : 256 * z + LANES * end + LANES, :] for z in range(2)]
            parts.append(
                jnp.dot(
                    jnp.concatenate(tiles, axis=1), jnp.concatenate(right, axis=0), preferred_element_type=F32
                )
            )
        ends[end] = (
            jnp.where(row == 0, 0.0, pltpu.roll(parts[0], 1, 0))
            + parts[1]
            + jnp.where(row == LANES - 1, 0.0, pltpu.roll(parts[2], LANES - 1, 0))
        )


def spread(row, copies):
    one = jnp.broadcast_to(row, (16, LANES)).astype(BF)
    return jnp.concatenate([one] * copies, axis=0)


def numbers(rows):
    return iota((rows, LANES), 0).astype(F32).astype(BF)


def line_partners(frag, y_code, x, first, hot_before):
    names = numbers(F)
    line = pl.ds(x, 1)
    hot = [spread(frag[z, line, :], 4) == names for z in range(2)]
    if hot_before is None:
        before = [frag[z, pl.ds(jnp.maximum(x - 1, 0), 1), :] + first for z in range(2)]
        hot_before = [spread(row, 4) == names for row in before]
    y_hot = [spread(y_code[z, line, :], 4) == names for z in range(2)]
    return hot, hot_before, y_hot


def faces_product(own, partner, weight):
    names = numbers(F)
    one, none = jnp.ones((F, LANES), BF), jnp.zeros((F, LANES), BF)
    left = [jnp.where(spread(row, 4) == names, one, none) for row in own]
    right = [jnp.where(spread(row, 4) == names, spread(value, 4), none) for row, value in zip(partner, weight)]
    return outer_product(jnp.concatenate(left, axis=1), jnp.concatenate(right, axis=1))


def load_numbers(frag, plain, y_code):
    lane = iota((LANES, LANES), 1)
    for z in range(2):
        value = frag[z].astype(F32)
        plain[z] = value
        y_code[z] = jnp.where(lane == 0, -1.0, pltpu.roll(value, 1, 1))


def y_partner(y_low, z, has_low):
    return jnp.where(has_low, y_low[z, TILES - 1 :, :].astype(F32)[8:9], -1.0)


def count_kernel(frag, x_code, y_low, first_col, flags, out, own_hot, pair_hot, plain, y_code):
    load_numbers(frag, plain, y_code)
    one = jnp.ones((F, LANES), BF)
    none = jnp.zeros((F, LANES), BF)

    def body(t, total):
        hot_before = None
        first = jnp.where(t > 0, 0.0, -128.0)
        for j in range(32):
            spot = slice(LANES * j, LANES * (j + 1))
            hot, x_hot, y_hot = line_partners(plain, y_code, 32 * t + j, first, hot_before)
            hot_before = hot
            for z in range(2):
                own_hot[z, :, spot] = jnp.where(hot[z], one, none).astype(F8)
                pairs = jnp.where(x_hot[z], one, none) + jnp.where(y_hot[z], one, none)
                if z == 1:
                    pairs = pairs + jnp.where(hot[0], one, none)
                pair_hot[z, :, spot] = pairs.astype(F8)
        for z in range(2):
            total = total + outer_product(own_hot[z], pair_hot[z])
        return total

    own = lax.fori_loop(0, 4, body, jnp.zeros((F, F), F32))
    ones = [jnp.ones((1, LANES), F32)] * 2
    x_outer = faces_product([plain[z, 0:1, :] for z in range(2)], [x_code[z] for z in range(2)], ones)
    y_outer = faces_product(
        [first_col[z : z + 1, :] for z in range(2)], [y_partner(y_low, z, flags[Y_LOW] > 0) for z in range(2)], ones
    )
    out[...] = jnp.concatenate([own, jnp.zeros((F, F), F32), x_outer, y_outer], axis=1)


def slots_kernel(owner, recv, rank, place):
    slots = owner.shape[1]
    devices = place.shape[0]
    capacity = recv.shape[1] // devices
    hot = iota((devices, slots), 0) == owner[...]
    before = iota((slots, slots), 0) < iota((slots, slots), 1)
    earlier = jnp.dot(
        jnp.where(hot, 1.0, 0.0).astype(BF), jnp.where(before, 1.0, 0.0).astype(BF), preferred_element_type=F32
    )
    rank[...] = jnp.sum(jnp.where(hot, earlier, 0.0), axis=0, keepdims=True).astype(jnp.int32)
    place[...] = jnp.full(place.shape, -4 * LANES, jnp.int32)
    for p in range(devices):
        piece = recv[:, capacity * p : capacity * (p + 1)]
        place[p : p + 1, 0:capacity] = piece
        place[p : p + 1, F : F + capacity] = piece


def finish_kernel(
    acc,
    plane_one,
    plane_two,
    ring_one,
    ring_two,
    inner_lines,
    inner_ends,
    outer,
    head_weight,
    frag,
    x_code,
    y_low,
    first_col,
    counts,
    cells,
    owner,
    rank,
    head_bias,
    flags,
    affinity,
    outgoing,
    planes,
    scr,
    lines,
    kept,
    own_hot,
    pair_hot,
    plain,
    y_code,
    z_code,
):
    load_numbers(frag, plain, y_code)
    odd = flags[Z_ODD]
    below = jnp.where(odd > 0, plane_one[:, WIDE:], plane_two[:, WIDE:])
    z_code[...] = jnp.where(flags[Z_LOW] > 0, below.astype(F32), -1.0)
    lane = iota((LANES, LANES), 1)
    for plane, ring, i in ((plane_one, ring_one, 1 - odd), (plane_two, ring_two, odd)):
        live = jnp.where(i > 0, flags[Z_HIGH], flags[Z_LOW]) > 0
        planes[i, :, LANES : WIDE - LANES] = plane[:, LANES : WIDE - LANES]
        around = jnp.where(live, ring[...], jnp.zeros(ring.shape, BF))
        face = around[:LANES, :]
        planes[i, :, :LANES] = jnp.where(lane < 32, face, plane[:, :LANES])
        planes[i, :, WIDE - LANES :] = jnp.where(
            (lane >= 32) & (lane < 64), face, plane[:, WIDE - LANES : WIDE]
        )
        for side, dy in ((0, 0), (1, 2)):
            chunks = around[LANES + EDGE * side : LANES + EDGE * (side + 1), :]
            lines[side, i] = jnp.dot(
                line_windows(chunks), outer[i, :, LANES * dy : LANES * (dy + 1)], preferred_element_type=F32
            )
    for i in range(2):
        for side in range(2):
            lines[side, i] = lines[side, i] + inner_lines[side, :, LANES * i : LANES * (i + 1)]
    line, spot = iota((8, 256), 0), iota((8, 256), 1)
    head = []
    for d in range(3):
        weights = jnp.concatenate([head_weight[d : d + 1, :].astype(F32)] * 8, axis=1)
        for z in range(2):
            match = (spot // LANES == z) & ((spot // 32) % 4 == line % 4)
            head.append(jnp.where(match, jnp.broadcast_to(weights, (8, 256)), 0.0))
    head = jnp.concatenate(head, axis=0).astype(BF)
    top_half = iota((8, LANES), 0) < 4

    def weight_row(d, z, x):
        return spread(kept[2 * d + z, pl.ds(x, 1), :], 4)

    def table_lines(x0, first, own_hot, pair_hot):
        names, one, none = numbers(F), jnp.ones((F, LANES), BF), jnp.zeros((F, LANES), BF)
        hot_before = None
        for j in range(16):
            x = x0 + j
            spot = slice(LANES * j, LANES * (j + 1))
            hot, x_hot, y_hot = line_partners(plain, y_code, x, first, hot_before)
            hot_before = hot
            for z in range(2):
                own_hot[z, :, spot] = jnp.where(hot[z], one, none)
                pair_hot[z, 0:F, spot] = jnp.where(x_hot[z], weight_row(1, z, x), none) + jnp.where(
                    y_hot[z], weight_row(2, z, x), none
                )
            pair_hot[1, F : 2 * F, spot] = jnp.where(hot[0], weight_row(0, 1, x), none)
            z_hot = spread(z_code[pl.ds(x, 1), :], 4) == names
            pair_hot[0, F : 2 * F, spot] = jnp.where(z_hot, weight_row(0, 0, x), none)
            pair_hot[0, 2 * F :, spot] = jnp.where(z_hot, one, none)

    def body(s, carry):
        low, high = carry
        base = s * STACK
        for i in range(2):
            left = jnp.concatenate(
                [
                    planes[i, :, pl.ds(pl.multiple_of((base + g) * LANES, LANES), 2 * LANES)]
                    for g in range(STACK)
                ],
                axis=0,
            )
            part = jnp.dot(left, outer[i], preferred_element_type=F32)
            ends = [lines[side, i, pl.ds(pl.multiple_of(base, 8), STACK), :] for side in range(2)]
            for g in range(STACK):
                o = STEP * g
                scr[i, o + 8 : o + STEP, :] = part[LANES * g : LANES * (g + 1)]
                scr[i, o + 7 : o + 8, 0:LANES] = ends[0][g : g + 1]
                scr[i, o + STEP : o + STEP + 1, 2 * LANES :] = ends[1][g : g + 1]
        hidden = []
        for g in range(STACK):
            o = STEP * g
            outside = [
                scr[i, o + 7 : o + 135, 0:LANES]
                + scr[i, o + 8 : o + 136, LANES : 2 * LANES]
                + scr[i, o + 9 : o + 137, 2 * LANES :]
                for i in range(2)
            ]
            total = acc[base + g] + jnp.concatenate(outside, axis=1)
            if g == 0:
                total = total + jnp.where(s == 0, inner_ends[0], 0.0)
            if g == STACK - 1:
                total = total + jnp.where(s == GROUPS // STACK - 1, inner_ends[1], 0.0)
            hidden.append(jnp.maximum(total, 0.0).astype(BF))
        logits = outer_product(head, jnp.concatenate(hidden, axis=0))
        for i in range(6):
            for pair in range(STACK // 2):
                at = 2 * LANES * pair
                both = logits[8 * i : 8 * i + 8]
                value = jnp.where(top_half, both[:, at : at + LANES], both[:, at + LANES : at + 2 * LANES])
                value = jax.nn.sigmoid(value + head_bias[i // 2]).astype(BF).astype(F32)
                kept[i, pl.ds(pl.multiple_of(4 * STACK * s + 8 * pair, 8), 8), :] = value
            all_lines = pl.ds(pl.multiple_of(4 * STACK * s, 16), 4 * STACK)
            affinity[i // 2, i % 2, all_lines, :] = kept[i, all_lines, :].astype(BF)
        for t in range(2):
            first = jnp.where(s > 0, 0.0, -128.0) if t == 0 else 0.0
            table_lines(4 * STACK * s + 16 * t, first, own_hot.at[t], pair_hot.at[t])
            low = low + outer_product(own_hot[t, 0], pair_hot[t, 0])
            high = high + outer_product(own_hot[t, 1], pair_hot[t, 1, : 2 * F])
        return low, high

    low, high = lax.fori_loop(
        0, GROUPS // STACK, body, (jnp.zeros((F, 3 * F), F32), jnp.zeros((F, 2 * F), F32))
    )
    own = low[:, :F] + high[:, :F] + high[:, F:]
    x_outer = faces_product(
        [plain[z, 0:1, :] for z in range(2)],
        [x_code[z] for z in range(2)],
        [kept[2 + z, 0:1, :] for z in range(2)],
    )
    y_outer = faces_product(
        [first_col[z : z + 1, :] for z in range(2)],
        [y_partner(y_low, z, flags[Y_LOW] > 0) for z in range(2)],
        [kept[4 + z].T[0:1, :] for z in range(2)],
    )
    sums = jnp.concatenate([own, low[:, F : 2 * F], x_outer, y_outer], axis=1)
    tally = counts[...] + jnp.concatenate(
        [jnp.zeros((F, F), F32), low[:, 2 * F :], jnp.zeros((F, 2 * F), F32)], axis=1
    )
    slots = cells.shape[1]
    code = jnp.concatenate([cells[0:1, :], cells[1:2, :]], axis=1)
    column_hot = jnp.where(iota((4 * F, 2 * slots), 0) == (code & (4 * F - 1)), 1.0, 0.0).astype(BF)
    picked = jnp.dot(
        jnp.concatenate(halves(sums) + halves(tally), axis=0), column_hot, preferred_element_type=F32
    )
    line_hot = iota((F, 2 * slots), 0) == (code >> 8)
    alive = iota((1, slots), 1) < flags[LIVE]

    def part_of(value):
        total = jnp.sum(jnp.where(line_hot, value, 0.0), axis=0, keepdims=True)
        return jnp.where(alive, total[:, :slots] + total[:, slots:], 0.0)

    part_sum = part_of(picked[:F] + picked[F : 2 * F])
    part_count = part_of(picked[2 * F : 3 * F] + picked[3 * F :])
    to_owner = iota((outgoing.shape[0], slots), 0) == owner[...]
    lanes = iota((LANES, slots), 0)
    low_hot = jnp.where(lanes == rank[...], 1.0, 0.0).astype(BF)
    high_hot = jnp.where(lanes == rank[...] + F, 1.0, 0.0).astype(BF)
    left = [
        jnp.where(to_owner, piece.astype(F32), 0.0).astype(BF) for piece in halves(part_sum) + halves(part_count)
    ]
    sent = outer_product(
        jnp.concatenate(left, axis=1), jnp.concatenate([low_hot, low_hot, high_hot, high_hot], axis=1)
    )
    outgoing[...] = sent.reshape(outgoing.shape)


def settle_kernel(received, slot, out, left, right):
    devices = received.shape[0]
    groups = out.shape[1] // LANES
    names = iota((LANES, LANES), 0)
    row, lane = iota((16, LANES), 0), iota((16, LANES), 1)
    of_count = row >= 2 * groups
    inner = jnp.where(of_count, row - 2 * groups, row)
    is_low = inner >= groups
    group = jnp.where(is_low, inner - groups, inner)
    group = jnp.where((lane >= F) == of_count, group, -1)
    group = jnp.where(row < 4 * groups, group, -1)

    def body(p, _):
        spot = pl.ds(pl.multiple_of(p * LANES, LANES), LANES)
        code = slot[pl.ds(p, 1), :]
        value = received[p]
        high = value.astype(BF).astype(F32)
        piece = jnp.where(is_low, value - high, high)
        left[:, spot] = jnp.where((code >> 7) == group, piece, 0.0).astype(BF)
        right[:, spot] = jnp.where((code & (LANES - 1)) == names, 1.0, 0.0).astype(BF)
        return 0

    lax.fori_loop(0, devices, body, 0, unroll=8)
    total = outer_product(left[...], right[...])
    for g in range(groups):
        total_sum = total[g : g + 1] + total[groups + g : groups + g + 1]
        total_count = total[2 * groups + g : 2 * groups + g + 1] + total[3 * groups + g : 3 * groups + g + 1]
        out[:, LANES * g : LANES * (g + 1)] = total_sum / jnp.maximum(total_count, 1.0)


def swap(one, two, axis, closed):
    n = lax.axis_size(axis)
    if n == 1:
        return jnp.zeros_like(one), jnp.zeros_like(two)
    rounds = [[(i, i + 1) for i in range(start, n - 1, 2)] for start in range(2)]
    if n == 2:
        got = lax.ppermute(one, axis, [(0, 1), (1, 0)])
        return got, got
    if closed and n % 2 == 0:
        rounds[1].append((0, n - 1))
    return tuple(
        lax.ppermute(value, axis, [pair for a, b in pairs for pair in ((a, b), (b, a))])
        for value, pairs in zip((one, two), rounds)
    )


def shards(
    features,
    conv_weight,
    conv_bias,
    head_weight,
    head_bias,
    fragments,
    edge_cells,
    edge_owner,
    edge_count,
    recv_slot,
):
    axes = ("gx", "gy", "gz")
    size = {axis: lax.axis_size(axis) for axis in axes}
    at = {axis: lax.axis_index(axis) for axis in axes}
    devices = size["gx"] * size["gy"] * size["gz"]
    capacity = recv_slot.shape[1] // devices
    slots = edge_cells.shape[1]
    own_slots = devices * capacity // 4
    flags = []
    for axis in axes:
        flags += [at[axis], size[axis] - 1 - at[axis], at[axis] % 2]
    flags = jnp.stack(flags + [edge_count[0]]).astype(jnp.int32)

    xt_low, xt_high, z_one, z_two, x_one, x_two, edge, first_col = pl.pallas_call(
        layout_kernel,
        out_shape=(
            shape((LANES, WIDE), BF),
            shape((LANES, WIDE), BF),
            shape((LANES, WIDE + LANES), BF),
            shape((LANES, WIDE + LANES), BF),
            shape((2 * LANES + 16, LANES), BF),
            shape((2 * LANES + 16, LANES), BF),
            shape((4, EDGE, LANES), BF),
            shape((2, LANES), F32),
        ),
        in_specs=[SMEM, pl.BlockSpec(memory_space=pl.ANY), VMEM],
        out_specs=(VMEM,) * 8,
        scratch_shapes=[
            pltpu.VMEM((4, EDGE, LANES), F32),
            pltpu.VMEM(features.shape, BF),
            pltpu.SemaphoreType.DMA((8,)),
        ],
        compiler_params=pltpu.CompilerParams(vmem_limit_bytes=28 << 20),
        cost_estimate=pl.CostEstimate(flops=1_000_000, bytes_accessed=1 << 20, transcendentals=0),
        name="layout",
    )(flags, features, fragments)
    plane_one, plane_two = swap(z_one, z_two, "gz", False)
    x_got = swap(x_one, x_two, "gx", True)

    acc, inner, outer = call(
        own_kernel,
        "own_planes",
        (shape((GROUPS, LANES, 256), F32), shape((3, 512, 256), BF), shape((2, 256, 3 * LANES), BF)),
        (xt_low, xt_high, conv_weight, conv_bias.reshape(1, -1)),
        0,
        [pltpu.VMEM((27, 32, LANES), BF), pltpu.VMEM((STEP * STACK + 8, 768), F32)],
        flops=5_000_000_000,
    )
    owner = edge_owner.reshape(1, slots)
    rank, place = call(
        slots_kernel,
        "slots",
        (shape((1, slots), jnp.int32), shape((devices, LANES), jnp.int32)),
        (owner, recv_slot),
        0,
    )
    face, x_code, y_one, y_two = call(
        x_face_kernel,
        "x_face",
        (
            shape((2, LANES, LANES), BF),
            shape((2, 1, LANES), F32),
            shape((2, EDGE, LANES), BF),
            shape((2, EDGE, LANES), BF),
        ),
        (*x_got, edge, flags),
        1,
    )
    y_low, y_high, ring_one, ring_two = call(
        ring_kernel,
        "ring",
        (shape((2, EDGE, LANES), BF),) * 2 + (shape((LANES + 2 * EDGE, LANES), BF),) * 2,
        (face, *swap(y_one, y_two, "gy", True), flags),
        1,
    )
    ring_one, ring_two = swap(ring_one, ring_two, "gz", True)

    lines, ends = call(
        edge_kernel,
        "edges",
        (shape((2, GROUPS, 256), F32), shape((2, LANES, 256), F32)),
        (face, y_low, y_high, inner),
        0,
        flops=500_000_000,
    )
    counts = call(
        count_kernel,
        "pair_counts",
        shape((F, 4 * F), F32),
        (fragments, x_code, y_low, first_col, flags),
        1,
        [
            pltpu.VMEM((2, F, 4096), F8),
            pltpu.VMEM((2, F, 4096), F8),
            pltpu.VMEM((2, LANES, LANES), F32),
            pltpu.VMEM((2, LANES, LANES), F32),
        ],
        flops=4_000_000_000,
    )
    affinity, outgoing = call(
        finish_kernel,
        "finish",
        (shape((3, 2, LANES, LANES), BF), shape((devices, 1, LANES), F32)),
        (
            acc,
            plane_one,
            plane_two,
            ring_one,
            ring_two,
            lines,
            ends,
            outer,
            head_weight,
            fragments,
            x_code,
            y_low,
            first_col,
            counts,
            edge_cells,
            owner,
            rank,
            head_bias,
            flags,
        ),
        2,
        [
            pltpu.VMEM((2, LANES, WIDE), BF),
            pltpu.VMEM((2, STEP * STACK + 8, 3 * LANES), F32),
            pltpu.VMEM((2, 2, GROUPS, LANES), F32),
            pltpu.VMEM((6, LANES, LANES), F32),
            pltpu.VMEM((2, 2, F, 2048), BF),
            pltpu.VMEM((2, 2, 3 * F, 2048), BF),
            pltpu.VMEM((2, LANES, LANES), F32),
            pltpu.VMEM((2, LANES, LANES), F32),
            pltpu.VMEM((LANES, LANES), F32),
        ],
        flops=8_000_000_000,
    )
    received = lax.all_to_all(outgoing, axes, split_axis=0, concat_axis=0, tiled=True)
    edge_mean = call(
        settle_kernel,
        "settle",
        shape((1, own_slots), F32),
        (received, place),
        0,
        [pltpu.VMEM((16, devices * LANES), BF), pltpu.VMEM((LANES, devices * LANES), BF)],
    )
    return affinity, edge_mean


def solution(mesh):
    in_specs = (
        P(None, "gz", "gx", "gy"),
        P(),
        P(),
        P(),
        P(),
        P("gz", "gx", "gy"),
        P(None, ("gx", "gy", "gz")),
        P(("gx", "gy", "gz"), None),
        P(("gx", "gy", "gz")),
        P(("gx", "gy", "gz"), None),
    )
    out_specs = (P(None, "gz", "gx", "gy"), P(("gx", "gy", "gz"), None))
    return jax.shard_map(shards, mesh=mesh, in_specs=in_specs, out_specs=out_specs, check_vma=False)
```

```python
import jax
import jax.numpy as jnp
from jax import lax
from jax.experimental import pallas as pl
from jax.experimental.pallas import tpu as pltpu
from jax.sharding import PartitionSpec as P

F = 64
LANES = 128
GROUPS = 32
TILES = GROUPS + 1
WIDE = TILES * LANES
STACK = 8
STEP = LANES + 8
EDGE = 48
HEAD_STACKS = 3
HEAD_GROUPS = HEAD_STACKS * STACK
HEAD = (HEAD_GROUPS + 1) * LANES
HEAD_LINES = 4 * HEAD_GROUPS
BF = jnp.bfloat16
F32 = jnp.float32
F8 = jnp.float8_e4m3fn
VMEM = pl.BlockSpec(memory_space=pltpu.VMEM)
SMEM = pl.BlockSpec(memory_space=pltpu.SMEM)


def call(kernel, name, out_shape, args, smem, scratch=(), flops=1_000_000):
    return pl.pallas_call(
        kernel,
        out_shape=out_shape,
        in_specs=[VMEM] * (len(args) - smem) + [SMEM] * smem,
        out_specs=jax.tree.map(lambda _: VMEM, out_shape),
        scratch_shapes=list(scratch),
        compiler_params=pltpu.CompilerParams(vmem_limit_bytes=28 << 20),
        cost_estimate=pl.CostEstimate(flops=flops, bytes_accessed=1 << 20, transcendentals=0),
        name=name,
    )(*args)


def shape(dims, dtype):
    return jax.ShapeDtypeStruct(dims, dtype)


def iota(dims, axis):
    return lax.broadcasted_iota(jnp.int32, dims, axis)


X_LOW, X_HIGH, X_ODD, Y_LOW, Y_HIGH, Y_ODD, Z_LOW, Z_HIGH, Z_ODD, LIVE = range(10)


def outer_product(left, right):
    return lax.dot_general(left, right, (((1,), (1,)), ((), ())), preferred_element_type=F32)


def halves(value):
    high = value.astype(BF)
    return high, (value - high.astype(F32)).astype(BF)


def layout_kernel(flags, feat, frag, low, high, z_one, z_two, end_one, end_two, x_one, x_two, edge, first_col, rows):
    x_odd, z_odd = flags[X_ODD] > 0, flags[Z_ODD] > 0
    zero = jnp.zeros((32, LANES), BF)
    last = [zero, zero]
    tile_zero = [None, None]
    for t in range(9):
        both = []
        for z, plane in ((0, low), (1, high)):
            if t < 8:
                block = jnp.swapaxes(feat[:, z, 16 * t : 16 * t + 16, :], 0, 1).reshape(512, LANES)
                turned = jnp.concatenate([last[z], block[:480]], axis=0).T
                last[z] = block[480:]
            else:
                turned = jnp.concatenate([last[z], zero, zero, zero], axis=0).T
            wide = turned.shape[1]
            plane[:, 512 * t : 512 * t + wide] = turned
            both.append(turned)
            for side, line in ((0, turned[112:128].astype(F32)[15:16]), (1, turned[0:16].astype(F32)[0:1])):
                for q in range(wide // LANES):
                    spot = 4 * t + q
                    rows[2 * side + z, spot : spot + 1, :] = line[:, LANES * q : LANES * (q + 1)]
            if t == 0:
                tile_zero[z] = turned[:, :LANES]
            if t == 8:
                lines = slice(LANES * z, LANES * (z + 1))
                x_one[lines, :] = jnp.where(x_odd, tile_zero[z], turned)
                x_two[lines, :] = jnp.where(x_odd, turned, tile_zero[z])
        for head, end, value in (
            (z_one, end_one, jnp.where(z_odd, both[0], both[1])),
            (z_two, end_two, jnp.where(z_odd, both[1], both[0])),
        ):
            cut = min(max(HEAD - 512 * t, 0), wide)
            if cut > 0:
                head[:, 512 * t : 512 * t + cut] = value[:, :cut]
            if cut < wide:
                end[:, 512 * t + cut - HEAD : 512 * t + wide - HEAD] = value[:, cut:]
    for z in range(2):
        turned = frag[z].astype(F32).T
        first_col[z : z + 1, :] = turned[0:1]
        for side in range(2):
            rows[2 * side + z, TILES:EDGE, :] = jnp.broadcast_to(turned[127:128], (EDGE - TILES, LANES))
            edge[2 * side + z] = rows[2 * side + z].astype(BF)
    top = frag[1].astype(F32).astype(BF)
    lines = [jnp.broadcast_to(frag[z, 127:128, :], (8, LANES)).astype(F32) for z in range(2)]
    lines = jnp.concatenate(lines, axis=0).astype(BF)
    for out in (z_one, z_two):
        out[:, HEAD:] = top
    for out in (x_one, x_two):
        out[2 * LANES :, :] = lines


def x_face_kernel(got_one, got_two, edge, flags, face, x_code, y_one, y_two):
    has_low, has_high, odd = flags[X_LOW] > 0, flags[X_HIGH] > 0, flags[X_ODD] > 0
    y_odd = flags[Y_ODD] > 0
    lane = iota((LANES, LANES), 1)
    is_low = (lane < 32) & has_low
    is_high = (lane >= 32) & (lane < 64) & has_high
    none = jnp.zeros((LANES, LANES), BF)
    row, place = iota((EDGE, LANES), 0), iota((EDGE, LANES), 1)
    ends = ((row == 0) & (place < 32)) | ((row == TILES - 1) & (place >= 32) & (place < 64))
    other = jnp.where(odd, got_one[2 * LANES :, :], got_two[2 * LANES :, :]).astype(F32)
    for z in range(2):
        lines = slice(LANES * z, LANES * (z + 1))
        low = jnp.where(odd, got_one[lines, :], got_two[lines, :])
        high = jnp.where(odd, got_two[lines, :], got_one[lines, :])
        tile = jnp.where(is_low, low, jnp.where(is_high, high, none))
        face[z] = tile
        patched = []
        for side in range(2):
            near = (tile[112:128].astype(F32)[15:16], tile[0:16].astype(F32)[0:1])[side]
            line = edge[2 * side + z].astype(F32)
            patched.append(jnp.where(ends, jnp.broadcast_to(near, (EDGE, LANES)), line).astype(BF))
        y_one[z] = jnp.where(y_odd, patched[1], patched[0])
        y_two[z] = jnp.where(y_odd, patched[0], patched[1])
        x_code[z] = jnp.where(has_low, other[8 * z : 8 * z + 1], -1.0)


def ring_kernel(face, got_one, got_two, flags, y_low, y_high, z_one, z_two):
    odd, z_odd = flags[Y_ODD] > 0, flags[Z_ODD] > 0
    none = jnp.zeros((EDGE, LANES), BF)
    rings = []
    for z in range(2):
        low = jnp.where(flags[Y_LOW] > 0, jnp.where(odd, got_one[z], got_two[z]), none)
        high = jnp.where(flags[Y_HIGH] > 0, jnp.where(odd, got_two[z], got_one[z]), none)
        y_low[z] = low
        y_high[z] = high
        rings.append(jnp.concatenate([face[z], low, high], axis=0))
    z_one[...] = jnp.where(z_odd, rings[0], rings[1])
    z_two[...] = jnp.where(z_odd, rings[1], rings[0])


def banded(weight, z_off, dy, slot, quarter):
    tile = jnp.zeros((32, LANES), BF)
    if abs(z_off) <= 1:
        for q in range(4):
            dx = slot - 1 - q
            if abs(dx) <= 1:
                tile = jnp.where(quarter == q, weight[9 * (z_off + 1) + 3 * (dx + 1) + dy], tile)
    return tile


def own_kernel(low, high, conv_weight, conv_bias, acc, inner, outer, weight, scr):
    quarter = iota((32, LANES), 1) // 32
    for k in range(27):
        one = conv_weight[k].astype(F32).T.astype(BF)
        weight[k] = jnp.concatenate([one] * 4, axis=1)
    for dy in range(3):
        for slot in range(8):
            for z in range(2):
                line = slice(256 * z + 32 * slot, 256 * z + 32 * slot + 32)
                for zo in range(2):
                    inner[dy, line, LANES * zo : LANES * (zo + 1)] = banded(weight, z - zo, dy, slot, quarter)
                outer[z, 32 * slot : 32 * slot + 32, LANES * dy : LANES * (dy + 1)] = banded(
                    weight, 2 * z - 1, dy, slot, quarter
                )
    bias = jnp.concatenate([conv_bias[...]] * 8, axis=1)
    for g in range(STACK):
        scr[STEP * g + 7 : STEP * g + 8, :] = jnp.zeros((1, 768), F32)
        scr[STEP * g + STEP : STEP * g + STEP + 1, :] = jnp.zeros((1, 768), F32)

    def body(s, _):
        base = s * STACK
        left = jnp.concatenate(
            [
                jnp.concatenate(
                    [plane[:, pl.ds(pl.multiple_of((base + g) * LANES, LANES), 2 * LANES)] for g in range(STACK)],
                    axis=0,
                )
                for plane in (low, high)
            ],
            axis=1,
        )
        for dy in range(3):
            part = jnp.dot(left, inner[dy], preferred_element_type=F32)
            for g in range(STACK):
                scr[STEP * g + 8 : STEP * g + STEP, 256 * dy : 256 * dy + 256] = part[LANES * g : LANES * (g + 1)]
        for g in range(STACK):
            o = STEP * g
            acc[base + g] = (
                scr[o + 7 : o + 135, 0:256] + scr[o + 8 : o + 136, 256:512] + scr[o + 9 : o + 137, 512:768] + bias
            )
        return 0

    lax.fori_loop(0, GROUPS // STACK, body, 0)


def line_windows(chunks):
    wide = chunks.astype(F32)
    return jnp.concatenate([wide[:GROUPS], wide[1:TILES]], axis=1).astype(BF)


def edge_kernel(face, y_low, y_high, inner, lines, ends):
    for side, (dy, source) in enumerate(((0, y_low), (2, y_high))):
        left = jnp.concatenate([line_windows(source[z]) for z in range(2)], axis=1)
        lines[side] = jnp.dot(left, inner[dy], preferred_element_type=F32)
    row = iota((LANES, 256), 0)
    lane = iota((LANES, LANES), 1)
    none = jnp.zeros((LANES, LANES), BF)
    for end in range(2):
        keep = lane < 32 if end == 0 else lane >= 32
        tiles = [jnp.where(keep, face[z], none) for z in range(2)]
        parts = []
        for dy in range(3):
            right = [inner[dy, 256 * z + LANES * end : 256 * z + LANES * end + LANES, :] for z in range(2)]
            parts.append(
                jnp.dot(
                    jnp.concatenate(tiles, axis=1), jnp.concatenate(right, axis=0), preferred_element_type=F32
                )
            )
        ends[end] = (
            jnp.where(row == 0, 0.0, pltpu.roll(parts[0], 1, 0))
            + parts[1]
            + jnp.where(row == LANES - 1, 0.0, pltpu.roll(parts[2], LANES - 1, 0))
        )


def spread(row, copies):
    one = jnp.broadcast_to(row, (16, LANES)).astype(BF)
    return jnp.concatenate([one] * copies, axis=0)


def numbers(rows):
    return iota((rows, LANES), 0).astype(F32).astype(BF)


def line_partners(frag, y_code, x, first, hot_before):
    names = numbers(F)
    line = pl.ds(x, 1)
    hot = [spread(frag[z, line, :], 4) == names for z in range(2)]
    if hot_before is None:
        before = [frag[z, pl.ds(jnp.maximum(x - 1, 0), 1), :] + first for z in range(2)]
        hot_before = [spread(row, 4) == names for row in before]
    y_hot = [spread(y_code[z, line, :], 4) == names for z in range(2)]
    return hot, hot_before, y_hot


def faces_product(own, partner, weight):
    names = numbers(F)
    one, none = jnp.ones((F, LANES), BF), jnp.zeros((F, LANES), BF)
    left = [jnp.where(spread(row, 4) == names, one, none) for row in own]
    right = [jnp.where(spread(row, 4) == names, spread(value, 4), none) for row, value in zip(partner, weight)]
    return outer_product(jnp.concatenate(left, axis=1), jnp.concatenate(right, axis=1))


def load_numbers(frag, plain, y_code):
    lane = iota((LANES, LANES), 1)
    for z in range(2):
        value = frag[z].astype(F32)
        plain[z] = value
        y_code[z] = jnp.where(lane == 0, -1.0, pltpu.roll(value, 1, 1))


def y_partner(y_low, z, has_low):
    return jnp.where(has_low, y_low[z, TILES - 1 :, :].astype(F32)[8:9], -1.0)


def count_kernel(frag, x_code, y_low, first_col, flags, out, plain, y_code, own_hot, pair_hot):
    load_numbers(frag, plain, y_code)
    one = jnp.ones((F, LANES), BF)
    none = jnp.zeros((F, LANES), BF)

    def body(t, total):
        hot_before = None
        first = jnp.where(t > 0, 0.0, -128.0)
        for j in range(32):
            spot = slice(LANES * j, LANES * (j + 1))
            hot, x_hot, y_hot = line_partners(plain, y_code, 32 * t + j, first, hot_before)
            hot_before = hot
            for z in range(2):
                own_hot[z, :, spot] = jnp.where(hot[z], one, none).astype(F8)
                pairs = jnp.where(x_hot[z], one, none) + jnp.where(y_hot[z], one, none)
                if z == 1:
                    pairs = pairs + jnp.where(hot[0], one, none)
                pair_hot[z, :, spot] = pairs.astype(F8)
        for z in range(2):
            total = total + outer_product(own_hot[z], pair_hot[z])
        return total

    own = lax.fori_loop(0, 4, body, jnp.zeros((F, F), F32))
    ones = [jnp.ones((1, LANES), F32)] * 2
    x_outer = faces_product([plain[z, 0:1, :] for z in range(2)], [x_code[z] for z in range(2)], ones)
    y_outer = faces_product(
        [first_col[z : z + 1, :] for z in range(2)], [y_partner(y_low, z, flags[Y_LOW] > 0) for z in range(2)], ones
    )
    out[...] = jnp.concatenate([own, jnp.zeros((F, F), F32), x_outer, y_outer], axis=1)


def slots_kernel(cells, owner, recv, rank_hot, column_hot, group, name_hot, place):
    slots = owner.shape[1]
    devices = group.shape[0]
    capacity = recv.shape[1] // devices
    hot = iota((devices, slots), 0) == owner[...]
    before = iota((slots, slots), 0) < iota((slots, slots), 1)
    earlier = jnp.dot(
        jnp.where(hot, 1.0, 0.0).astype(BF), jnp.where(before, 1.0, 0.0).astype(BF), preferred_element_type=F32
    )
    rank = jnp.sum(jnp.where(hot, earlier, 0.0), axis=0, keepdims=True).astype(jnp.int32)
    lanes = iota((LANES, slots), 0)
    rank_hot[0] = jnp.where(lanes == rank, 1.0, 0.0).astype(BF)
    rank_hot[1] = jnp.where(lanes == rank + F, 1.0, 0.0).astype(BF)
    code = jnp.concatenate([cells[0:1, :], cells[1:2, :]], axis=1)
    column_hot[...] = jnp.where(iota((4 * F, 2 * slots), 0) == (code & (4 * F - 1)), 1.0, 0.0).astype(BF)
    place[...] = jnp.full(place.shape, -4 * LANES, jnp.int32)
    for p in range(devices):
        piece = recv[:, capacity * p : capacity * (p + 1)]
        place[p : p + 1, 0:capacity] = piece
        place[p : p + 1, F : F + capacity] = piece
    group[...] = place[...] >> 7
    names = iota((LANES, LANES), 0)

    def body(p, _):
        spot = pl.ds(pl.multiple_of(p * LANES, LANES), LANES)
        name_hot[:, spot] = jnp.where((place[pl.ds(p, 1), :] & (LANES - 1)) == names, 1.0, 0.0).astype(BF)
        return 0

    lax.fori_loop(0, devices, body, 0, unroll=8)


def head_rows(head_weight):
    line, spot = iota((8, 256), 0), iota((8, 256), 1)
    head = []
    for d in range(3):
        weights = jnp.concatenate([head_weight[d : d + 1, :].astype(F32)] * 8, axis=1)
        for z in range(2):
            match = (spot // LANES == z) & ((spot // 32) % 4 == line % 4)
            head.append(jnp.where(match, jnp.broadcast_to(weights, (8, 256)), 0.0))
    return jnp.concatenate(head, axis=0).astype(BF)


def stack_affinity(groups, tile, acc, add, planes, outer, lines, head, head_bias, scr, kept, kept_at):
    for i in range(2):
        left = jnp.concatenate(
            [
                planes[i, :, pl.ds(pl.multiple_of((tile + g) * LANES, LANES), 2 * LANES)]
                for g in range(STACK)
            ],
            axis=0,
        )
        part = jnp.dot(left, outer[i], preferred_element_type=F32)
        ends = [lines[side, i, groups, :] for side in range(2)]
        for g in range(STACK):
            o = STEP * g
            scr[i, o + 8 : o + STEP, :] = part[LANES * g : LANES * (g + 1)]
            scr[i, o + 7 : o + 8, 0:LANES] = ends[0][g : g + 1]
            scr[i, o + STEP : o + STEP + 1, 2 * LANES :] = ends[1][g : g + 1]
    hidden = []
    for g in range(STACK):
        o = STEP * g
        outside = [
            scr[i, o + 7 : o + 135, 0:LANES]
            + scr[i, o + 8 : o + 136, LANES : 2 * LANES]
            + scr[i, o + 9 : o + 137, 2 * LANES :]
            for i in range(2)
        ]
        total = acc(g) + jnp.concatenate(outside, axis=1)
        if add[g] is not None:
            total = total + add[g]
        hidden.append(jnp.maximum(total, 0.0).astype(BF))
    logits = outer_product(head, jnp.concatenate(hidden, axis=0))
    top_half = iota((8, LANES), 0) < 4
    for i in range(6):
        for pair in range(STACK // 2):
            at = 2 * LANES * pair
            both = logits[8 * i : 8 * i + 8]
            value = jnp.where(top_half, both[:, at : at + LANES], both[:, at + LANES : at + 2 * LANES])
            value = jax.nn.sigmoid(value + head_bias[i // 2]).astype(BF).astype(F32)
            kept[i, pl.ds(pl.multiple_of(kept_at + 8 * pair, 8), 8), :] = value


def stack_table(x0, kept_at, first, plain, y_code, z_code, kept, own_hot, pair_hot):
    names, one, none = numbers(F), jnp.ones((F, LANES), BF), jnp.zeros((F, LANES), BF)
    hot_before = None
    for j in range(32):
        t, x = j // 16, x0 + j
        spot = slice(LANES * (j % 16), LANES * (j % 16 + 1))
        weight = [spread(kept[i, pl.ds(kept_at + j, 1), :], 4) for i in range(6)]
        hot, x_hot, y_hot = line_partners(plain, y_code, x, first, hot_before)
        hot_before = hot
        for z in range(2):
            own_hot[t, z, :, spot] = jnp.where(hot[z], one, none)
            pair_hot[t, z, 0:F, spot] = jnp.where(x_hot[z], weight[2 + z], none) + jnp.where(
                y_hot[z], weight[4 + z], none
            )
        pair_hot[t, 1, F : 2 * F, spot] = jnp.where(hot[0], weight[1], none)
        z_hot = spread(z_code[pl.ds(x, 1), :], 4) == names
        pair_hot[t, 0, F : 2 * F, spot] = jnp.where(z_hot, weight[0], none)
        pair_hot[t, 0, 2 * F :, spot] = jnp.where(z_hot, one, none)
    low = outer_product(own_hot[0, 0], pair_hot[0, 0]) + outer_product(own_hot[1, 0], pair_hot[1, 0])
    high = outer_product(own_hot[0, 1], pair_hot[0, 1, : 2 * F]) + outer_product(own_hot[1, 1], pair_hot[1, 1, : 2 * F])
    return low, high


def first_kernel(
    acc,
    plane_one,
    plane_two,
    ring_one,
    ring_two,
    inner_lines,
    inner_ends,
    outer,
    head_weight,
    plain,
    y_code,
    x_code,
    head_bias,
    flags,
    affinity,
    kept_y,
    low_out,
    high_out,
    x_outer,
    lines,
    z_code,
    carry,
    planes,
    scr,
    kept,
    own_hot,
    pair_hot,
):
    odd = flags[Z_ODD]
    below = jnp.where(odd > 0, plane_one[:, HEAD:], plane_two[:, HEAD:])
    z_code[...] = jnp.where(flags[Z_LOW] > 0, below.astype(F32), -1.0)
    lane = iota((LANES, LANES), 1)
    for plane, ring, i in ((plane_one, ring_one, 1 - odd), (plane_two, ring_two, odd)):
        live = jnp.where(i > 0, flags[Z_HIGH], flags[Z_LOW]) > 0
        around = jnp.where(live, ring[...], jnp.zeros(ring.shape, BF))
        face = around[:LANES, :]
        planes[i, :, LANES:] = plane[:, LANES:HEAD]
        planes[i, :, :LANES] = jnp.where(lane < 32, face, plane[:, :LANES])
        carry[i] = plane[:, HEAD - LANES : HEAD]
        carry[2 + i] = face
        for side, dy in ((0, 0), (1, 2)):
            chunks = around[LANES + EDGE * side : LANES + EDGE * (side + 1), :]
            lines[side, i] = jnp.dot(
                line_windows(chunks), outer[i, :, LANES * dy : LANES * (dy + 1)], preferred_element_type=F32
            )
    for i in range(2):
        for side in range(2):
            lines[side, i] = lines[side, i] + inner_lines[side, :, LANES * i : LANES * (i + 1)]
    head = head_rows(head_weight)

    def body(s, total):
        base = pl.multiple_of(s * STACK, STACK)
        x0 = pl.multiple_of(4 * STACK * s, 4 * STACK)
        add = [None] * STACK
        add[0] = jnp.where(s == 0, inner_ends[0], 0.0)
        stack_affinity(
            pl.ds(base, STACK), base, lambda g: acc[base + g], add, planes, outer, lines, head, head_bias, scr, kept, x0
        )
        all_lines = pl.ds(x0, 4 * STACK)
        for i in range(6):
            affinity[i // 2, i % 2, all_lines, :] = kept[i, all_lines, :].astype(BF)
        first = jnp.where(s > 0, 0.0, -128.0)
        low, high = stack_table(x0, x0, first, plain, y_code, z_code, kept, own_hot, pair_hot)
        return total[0] + low, total[1] + high

    low, high = lax.fori_loop(0, HEAD_STACKS, body, (jnp.zeros((F, 3 * F), F32), jnp.zeros((F, 2 * F), F32)))
    low_out[...] = low
    high_out[...] = high
    kept_y[...] = kept[4:6]
    x_outer[...] = faces_product(
        [plain[z, 0:1, :] for z in range(2)],
        [x_code[z] for z in range(2)],
        [kept[2 + z, 0:1, :] for z in range(2)],
    )


def second_kernel(
    acc,
    plane_one,
    plane_two,
    inner_ends,
    outer,
    head_weight,
    plain,
    y_code,
    y_low,
    first_col,
    counts,
    affinity_head,
    kept_y,
    low_head,
    high_head,
    x_outer,
    lines,
    z_code,
    carry,
    cells,
    owner,
    rank_hot,
    column_hot,
    head_bias,
    flags,
    affinity,
    outgoing,
    planes,
    scr,
    kept,
    own_hot,
    pair_hot,
):
    odd = flags[Z_ODD]
    lane = iota((LANES, LANES), 1)
    wide = WIDE - HEAD
    for i in range(2):
        planes[i, :, :LANES] = carry[i]
    for plane, i in ((plane_one, 1 - odd), (plane_two, odd)):
        planes[i, :, LANES:wide] = plane[:, : wide - LANES]
        planes[i, :, wide:] = jnp.where((lane >= 32) & (lane < 64), carry[2 + i], plane[:, wide - LANES :])
    add = [None] * STACK
    add[-1] = inner_ends[1]
    groups = pl.ds(HEAD_GROUPS, STACK)
    stack_affinity(
        groups, 0, lambda g: acc[HEAD_GROUPS + g], add, planes, outer, lines, head_rows(head_weight), head_bias, scr, kept, 0
    )
    for i in range(6):
        affinity[i // 2, i % 2, :HEAD_LINES, :] = affinity_head[i // 2, i % 2]
        affinity[i // 2, i % 2, HEAD_LINES:, :] = kept[i].astype(BF)
    low, high = stack_table(HEAD_LINES, 0, 0.0, plain, y_code, z_code, kept, own_hot, pair_hot)
    low, high = low_head[...] + low, high_head[...] + high
    own = low[:, :F] + high[:, :F] + high[:, F:]
    y_outer = faces_product(
        [first_col[z : z + 1, :] for z in range(2)],
        [y_partner(y_low, z, flags[Y_LOW] > 0) for z in range(2)],
        [jnp.concatenate([kept_y[z], kept[4 + z]], axis=0).T[0:1, :] for z in range(2)],
    )
    sums = jnp.concatenate([own, low[:, F : 2 * F], x_outer[...], y_outer], axis=1)
    tally = counts[...] + jnp.concatenate(
        [jnp.zeros((F, F), F32), low[:, 2 * F :], jnp.zeros((F, 2 * F), F32)], axis=1
    )
    slots = cells.shape[1]
    picked = jnp.dot(
        jnp.concatenate(halves(sums) + halves(tally), axis=0), column_hot[...], preferred_element_type=F32
    )
    code = jnp.concatenate([cells[0:1, :], cells[1:2, :]], axis=1)
    line_hot = iota((F, 2 * slots), 0) == (code >> 8)
    alive = iota((1, slots), 1) < flags[LIVE]

    def part_of(value):
        total = jnp.sum(jnp.where(line_hot, value, 0.0), axis=0, keepdims=True)
        return jnp.where(alive, total[:, :slots] + total[:, slots:], 0.0)

    part_sum = part_of(picked[:F] + picked[F : 2 * F])
    part_count = part_of(picked[2 * F : 3 * F] + picked[3 * F :])
    to_owner = iota((outgoing.shape[0], slots), 0) == owner[...]
    left = [
        jnp.where(to_owner, piece.astype(F32), 0.0).astype(BF) for piece in halves(part_sum) + halves(part_count)
    ]
    sent = outer_product(
        jnp.concatenate(left, axis=1),
        jnp.concatenate([rank_hot[0], rank_hot[0], rank_hot[1], rank_hot[1]], axis=1),
    )
    outgoing[...] = sent.reshape(outgoing.shape)


def settle_kernel(received, group_of, name_hot, out, left):
    devices = received.shape[0]
    groups = out.shape[1] // LANES
    row, lane = iota((16, LANES), 0), iota((16, LANES), 1)
    of_count = row >= 2 * groups
    inner = jnp.where(of_count, row - 2 * groups, row)
    is_low = inner >= groups
    group = jnp.where(is_low, inner - groups, inner)
    group = jnp.where((lane >= F) == of_count, group, -1)
    group = jnp.where(row < 4 * groups, group, -1)

    def body(p, _):
        spot = pl.ds(pl.multiple_of(p * LANES, LANES), LANES)
        value = received[p]
        high = value.astype(BF).astype(F32)
        piece = jnp.where(is_low, value - high, high)
        left[:, spot] = jnp.where(group_of[pl.ds(p, 1), :] == group, piece, 0.0).astype(BF)
        return 0

    lax.fori_loop(0, devices, body, 0, unroll=8)
    total = outer_product(left[...], name_hot[...])
    for g in range(groups):
        total_sum = total[g : g + 1] + total[groups + g : groups + g + 1]
        total_count = total[2 * groups + g : 2 * groups + g + 1] + total[3 * groups + g : 3 * groups + g + 1]
        out[:, LANES * g : LANES * (g + 1)] = total_sum / jnp.maximum(total_count, 1.0)


def swap(one, two, axis, closed):
    n = lax.axis_size(axis)
    if n == 1:
        return jnp.zeros_like(one), jnp.zeros_like(two)
    rounds = [[(i, i + 1) for i in range(start, n - 1, 2)] for start in range(2)]
    if n == 2:
        got = lax.ppermute(one, axis, [(0, 1), (1, 0)])
        return got, got
    if closed and n % 2 == 0:
        rounds[1].append((0, n - 1))
    return tuple(
        lax.ppermute(value, axis, [pair for a, b in pairs for pair in ((a, b), (b, a))])
        for value, pairs in zip((one, two), rounds)
    )


def shards(
    features,
    conv_weight,
    conv_bias,
    head_weight,
    head_bias,
    fragments,
    edge_cells,
    edge_owner,
    edge_count,
    recv_slot,
):
    axes = ("gx", "gy", "gz")
    size = {axis: lax.axis_size(axis) for axis in axes}
    at = {axis: lax.axis_index(axis) for axis in axes}
    devices = size["gx"] * size["gy"] * size["gz"]
    capacity = recv_slot.shape[1] // devices
    slots = edge_cells.shape[1]
    own_slots = devices * capacity // 4
    flags = []
    for axis in axes:
        flags += [at[axis], size[axis] - 1 - at[axis], at[axis] % 2]
    flags = jnp.stack(flags + [edge_count[0]]).astype(jnp.int32)

    xt_low, xt_high, z_one, z_two, end_one, end_two, x_one, x_two, edge, first_col = pl.pallas_call(
        layout_kernel,
        out_shape=(
            shape((LANES, WIDE), BF),
            shape((LANES, WIDE), BF),
            shape((LANES, HEAD + LANES), BF),
            shape((LANES, HEAD + LANES), BF),
            shape((LANES, WIDE - HEAD), BF),
            shape((LANES, WIDE - HEAD), BF),
            shape((2 * LANES + 16, LANES), BF),
            shape((2 * LANES + 16, LANES), BF),
            shape((4, EDGE, LANES), BF),
            shape((2, LANES), F32),
        ),
        in_specs=[SMEM, VMEM, VMEM],
        out_specs=(VMEM,) * 10,
        scratch_shapes=[pltpu.VMEM((4, EDGE, LANES), F32)],
        compiler_params=pltpu.CompilerParams(vmem_limit_bytes=28 << 20),
        cost_estimate=pl.CostEstimate(flops=1_000_000, bytes_accessed=1 << 20, transcendentals=0),
        name="layout",
    )(flags, features, fragments)
    plane_one, plane_two = swap(z_one, z_two, "gz", False)
    x_got = swap(x_one, x_two, "gx", True)

    acc, inner, outer = call(
        own_kernel,
        "own_planes",
        (shape((GROUPS, LANES, 256), F32), shape((3, 512, 256), BF), shape((2, 256, 3 * LANES), BF)),
        (xt_low, xt_high, conv_weight, conv_bias.reshape(1, -1)),
        0,
        [pltpu.VMEM((27, 32, LANES), BF), pltpu.VMEM((STEP * STACK + 8, 768), F32)],
        flops=5_000_000_000,
    )
    owner = edge_owner.reshape(1, slots)
    rank_hot, column_hot, group, name_hot = call(
        slots_kernel,
        "slots",
        (
            shape((2, LANES, slots), BF),
            shape((4 * F, 2 * slots), BF),
            shape((devices, LANES), jnp.int32),
            shape((LANES, devices * LANES), BF),
        ),
        (edge_cells, owner, recv_slot),
        0,
        [pltpu.VMEM((devices, LANES), jnp.int32)],
    )
    face, x_code, y_one, y_two = call(
        x_face_kernel,
        "x_face",
        (
            shape((2, LANES, LANES), BF),
            shape((2, 1, LANES), F32),
            shape((2, EDGE, LANES), BF),
            shape((2, EDGE, LANES), BF),
        ),
        (*x_got, edge, flags),
        1,
    )
    y_low, y_high, ring_one, ring_two = call(
        ring_kernel,
        "ring",
        (shape((2, EDGE, LANES), BF),) * 2 + (shape((LANES + 2 * EDGE, LANES), BF),) * 2,
        (face, *swap(y_one, y_two, "gy", True), flags),
        1,
    )
    ring_one, ring_two = swap(ring_one, ring_two, "gz", True)

    lines, ends = call(
        edge_kernel,
        "edges",
        (shape((2, GROUPS, 256), F32), shape((2, LANES, 256), F32)),
        (face, y_low, y_high, inner),
        0,
        flops=500_000_000,
    )
    counts, plain, y_code = call(
        count_kernel,
        "pair_counts",
        (shape((F, 4 * F), F32), shape((2, LANES, LANES), F32), shape((2, LANES, LANES), F32)),
        (fragments, x_code, y_low, first_col, flags),
        1,
        [pltpu.VMEM((2, F, 4096), F8), pltpu.VMEM((2, F, 4096), F8)],
        flops=4_000_000_000,
    )
    end_one, end_two, counts = lax.optimization_barrier((end_one, end_two, counts))
    end_one, end_two = swap(end_one, end_two, "gz", False)

    def stack_scratch(tiles, kept_lines):
        return [
            pltpu.VMEM((2, LANES, tiles * LANES), BF),
            pltpu.VMEM((2, STEP * STACK + 8, 3 * LANES), F32),
            pltpu.VMEM((6, kept_lines, LANES), F32),
            pltpu.VMEM((2, 2, F, 2048), BF),
            pltpu.VMEM((2, 2, 3 * F, 2048), BF),
        ]

    done = call(
        first_kernel,
        "first_lines",
        (
            shape((3, 2, HEAD_LINES, LANES), BF),
            shape((2, HEAD_LINES, LANES), F32),
            shape((F, 3 * F), F32),
            shape((F, 2 * F), F32),
            shape((F, F), F32),
            shape((2, 2, GROUPS, LANES), F32),
            shape((LANES, LANES), F32),
            shape((4, LANES, LANES), BF),
        ),
        (
            acc,
            plane_one,
            plane_two,
            ring_one,
            ring_two,
            lines,
            ends,
            outer,
            head_weight,
            plain,
            y_code,
            x_code,
            head_bias,
            flags,
        ),
        2,
        stack_scratch(HEAD_GROUPS + 1, HEAD_LINES),
        flops=6_000_000_000,
    )
    affinity, outgoing = call(
        second_kernel,
        "last_lines",
        (shape((3, 2, LANES, LANES), BF), shape((devices, 1, LANES), F32)),
        (
            acc,
            end_one,
            end_two,
            ends,
            outer,
            head_weight,
            plain,
            y_code,
            y_low,
            first_col,
            counts,
            *done,
            edge_cells,
            owner,
            rank_hot,
            column_hot,
            head_bias,
            flags,
        ),
        2,
        stack_scratch(TILES - HEAD_GROUPS, LANES - HEAD_LINES),
        flops=3_000_000_000,
    )
    received = lax.all_to_all(outgoing, axes, split_axis=0, concat_axis=0, tiled=True)
    edge_mean = call(
        settle_kernel,
        "settle",
        shape((1, own_slots), F32),
        (received, group, name_hot),
        0,
        [pltpu.VMEM((16, devices * LANES), BF)],
    )
    return affinity, edge_mean


def solution(mesh):
    in_specs = (
        P(None, "gz", "gx", "gy"),
        P(),
        P(),
        P(),
        P(),
        P("gz", "gx", "gy"),
        P(None, ("gx", "gy", "gz")),
        P(("gx", "gy", "gz"), None),
        P(("gx", "gy", "gz")),
        P(("gx", "gy", "gz"), None),
    )
    out_specs = (P(None, "gz", "gx", "gy"), P(("gx", "gy", "gz"), None))
    return jax.shard_map(shards, mesh=mesh, in_specs=in_specs, out_specs=out_specs, check_vma=False)
```

```python
import jax
import jax.numpy as jnp
from jax import lax
from jax.experimental import pallas as pl
from jax.experimental.pallas import tpu as pltpu
from jax.sharding import PartitionSpec as P

F = 64
LANES = 128
GROUPS = 32
TILES = GROUPS + 1
WIDE = TILES * LANES
STACK = 8
STEP = LANES + 8
EDGE = 48
RING = LANES + 2 * EDGE
HEAD_STACKS = 3
HEAD_GROUPS = HEAD_STACKS * STACK
HEAD = (HEAD_GROUPS + 1) * LANES
HEAD_LINES = 4 * HEAD_GROUPS
BF = jnp.bfloat16
F32 = jnp.float32
F8 = jnp.float8_e4m3fn
VMEM = pl.BlockSpec(memory_space=pltpu.VMEM)
SMEM = pl.BlockSpec(memory_space=pltpu.SMEM)


def call(kernel, name, out_shape, args, smem, scratch=(), flops=1_000_000):
    return pl.pallas_call(
        kernel,
        out_shape=out_shape,
        in_specs=[VMEM] * (len(args) - smem) + [SMEM] * smem,
        out_specs=jax.tree.map(lambda _: VMEM, out_shape),
        scratch_shapes=list(scratch),
        compiler_params=pltpu.CompilerParams(vmem_limit_bytes=28 << 20),
        cost_estimate=pl.CostEstimate(flops=flops, bytes_accessed=1 << 17, transcendentals=0),
        name=name,
    )(*args)


def shape(dims, dtype):
    return jax.ShapeDtypeStruct(dims, dtype)


def iota(dims, axis):
    return lax.broadcasted_iota(jnp.int32, dims, axis)


X_LOW, X_HIGH, X_ODD, Y_LOW, Y_HIGH, Y_ODD, Z_LOW, Z_HIGH, Z_ODD, LIVE = range(10)


def outer_product(left, right):
    return lax.dot_general(left, right, (((1,), (1,)), ((), ())), preferred_element_type=F32)


def halves(value):
    high = value.astype(BF)
    return high, (value - high.astype(F32)).astype(BF)


def layout_kernel(flags, feat_hbm, low, high, z_one, z_two, end_one, end_two, feat, sems):
    copies = []
    for t in range(8):
        lines = slice(16 * t, 16 * t + 16)
        copies.append(pltpu.make_async_copy(feat_hbm.at[:, :, lines, :], feat.at[:, :, lines, :], sems.at[t]))
        copies[-1].start()
    odd = flags[Z_ODD] > 0
    zero = jnp.zeros((32, LANES), BF)
    last = [zero, zero]
    for t in range(9):
        if t < 8:
            copies[t].wait()
        both = []
        for z, plane in ((0, low), (1, high)):
            if t < 8:
                block = jnp.swapaxes(feat[:, z, 16 * t : 16 * t + 16, :], 0, 1).reshape(512, LANES)
                turned = jnp.concatenate([last[z], block[:480]], axis=0).T
                last[z] = block[480:]
            else:
                turned = jnp.concatenate([last[z], zero, zero, zero], axis=0).T
            wide = turned.shape[1]
            plane[:, 512 * t : 512 * t + wide] = turned
            both.append(turned)
        for head, end, value in (
            (z_one, end_one, jnp.where(odd, both[0], both[1])),
            (z_two, end_two, jnp.where(odd, both[1], both[0])),
        ):
            cut = min(max(HEAD - 512 * t, 0), wide)
            if cut > 0:
                head[:, 512 * t : 512 * t + cut] = value[:, :cut]
            if cut < wide:
                end[:, 512 * t + cut - HEAD : 512 * t + wide - HEAD] = value[:, cut:]


def face_kernel(low, high, frag, flags, x_one, x_two, edge, first_col, rows):
    odd = flags[X_ODD] > 0
    for z, plane in ((0, low), (1, high)):
        lines = slice(LANES * z, LANES * (z + 1))
        start, end = plane[:, :LANES], plane[:, WIDE - LANES :]
        x_one[lines, :] = jnp.where(odd, start, end)
        x_two[lines, :] = jnp.where(odd, end, start)
        turned = frag[z].astype(F32).T
        first_col[z : z + 1, :] = turned[0:1]
        for side, line in ((0, plane[112:128, :].astype(F32)[15:16]), (1, plane[0:16, :].astype(F32)[0:1])):
            for q in range(TILES):
                rows[2 * side + z, q : q + 1, :] = line[:, LANES * q : LANES * (q + 1)]
            rows[2 * side + z, TILES:EDGE, :] = jnp.broadcast_to(turned[127:128], (EDGE - TILES, LANES))
            edge[2 * side + z] = rows[2 * side + z].astype(BF)
    lines = [jnp.broadcast_to(frag[z, 127:128, :], (8, LANES)).astype(F32) for z in range(2)]
    lines = jnp.concatenate(lines, axis=0).astype(BF)
    for out in (x_one, x_two):
        out[2 * LANES :, :] = lines


def x_face_kernel(got_one, got_two, edge, flags, face, x_code, y_one, y_two):
    has_low, has_high, odd = flags[X_LOW] > 0, flags[X_HIGH] > 0, flags[X_ODD] > 0
    y_odd = flags[Y_ODD] > 0
    lane = iota((LANES, LANES), 1)
    is_low = (lane < 32) & has_low
    is_high = (lane >= 32) & (lane < 64) & has_high
    none = jnp.zeros((LANES, LANES), BF)
    row, place = iota((EDGE, LANES), 0), iota((EDGE, LANES), 1)
    ends = ((row == 0) & (place < 32)) | ((row == TILES - 1) & (place >= 32) & (place < 64))
    other = jnp.where(odd, got_one[2 * LANES :, :], got_two[2 * LANES :, :]).astype(F32)
    for z in range(2):
        lines = slice(LANES * z, LANES * (z + 1))
        low = jnp.where(odd, got_one[lines, :], got_two[lines, :])
        high = jnp.where(odd, got_two[lines, :], got_one[lines, :])
        tile = jnp.where(is_low, low, jnp.where(is_high, high, none))
        face[z] = tile
        patched = []
        for side in range(2):
            near = (tile[112:128].astype(F32)[15:16], tile[0:16].astype(F32)[0:1])[side]
            line = edge[2 * side + z].astype(F32)
            patched.append(jnp.where(ends, jnp.broadcast_to(near, (EDGE, LANES)), line).astype(BF))
        y_one[z] = jnp.where(y_odd, patched[1], patched[0])
        y_two[z] = jnp.where(y_odd, patched[0], patched[1])
        x_code[z] = jnp.where(has_low, other[8 * z : 8 * z + 1], -1.0)


def ring_kernel(face, got_one, got_two, frag, flags, y_low, y_high, z_one, z_two):
    odd, z_odd = flags[Y_ODD] > 0, flags[Z_ODD] > 0
    none = jnp.zeros((EDGE, LANES), BF)
    rings = []
    for z in range(2):
        low = jnp.where(flags[Y_LOW] > 0, jnp.where(odd, got_one[z], got_two[z]), none)
        high = jnp.where(flags[Y_HIGH] > 0, jnp.where(odd, got_two[z], got_one[z]), none)
        y_low[z] = low
        y_high[z] = high
        rings.append(jnp.concatenate([face[z], low, high], axis=0))
    z_one[:RING, :] = jnp.where(z_odd, rings[0], rings[1])
    z_two[:RING, :] = jnp.where(z_odd, rings[1], rings[0])
    top = frag[1].astype(F32).astype(BF)
    for out in (z_one, z_two):
        out[RING:, :] = top


def banded(weight, z_off, dy, slot, quarter):
    tile = jnp.zeros((32, LANES), BF)
    if abs(z_off) <= 1:
        for q in range(4):
            dx = slot - 1 - q
            if abs(dx) <= 1:
                tile = jnp.where(quarter == q, weight[9 * (z_off + 1) + 3 * (dx + 1) + dy], tile)
    return tile


def own_kernel(low, high, conv_weight, conv_bias, acc, inner, outer, weight, scr):
    quarter = iota((32, LANES), 1) // 32
    for k in range(27):
        one = conv_weight[k].astype(F32).T.astype(BF)
        weight[k] = jnp.concatenate([one] * 4, axis=1)
    for dy in range(3):
        for slot in range(8):
            for z in range(2):
                line = slice(256 * z + 32 * slot, 256 * z + 32 * slot + 32)
                for zo in range(2):
                    inner[dy, line, LANES * zo : LANES * (zo + 1)] = banded(weight, z - zo, dy, slot, quarter)
                outer[z, 32 * slot : 32 * slot + 32, LANES * dy : LANES * (dy + 1)] = banded(
                    weight, 2 * z - 1, dy, slot, quarter
                )
    bias = jnp.concatenate([conv_bias[...]] * 8, axis=1)
    for g in range(STACK):
        scr[STEP * g + 7 : STEP * g + 8, :] = jnp.zeros((1, 768), F32)
        scr[STEP * g + STEP : STEP * g + STEP + 1, :] = jnp.zeros((1, 768), F32)

    def body(s, _):
        base = s * STACK
        left = jnp.concatenate(
            [
                jnp.concatenate(
                    [plane[:, pl.ds(pl.multiple_of((base + g) * LANES, LANES), 2 * LANES)] for g in range(STACK)],
                    axis=0,
                )
                for plane in (low, high)
            ],
            axis=1,
        )
        for dy in range(3):
            part = jnp.dot(left, inner[dy], preferred_element_type=F32)
            for g in range(STACK):
                scr[STEP * g + 8 : STEP * g + STEP, 256 * dy : 256 * dy + 256] = part[LANES * g : LANES * (g + 1)]
        for g in range(STACK):
            o = STEP * g
            acc[base + g] = (
                scr[o + 7 : o + 135, 0:256] + scr[o + 8 : o + 136, 256:512] + scr[o + 9 : o + 137, 512:768] + bias
            )
        return 0

    lax.fori_loop(0, GROUPS // STACK, body, 0)


def line_windows(chunks):
    wide = chunks.astype(F32)
    return jnp.concatenate([wide[:GROUPS], wide[1:TILES]], axis=1).astype(BF)


def edge_kernel(
    face, y_low, y_high, inner, plain, x_code, first_col, own_counts, flags, lines, ends, counts
):
    for side, (dy, source) in enumerate(((0, y_low), (2, y_high))):
        left = jnp.concatenate([line_windows(source[z]) for z in range(2)], axis=1)
        lines[side] = jnp.dot(left, inner[dy], preferred_element_type=F32)
    row = iota((LANES, 256), 0)
    lane = iota((LANES, LANES), 1)
    none = jnp.zeros((LANES, LANES), BF)
    for end in range(2):
        keep = lane < 32 if end == 0 else lane >= 32
        tiles = [jnp.where(keep, face[z], none) for z in range(2)]
        parts = []
        for dy in range(3):
            right = [inner[dy, 256 * z + LANES * end : 256 * z + LANES * end + LANES, :] for z in range(2)]
            parts.append(
                jnp.dot(
                    jnp.concatenate(tiles, axis=1), jnp.concatenate(right, axis=0), preferred_element_type=F32
                )
            )
        ends[end] = (
            jnp.where(row == 0, 0.0, pltpu.roll(parts[0], 1, 0))
            + parts[1]
            + jnp.where(row == LANES - 1, 0.0, pltpu.roll(parts[2], LANES - 1, 0))
        )
    ones = [jnp.ones((1, LANES), F32)] * 2
    x_outer = faces_product([plain[z, 0:1, :] for z in range(2)], [x_code[z] for z in range(2)], ones)
    y_outer = faces_product(
        [first_col[z : z + 1, :] for z in range(2)], [y_partner(y_low, z, flags[Y_LOW] > 0) for z in range(2)], ones
    )
    counts[...] = jnp.concatenate([own_counts[...], jnp.zeros((F, F), F32), x_outer, y_outer], axis=1)


def spread(row, copies):
    one = jnp.broadcast_to(row, (16, LANES)).astype(BF)
    return jnp.concatenate([one] * copies, axis=0)


def numbers(rows):
    return iota((rows, LANES), 0).astype(F32).astype(BF)


def line_partners(frag, y_code, x, first, hot_before):
    names = numbers(F)
    line = pl.ds(x, 1)
    hot = [spread(frag[z, line, :], 4) == names for z in range(2)]
    if hot_before is None:
        before = [frag[z, pl.ds(jnp.maximum(x - 1, 0), 1), :] + first for z in range(2)]
        hot_before = [spread(row, 4) == names for row in before]
    y_hot = [spread(y_code[z, line, :], 4) == names for z in range(2)]
    return hot, hot_before, y_hot


def faces_product(own, partner, weight):
    names = numbers(F)
    one, none = jnp.ones((F, LANES), BF), jnp.zeros((F, LANES), BF)
    left = [jnp.where(spread(row, 4) == names, one, none) for row in own]
    right = [jnp.where(spread(row, 4) == names, spread(value, 4), none) for row, value in zip(partner, weight)]
    return outer_product(jnp.concatenate(left, axis=1), jnp.concatenate(right, axis=1))


def load_numbers(frag, plain, y_code):
    lane = iota((LANES, LANES), 1)
    for z in range(2):
        value = frag[z].astype(F32)
        plain[z] = value
        y_code[z] = jnp.where(lane == 0, -1.0, pltpu.roll(value, 1, 1))


def y_partner(y_low, z, has_low):
    return jnp.where(has_low, y_low[z, TILES - 1 :, :].astype(F32)[8:9], -1.0)


def count_kernel(frag, out, plain, y_code, own_hot, pair_hot):
    load_numbers(frag, plain, y_code)
    one = jnp.ones((F, LANES), BF)
    none = jnp.zeros((F, LANES), BF)

    def body(t, total):
        hot_before = None
        first = jnp.where(t > 0, 0.0, -128.0)
        for j in range(32):
            spot = slice(LANES * j, LANES * (j + 1))
            hot, x_hot, y_hot = line_partners(plain, y_code, 32 * t + j, first, hot_before)
            hot_before = hot
            for z in range(2):
                own_hot[z, :, spot] = jnp.where(hot[z], one, none).astype(F8)
                pairs = jnp.where(x_hot[z], one, none) + jnp.where(y_hot[z], one, none)
                if z == 1:
                    pairs = pairs + jnp.where(hot[0], one, none)
                pair_hot[z, :, spot] = pairs.astype(F8)
        for z in range(2):
            total = total + outer_product(own_hot[z], pair_hot[z])
        return total

    out[...] = lax.fori_loop(0, 4, body, jnp.zeros((F, F), F32))


def slots_kernel(cells, owner, recv, rank_hot, column_hot, group, name_hot, place):
    slots = owner.shape[1]
    devices = group.shape[0]
    capacity = recv.shape[1] // devices
    hot = iota((devices, slots), 0) == owner[...]
    before = iota((slots, slots), 0) < iota((slots, slots), 1)
    earlier = jnp.dot(
        jnp.where(hot, 1.0, 0.0).astype(BF), jnp.where(before, 1.0, 0.0).astype(BF), preferred_element_type=F32
    )
    rank = jnp.sum(jnp.where(hot, earlier, 0.0), axis=0, keepdims=True).astype(jnp.int32)
    lanes = iota((LANES, slots), 0)
    rank_hot[0] = jnp.where(lanes == rank, 1.0, 0.0).astype(BF)
    rank_hot[1] = jnp.where(lanes == rank + F, 1.0, 0.0).astype(BF)
    code = jnp.concatenate([cells[0:1, :], cells[1:2, :]], axis=1)
    column_hot[...] = jnp.where(iota((4 * F, 2 * slots), 0) == (code & (4 * F - 1)), 1.0, 0.0).astype(BF)
    place[...] = jnp.full(place.shape, -4 * LANES, jnp.int32)
    for p in range(devices):
        piece = recv[:, capacity * p : capacity * (p + 1)]
        place[p : p + 1, 0:capacity] = piece
        place[p : p + 1, F : F + capacity] = piece
    group[...] = place[...] >> 7
    names = iota((LANES, LANES), 0)

    def body(p, _):
        spot = pl.ds(pl.multiple_of(p * LANES, LANES), LANES)
        name_hot[:, spot] = jnp.where((place[pl.ds(p, 1), :] & (LANES - 1)) == names, 1.0, 0.0).astype(BF)
        return 0

    lax.fori_loop(0, devices, body, 0, unroll=8)


def ahead_kernel(
    cells,
    owner,
    recv,
    frag,
    rank_hot,
    column_hot,
    group,
    name_hot,
    counts,
    plain,
    y_code,
    place,
    own_hot,
    pair_hot,
):
    count_kernel(frag, counts, plain, y_code, own_hot, pair_hot)
    slots_kernel(cells, owner, recv, rank_hot, column_hot, group, name_hot, place)


def head_rows(head_weight):
    line, spot = iota((8, 256), 0), iota((8, 256), 1)
    head = []
    for d in range(3):
        weights = jnp.concatenate([head_weight[d : d + 1, :].astype(F32)] * 8, axis=1)
        for z in range(2):
            match = (spot // LANES == z) & ((spot // 32) % 4 == line % 4)
            head.append(jnp.where(match, jnp.broadcast_to(weights, (8, 256)), 0.0))
    return jnp.concatenate(head, axis=0).astype(BF)


def stack_affinity(groups, tile, acc, add, planes, outer, lines, head, head_bias, scr, kept, kept_at):
    for i in range(2):
        left = jnp.concatenate(
            [
                planes[i, :, (tile + g) * LANES : (tile + g + 2) * LANES]
                for g in range(STACK)
            ],
            axis=0,
        )
        part = jnp.dot(left, outer[i], preferred_element_type=F32)
        ends = [lines[side, i, groups, :] for side in range(2)]
        for g in range(STACK):
            o = STEP * g
            scr[i, o + 8 : o + STEP, :] = part[LANES * g : LANES * (g + 1)]
            scr[i, o + 7 : o + 8, 0:LANES] = ends[0][g : g + 1]
            scr[i, o + STEP : o + STEP + 1, 2 * LANES :] = ends[1][g : g + 1]
    hidden = []
    for g in range(STACK):
        o = STEP * g
        outside = [
            scr[i, o + 7 : o + 135, 0:LANES]
            + scr[i, o + 8 : o + 136, LANES : 2 * LANES]
            + scr[i, o + 9 : o + 137, 2 * LANES :]
            for i in range(2)
        ]
        total = acc(g) + jnp.concatenate(outside, axis=1)
        if add[g] is not None:
            total = total + add[g]
        hidden.append(jnp.maximum(total, 0.0).astype(BF))
    logits = outer_product(head, jnp.concatenate(hidden, axis=0))
    top_half = iota((8, LANES), 0) < 4
    for i in range(6):
        for pair in range(STACK // 2):
            at = 2 * LANES * pair
            both = logits[8 * i : 8 * i + 8]
            value = jnp.where(top_half, both[:, at : at + LANES], both[:, at + LANES : at + 2 * LANES])
            value = jax.nn.sigmoid(value + head_bias[i // 2]).astype(BF).astype(F32)
            kept[i, kept_at + 8 * pair : kept_at + 8 * pair + 8, :] = value


def stack_table(x0, kept_at, first, plain, y_code, z_code, kept, own_hot, pair_hot):
    names, one, none = numbers(F), jnp.ones((F, LANES), BF), jnp.zeros((F, LANES), BF)
    hot_before = None
    for j in range(32):
        t, x = j // 16, x0 + j
        spot = slice(LANES * (j % 16), LANES * (j % 16 + 1))
        weight = [spread(kept[i, pl.ds(kept_at + j, 1), :], 4) for i in range(6)]
        hot, x_hot, y_hot = line_partners(plain, y_code, x, first, hot_before)
        hot_before = hot
        for z in range(2):
            own_hot[t, z, :, spot] = jnp.where(hot[z], one, none)
            pair_hot[t, z, 0:F, spot] = jnp.where(x_hot[z], weight[2 + z], none) + jnp.where(
                y_hot[z], weight[4 + z], none
            )
        pair_hot[t, 1, F : 2 * F, spot] = jnp.where(hot[0], weight[1], none)
        z_hot = spread(z_code[pl.ds(x, 1), :], 4) == names
        pair_hot[t, 0, F : 2 * F, spot] = jnp.where(z_hot, weight[0], none)
        pair_hot[t, 0, 2 * F :, spot] = jnp.where(z_hot, one, none)
    low = outer_product(own_hot[0, 0], pair_hot[0, 0]) + outer_product(own_hot[1, 0], pair_hot[1, 0])
    high = outer_product(own_hot[0, 1], pair_hot[0, 1, : 2 * F]) + outer_product(own_hot[1, 1], pair_hot[1, 1, : 2 * F])
    return low, high


def first_kernel(
    acc,
    plane_one,
    plane_two,
    ring_one,
    ring_two,
    inner_lines,
    inner_ends,
    outer,
    head_weight,
    plain,
    y_code,
    x_code,
    head_bias,
    flags,
    affinity,
    kept_y,
    low_out,
    high_out,
    x_outer,
    lines,
    z_code,
    carry,
    planes,
    scr,
    kept,
    own_hot,
    pair_hot,
):
    odd = flags[Z_ODD]
    below = jnp.where(odd > 0, ring_one[RING:, :], ring_two[RING:, :])
    z_code[...] = jnp.where(flags[Z_LOW] > 0, below.astype(F32), -1.0)
    lane = iota((LANES, LANES), 1)
    for plane, ring, i in ((plane_one, ring_one, 1 - odd), (plane_two, ring_two, odd)):
        live = jnp.where(i > 0, flags[Z_HIGH], flags[Z_LOW]) > 0
        around = jnp.where(live, ring[:RING, :], jnp.zeros((RING, LANES), BF))
        face = around[:LANES, :]
        planes[i, :, LANES:] = plane[:, LANES:HEAD]
        planes[i, :, :LANES] = jnp.where(lane < 32, face, plane[:, :LANES])
        carry[i] = plane[:, HEAD - LANES : HEAD]
        carry[2 + i] = face
        for side, dy in ((0, 0), (1, 2)):
            chunks = around[LANES + EDGE * side : LANES + EDGE * (side + 1), :]
            lines[side, i] = jnp.dot(
                line_windows(chunks), outer[i, :, LANES * dy : LANES * (dy + 1)], preferred_element_type=F32
            )
    for i in range(2):
        for side in range(2):
            lines[side, i] = lines[side, i] + inner_lines[side, :, LANES * i : LANES * (i + 1)]
    head = head_rows(head_weight)

    def affinities(s):
        base, x0 = STACK * s, 4 * STACK * s
        add = [None] * STACK
        if s == 0:
            add[0] = inner_ends[0]
        stack_affinity(
            slice(base, base + STACK), base, lambda g: acc[base + g], add, planes, outer, lines, head, head_bias, scr, kept, x0
        )
        all_lines = slice(x0, x0 + 4 * STACK)
        for i in range(6):
            affinity[i // 2, i % 2, all_lines, :] = kept[i, all_lines, :].astype(BF)

    def table(s):
        x0 = 4 * STACK * s
        return stack_table(x0, x0, 0.0 if s else -128.0, plain, y_code, z_code, kept, own_hot, pair_hot)

    affinities(0)
    low, high = jnp.zeros((F, 3 * F), F32), jnp.zeros((F, 2 * F), F32)
    for s in range(HEAD_STACKS):
        if s + 1 < HEAD_STACKS:
            affinities(s + 1)
        more = table(s)
        low, high = low + more[0], high + more[1]
    low_out[...] = low
    high_out[...] = high
    kept_y[...] = kept[4:6]
    x_outer[...] = faces_product(
        [plain[z, 0:1, :] for z in range(2)],
        [x_code[z] for z in range(2)],
        [kept[2 + z, 0:1, :] for z in range(2)],
    )


def second_kernel(
    acc,
    plane_one,
    plane_two,
    inner_ends,
    outer,
    head_weight,
    plain,
    y_code,
    y_low,
    first_col,
    counts,
    affinity_head,
    kept_y,
    low_head,
    high_head,
    x_outer,
    lines,
    z_code,
    carry,
    cells,
    owner,
    rank_hot,
    column_hot,
    head_bias,
    flags,
    affinity,
    outgoing,
    planes,
    scr,
    kept,
    own_hot,
    pair_hot,
):
    odd = flags[Z_ODD]
    lane = iota((LANES, LANES), 1)
    wide = WIDE - HEAD
    for i in range(2):
        planes[i, :, :LANES] = carry[i]
    for plane, i in ((plane_one, 1 - odd), (plane_two, odd)):
        planes[i, :, LANES:wide] = plane[:, : wide - LANES]
        planes[i, :, wide:] = jnp.where((lane >= 32) & (lane < 64), carry[2 + i], plane[:, wide - LANES :])
    add = [None] * STACK
    add[-1] = inner_ends[1]
    groups = pl.ds(HEAD_GROUPS, STACK)
    stack_affinity(
        groups, 0, lambda g: acc[HEAD_GROUPS + g], add, planes, outer, lines, head_rows(head_weight), head_bias, scr, kept, 0
    )
    for i in range(6):
        affinity[i // 2, i % 2, :HEAD_LINES, :] = affinity_head[i // 2, i % 2]
        affinity[i // 2, i % 2, HEAD_LINES:, :] = kept[i].astype(BF)
    low, high = stack_table(HEAD_LINES, 0, 0.0, plain, y_code, z_code, kept, own_hot, pair_hot)
    low, high = low_head[...] + low, high_head[...] + high
    own = low[:, :F] + high[:, :F] + high[:, F:]
    y_outer = faces_product(
        [first_col[z : z + 1, :] for z in range(2)],
        [y_partner(y_low, z, flags[Y_LOW] > 0) for z in range(2)],
        [jnp.concatenate([kept_y[z], kept[4 + z]], axis=0).T[0:1, :] for z in range(2)],
    )
    sums = jnp.concatenate([own, low[:, F : 2 * F], x_outer[...], y_outer], axis=1)
    tally = counts[...] + jnp.concatenate(
        [jnp.zeros((F, F), F32), low[:, 2 * F :], jnp.zeros((F, 2 * F), F32)], axis=1
    )
    slots = cells.shape[1]
    picked = jnp.dot(
        jnp.concatenate(halves(sums) + halves(tally), axis=0), column_hot[...], preferred_element_type=F32
    )
    code = jnp.concatenate([cells[0:1, :], cells[1:2, :]], axis=1)
    line_hot = iota((F, 2 * slots), 0) == (code >> 8)
    alive = iota((1, slots), 1) < flags[LIVE]

    def part_of(value):
        total = jnp.sum(jnp.where(line_hot, value, 0.0), axis=0, keepdims=True)
        return jnp.where(alive, total[:, :slots] + total[:, slots:], 0.0)

    part_sum = part_of(picked[:F] + picked[F : 2 * F])
    part_count = part_of(picked[2 * F : 3 * F] + picked[3 * F :])
    to_owner = iota((outgoing.shape[0], slots), 0) == owner[...]
    left = [
        jnp.where(to_owner, piece.astype(F32), 0.0).astype(BF) for piece in halves(part_sum) + halves(part_count)
    ]
    sent = outer_product(
        jnp.concatenate(left, axis=1),
        jnp.concatenate([rank_hot[0], rank_hot[0], rank_hot[1], rank_hot[1]], axis=1),
    )
    outgoing[...] = sent.reshape(outgoing.shape)


def settle_kernel(received, group_of, name_hot, out, left):
    devices = received.shape[0]
    groups = out.shape[1] // LANES
    row, lane = iota((16, LANES), 0), iota((16, LANES), 1)
    of_count = row >= 2 * groups
    inner = jnp.where(of_count, row - 2 * groups, row)
    is_low = inner >= groups
    group = jnp.where(is_low, inner - groups, inner)
    group = jnp.where((lane >= F) == of_count, group, -1)
    group = jnp.where(row < 4 * groups, group, -1)

    def body(p, _):
        spot = pl.ds(pl.multiple_of(p * LANES, LANES), LANES)
        value = received[p]
        high = value.astype(BF).astype(F32)
        piece = jnp.where(is_low, value - high, high)
        left[:, spot] = jnp.where(group_of[pl.ds(p, 1), :] == group, piece, 0.0).astype(BF)
        return 0

    lax.fori_loop(0, devices, body, 0, unroll=8)
    total = outer_product(left[...], name_hot[...])
    for g in range(groups):
        total_sum = total[g : g + 1] + total[groups + g : groups + g + 1]
        total_count = total[2 * groups + g : 2 * groups + g + 1] + total[3 * groups + g : 3 * groups + g + 1]
        out[:, LANES * g : LANES * (g + 1)] = total_sum / jnp.maximum(total_count, 1.0)


def swap(one, two, axis, closed):
    n = lax.axis_size(axis)
    if n == 1:
        return jnp.zeros_like(one), jnp.zeros_like(two)
    rounds = [[(i, i + 1) for i in range(start, n - 1, 2)] for start in range(2)]
    if n == 2:
        got = lax.ppermute(one, axis, [(0, 1), (1, 0)])
        return got, got
    if closed and n % 2 == 0:
        rounds[1].append((0, n - 1))
    return tuple(
        lax.ppermute(value, axis, [pair for a, b in pairs for pair in ((a, b), (b, a))])
        for value, pairs in zip((one, two), rounds)
    )


def shards(
    features,
    conv_weight,
    conv_bias,
    head_weight,
    head_bias,
    fragments,
    edge_cells,
    edge_owner,
    edge_count,
    recv_slot,
):
    axes = ("gx", "gy", "gz")
    size = {axis: lax.axis_size(axis) for axis in axes}
    at = {axis: lax.axis_index(axis) for axis in axes}
    devices = size["gx"] * size["gy"] * size["gz"]
    capacity = recv_slot.shape[1] // devices
    slots = edge_cells.shape[1]
    own_slots = devices * capacity // 4
    flags = []
    for axis in axes:
        flags += [at[axis], size[axis] - 1 - at[axis], at[axis] % 2]
    flags = jnp.stack(flags + [edge_count[0]]).astype(jnp.int32)

    xt_low, xt_high, z_one, z_two, end_one, end_two = pl.pallas_call(
        layout_kernel,
        out_shape=(shape((LANES, WIDE), BF),) * 2
        + (shape((LANES, HEAD), BF),) * 2
        + (shape((LANES, WIDE - HEAD), BF),) * 2,
        in_specs=[SMEM, pl.BlockSpec(memory_space=pltpu.HBM)],
        out_specs=(VMEM,) * 6,
        scratch_shapes=[pltpu.VMEM(features.shape, BF), pltpu.SemaphoreType.DMA((8,))],
        compiler_params=pltpu.CompilerParams(vmem_limit_bytes=28 << 20),
        cost_estimate=pl.CostEstimate(flops=1_000_000, bytes_accessed=1 << 17, transcendentals=0),
        name="layout",
    )(flags, pltpu.with_memory_space_constraint(features, pltpu.HBM))
    plane_one, plane_two = swap(z_one, z_two, "gz", False)
    acc, inner, outer = call(
        own_kernel,
        "own_planes",
        (shape((GROUPS, LANES, 256), F32), shape((3, 512, 256), BF), shape((2, 256, 3 * LANES), BF)),
        (xt_low, xt_high, conv_weight, conv_bias.reshape(1, -1)),
        0,
        [pltpu.VMEM((27, 32, LANES), BF), pltpu.VMEM((STEP * STACK + 8, 768), F32)],
        flops=300_000_000,
    )
    x_one, x_two, edge, first_col = call(
        face_kernel,
        "faces",
        (
            shape((2 * LANES + 16, LANES), BF),
            shape((2 * LANES + 16, LANES), BF),
            shape((4, EDGE, LANES), BF),
            shape((2, LANES), F32),
        ),
        (xt_low, xt_high, fragments, flags),
        1,
        [pltpu.VMEM((4, EDGE, LANES), F32)],
    )
    x_got = swap(x_one, x_two, "gx", True)

    owner = edge_owner.reshape(1, slots)
    rank_hot, column_hot, group, name_hot, own_counts, plain, y_code = call(
        ahead_kernel,
        "ahead",
        (
            shape((2, LANES, slots), BF),
            shape((4 * F, 2 * slots), BF),
            shape((devices, LANES), jnp.int32),
            shape((LANES, devices * LANES), BF),
            shape((F, F), F32),
            shape((2, LANES, LANES), F32),
            shape((2, LANES, LANES), F32),
        ),
        (edge_cells, owner, recv_slot, fragments),
        0,
        [pltpu.VMEM((devices, LANES), jnp.int32), pltpu.VMEM((2, F, 4096), F8), pltpu.VMEM((2, F, 4096), F8)],
        flops=75_000_000,
    )
    *x_got, group = lax.optimization_barrier((*x_got, group))
    face, x_code, y_one, y_two = call(
        x_face_kernel,
        "x_face",
        (
            shape((2, LANES, LANES), BF),
            shape((2, 1, LANES), F32),
            shape((2, EDGE, LANES), BF),
            shape((2, EDGE, LANES), BF),
        ),
        (*x_got, edge, flags),
        1,
    )
    *y_got, outer = lax.optimization_barrier((*swap(y_one, y_two, "gy", True), outer))
    y_low, y_high, ring_one, ring_two = call(
        ring_kernel,
        "ring",
        (shape((2, EDGE, LANES), BF),) * 2 + (shape((RING + LANES, LANES), BF),) * 2,
        (face, *y_got, fragments, flags),
        1,
    )
    ring_one, ring_two = swap(ring_one, ring_two, "gz", False)

    lines, ends, counts = call(
        edge_kernel,
        "edges",
        (shape((2, GROUPS, 256), F32), shape((2, LANES, 256), F32), shape((F, 4 * F), F32)),
        (face, y_low, y_high, inner, plain, x_code, first_col, own_counts, flags),
        1,
        flops=50_000_000,
    )

    end_one, end_two, counts = lax.optimization_barrier((end_one, end_two, counts))
    end_one, end_two = swap(end_one, end_two, "gz", False)

    def stack_scratch(tiles, kept_lines):
        return [
            pltpu.VMEM((2, LANES, tiles * LANES), BF),
            pltpu.VMEM((2, STEP * STACK + 8, 3 * LANES), F32),
            pltpu.VMEM((6, kept_lines, LANES), F32),
            pltpu.VMEM((2, 2, F, 2048), BF),
            pltpu.VMEM((2, 2, 3 * F, 2048), BF),
        ]

    done = call(
        first_kernel,
        "first_lines",
        (
            shape((3, 2, HEAD_LINES, LANES), BF),
            shape((2, HEAD_LINES, LANES), F32),
            shape((F, 3 * F), F32),
            shape((F, 2 * F), F32),
            shape((F, F), F32),
            shape((2, 2, GROUPS, LANES), F32),
            shape((LANES, LANES), F32),
            shape((4, LANES, LANES), BF),
        ),
        (
            acc,
            plane_one,
            plane_two,
            ring_one,
            ring_two,
            lines,
            ends,
            outer,
            head_weight,
            plain,
            y_code,
            x_code,
            head_bias,
            flags,
        ),
        2,
        stack_scratch(HEAD_GROUPS + 1, HEAD_LINES),
        flops=6_000_000_000,
    )
    affinity, outgoing = call(
        second_kernel,
        "last_lines",
        (shape((3, 2, LANES, LANES), BF), shape((devices, 1, LANES), F32)),
        (
            acc,
            end_one,
            end_two,
            ends,
            outer,
            head_weight,
            plain,
            y_code,
            y_low,
            first_col,
            counts,
            *done,
            edge_cells,
            owner,
            rank_hot,
            column_hot,
            head_bias,
            flags,
        ),
        2,
        stack_scratch(TILES - HEAD_GROUPS, LANES - HEAD_LINES),
        flops=3_000_000_000,
    )
    received = lax.all_to_all(outgoing, axes, split_axis=0, concat_axis=0, tiled=True)
    edge_mean = call(
        settle_kernel,
        "settle",
        shape((1, own_slots), F32),
        (received, group, name_hot),
        0,
        [pltpu.VMEM((16, devices * LANES), BF)],
    )
    return affinity, edge_mean


def solution(mesh):
    in_specs = (
        P(None, "gz", "gx", "gy"),
        P(),
        P(),
        P(),
        P(),
        P("gz", "gx", "gy"),
        P(None, ("gx", "gy", "gz")),
        P(("gx", "gy", "gz"), None),
        P(("gx", "gy", "gz")),
        P(("gx", "gy", "gz"), None),
    )
    out_specs = (P(None, "gz", "gx", "gy"), P(("gx", "gy", "gz"), None))
    return jax.shard_map(shards, mesh=mesh, in_specs=in_specs, out_specs=out_specs, check_vma=False)
```

```python
import jax
import jax.numpy as jnp
from jax import lax
from jax.experimental import pallas as pl
from jax.experimental.pallas import tpu as pltpu
from jax.sharding import PartitionSpec as P

F = 64
LANES = 128
GROUPS = 32
TILES = GROUPS + 1
WIDE = TILES * LANES
STACK = 8
STEP = LANES + 8
EDGE = 48
RING = LANES + 2 * EDGE
PART = 8
HEAD_STACKS = 3
HEAD_GROUPS = HEAD_STACKS * STACK
HEAD = (HEAD_GROUPS + 1) * LANES
HEAD_LINES = 4 * HEAD_GROUPS
BF = jnp.bfloat16
F32 = jnp.float32
F8 = jnp.float8_e4m3fn
VMEM = pl.BlockSpec(memory_space=pltpu.VMEM)
SMEM = pl.BlockSpec(memory_space=pltpu.SMEM)


def call(kernel, name, out_shape, args, smem, scratch=(), flops=1_000_000):
    return pl.pallas_call(
        kernel,
        out_shape=out_shape,
        in_specs=[VMEM] * (len(args) - smem) + [SMEM] * smem,
        out_specs=jax.tree.map(lambda _: VMEM, out_shape),
        scratch_shapes=list(scratch),
        compiler_params=pltpu.CompilerParams(vmem_limit_bytes=28 << 20),
        cost_estimate=pl.CostEstimate(flops=flops, bytes_accessed=1 << 17, transcendentals=0),
        name=name,
    )(*args)


def shape(dims, dtype):
    return jax.ShapeDtypeStruct(dims, dtype)


def iota(dims, axis):
    return lax.broadcasted_iota(jnp.int32, dims, axis)


X_LOW, X_HIGH, X_ODD, Y_LOW, Y_HIGH, Y_ODD, Z_LOW, Z_HIGH, Z_ODD, LIVE = range(10)


def outer_product(left, right):
    return lax.dot_general(left, right, (((1,), (1,)), ((), ())), preferred_element_type=F32)


def halves(value):
    high = value.astype(BF)
    return high, (value - high.astype(F32)).astype(BF)


def layout_kernel(flags, feat_hbm, low, high, z_one, z_two, end_one, end_two, feat, sems):
    copies = []
    for t in range(8):
        lines = slice(16 * t, 16 * t + 16)
        copies.append(pltpu.make_async_copy(feat_hbm.at[:, :, lines, :], feat.at[:, :, lines, :], sems.at[t]))
        copies[-1].start()
    odd = flags[Z_ODD] > 0
    zero = jnp.zeros((32, LANES), BF)
    last = [zero, zero]
    for t in range(9):
        if t < 8:
            copies[t].wait()
        both = []
        for z, plane in ((0, low), (1, high)):
            if t < 8:
                block = jnp.swapaxes(feat[:, z, 16 * t : 16 * t + 16, :], 0, 1).reshape(512, LANES)
                turned = jnp.concatenate([last[z], block[:480]], axis=0).T
                last[z] = block[480:]
            else:
                turned = jnp.concatenate([last[z], zero, zero, zero], axis=0).T
            wide = turned.shape[1]
            plane[:, 512 * t : 512 * t + wide] = turned
            both.append(turned)
        for head, end, value in (
            (z_one, end_one, jnp.where(odd, both[0], both[1])),
            (z_two, end_two, jnp.where(odd, both[1], both[0])),
        ):
            cut = min(max(HEAD - 512 * t, 0), wide)
            if cut > 0:
                head[:, 512 * t : 512 * t + cut] = value[:, :cut]
            if cut < wide:
                end[:, 512 * t + cut - HEAD : 512 * t + wide - HEAD] = value[:, cut:]


def face_kernel(low, high, frag, flags, x_one, x_two):
    odd = flags[X_ODD] > 0
    for z, plane in ((0, low), (1, high)):
        lines = slice(LANES * z, LANES * (z + 1))
        start, end = plane[:, :LANES], plane[:, WIDE - LANES :]
        x_one[lines, :] = jnp.where(odd, start, end)
        x_two[lines, :] = jnp.where(odd, end, start)
    lines = [jnp.broadcast_to(frag[z, 127:128, :], (8, LANES)).astype(F32) for z in range(2)]
    lines = jnp.concatenate(lines, axis=0).astype(BF)
    for out in (x_one, x_two):
        out[2 * LANES :, :] = lines


def line_kernel(low, high, frag, edge, first_col, rows):
    for z, plane in ((0, low), (1, high)):
        turned = frag[z].astype(F32).T
        first_col[z : z + 1, :] = turned[0:1]
        for side, line in ((0, plane[112:128, :].astype(F32)[15:16]), (1, plane[0:16, :].astype(F32)[0:1])):
            for q in range(TILES):
                rows[2 * side + z, q : q + 1, :] = line[:, LANES * q : LANES * (q + 1)]
            rows[2 * side + z, TILES:EDGE, :] = jnp.broadcast_to(turned[127:128], (EDGE - TILES, LANES))
            edge[2 * side + z] = rows[2 * side + z].astype(BF)


def x_face_kernel(got_one, got_two, edge, flags, face, x_code, y_one, y_two):
    has_low, has_high, odd = flags[X_LOW] > 0, flags[X_HIGH] > 0, flags[X_ODD] > 0
    y_odd = flags[Y_ODD] > 0
    lane = iota((LANES, LANES), 1)
    is_low = (lane < 32) & has_low
    is_high = (lane >= 32) & (lane < 64) & has_high
    none = jnp.zeros((LANES, LANES), BF)
    row, place = iota((EDGE, LANES), 0), iota((EDGE, LANES), 1)
    ends = ((row == 0) & (place < 32)) | ((row == TILES - 1) & (place >= 32) & (place < 64))
    other = jnp.where(odd, got_one[2 * LANES :, :], got_two[2 * LANES :, :]).astype(F32)
    for z in range(2):
        lines = slice(LANES * z, LANES * (z + 1))
        low = jnp.where(odd, got_one[lines, :], got_two[lines, :])
        high = jnp.where(odd, got_two[lines, :], got_one[lines, :])
        tile = jnp.where(is_low, low, jnp.where(is_high, high, none))
        face[z] = tile
        patched = []
        for side in range(2):
            near = (tile[112:128].astype(F32)[15:16], tile[0:16].astype(F32)[0:1])[side]
            line = edge[2 * side + z].astype(F32)
            patched.append(jnp.where(ends, jnp.broadcast_to(near, (EDGE, LANES)), line).astype(BF))
        y_one[z] = jnp.where(y_odd, patched[1], patched[0])
        y_two[z] = jnp.where(y_odd, patched[0], patched[1])
        x_code[z] = jnp.where(has_low, other[8 * z : 8 * z + 1], -1.0)


def ring_kernel(face, got_one, got_two, frag, flags, y_low, y_high, z_one, z_two):
    odd, z_odd = flags[Y_ODD] > 0, flags[Z_ODD] > 0
    none = jnp.zeros((EDGE, LANES), BF)
    rings = []
    for z in range(2):
        low = jnp.where(flags[Y_LOW] > 0, jnp.where(odd, got_one[z], got_two[z]), none)
        high = jnp.where(flags[Y_HIGH] > 0, jnp.where(odd, got_two[z], got_one[z]), none)
        y_low[z] = low
        y_high[z] = high
        rings.append(jnp.concatenate([face[z], low, high], axis=0))
    z_one[:RING, :] = jnp.where(z_odd, rings[0], rings[1])
    z_two[:RING, :] = jnp.where(z_odd, rings[1], rings[0])
    top = frag[1].astype(F32).astype(BF)
    for out in (z_one, z_two):
        out[RING:, :] = top


def banded(weight, z_off, dy, slot, quarter):
    tile = jnp.zeros((32, LANES), BF)
    if abs(z_off) <= 1:
        for q in range(4):
            dx = slot - 1 - q
            if abs(dx) <= 1:
                tile = jnp.where(quarter == q, weight[9 * (z_off + 1) + 3 * (dx + 1) + dy], tile)
    return tile


def own_kernel(low, high, conv_weight, conv_bias, acc, inner, outer, weight, scr):
    quarter = iota((32, LANES), 1) // 32
    for k in range(27):
        one = conv_weight[k].astype(F32).T.astype(BF)
        weight[k] = jnp.concatenate([one] * 4, axis=1)
    for dy in range(3):
        for slot in range(8):
            for z in range(2):
                line = slice(256 * z + 32 * slot, 256 * z + 32 * slot + 32)
                for zo in range(2):
                    inner[dy, line, LANES * zo : LANES * (zo + 1)] = banded(weight, z - zo, dy, slot, quarter)
                outer[z, 32 * slot : 32 * slot + 32, LANES * dy : LANES * (dy + 1)] = banded(
                    weight, 2 * z - 1, dy, slot, quarter
                )
    bias = jnp.concatenate([conv_bias[...]] * 8, axis=1)
    for g in range(STACK):
        scr[STEP * g + 7 : STEP * g + 8, :] = jnp.zeros((1, 768), F32)
        scr[STEP * g + STEP : STEP * g + STEP + 1, :] = jnp.zeros((1, 768), F32)

    def body(s, _):
        base = s * STACK
        left = jnp.concatenate(
            [
                jnp.concatenate(
                    [plane[:, pl.ds(pl.multiple_of((base + g) * LANES, LANES), 2 * LANES)] for g in range(STACK)],
                    axis=0,
                )
                for plane in (low, high)
            ],
            axis=1,
        )
        for dy in range(3):
            part = jnp.dot(left, inner[dy], preferred_element_type=F32)
            for g in range(STACK):
                scr[STEP * g + 8 : STEP * g + STEP, 256 * dy : 256 * dy + 256] = part[LANES * g : LANES * (g + 1)]
        for g in range(STACK):
            o = STEP * g
            acc[base + g] = (
                scr[o + 7 : o + 135, 0:256] + scr[o + 8 : o + 136, 256:512] + scr[o + 9 : o + 137, 512:768] + bias
            )
        return 0

    lax.fori_loop(0, GROUPS // STACK, body, 0)


def line_windows(chunks):
    wide = chunks.astype(F32)
    return jnp.concatenate([wide[:GROUPS], wide[1:TILES]], axis=1).astype(BF)


def edge_kernel(
    face, y_low, y_high, inner, plain, x_code, first_col, own_counts, flags, lines, ends, counts
):
    for side, (dy, source) in enumerate(((0, y_low), (2, y_high))):
        left = jnp.concatenate([line_windows(source[z]) for z in range(2)], axis=1)
        lines[side] = jnp.dot(left, inner[dy], preferred_element_type=F32)
    row = iota((LANES, 256), 0)
    lane = iota((LANES, LANES), 1)
    none = jnp.zeros((LANES, LANES), BF)
    for end in range(2):
        keep = lane < 32 if end == 0 else lane >= 32
        tiles = [jnp.where(keep, face[z], none) for z in range(2)]
        parts = []
        for dy in range(3):
            right = [inner[dy, 256 * z + LANES * end : 256 * z + LANES * end + LANES, :] for z in range(2)]
            parts.append(
                jnp.dot(
                    jnp.concatenate(tiles, axis=1), jnp.concatenate(right, axis=0), preferred_element_type=F32
                )
            )
        ends[end] = (
            jnp.where(row == 0, 0.0, pltpu.roll(parts[0], 1, 0))
            + parts[1]
            + jnp.where(row == LANES - 1, 0.0, pltpu.roll(parts[2], LANES - 1, 0))
        )
    ones = [jnp.ones((1, LANES), F32)] * 2
    x_outer = faces_product([plain[z, 0:1, :] for z in range(2)], [x_code[z] for z in range(2)], ones)
    y_outer = faces_product(
        [first_col[z : z + 1, :] for z in range(2)], [y_partner(y_low, z, flags[Y_LOW] > 0) for z in range(2)], ones
    )
    counts[...] = jnp.concatenate([own_counts[...], jnp.zeros((F, F), F32), x_outer, y_outer], axis=1)


def spread(row, copies):
    one = jnp.broadcast_to(row, (16, LANES)).astype(BF)
    return jnp.concatenate([one] * copies, axis=0)


def numbers(rows):
    return iota((rows, LANES), 0).astype(F32).astype(BF)


def line_partners(frag, y_code, x, first, hot_before):
    names = numbers(F)
    line = pl.ds(x, 1)
    hot = [spread(frag[z, line, :], 4) == names for z in range(2)]
    if hot_before is None:
        before = [frag[z, pl.ds(jnp.maximum(x - 1, 0), 1), :] + first for z in range(2)]
        hot_before = [spread(row, 4) == names for row in before]
    y_hot = [spread(y_code[z, line, :], 4) == names for z in range(2)]
    return hot, hot_before, y_hot


def faces_product(own, partner, weight):
    names = numbers(F)
    one, none = jnp.ones((F, LANES), BF), jnp.zeros((F, LANES), BF)
    left = [jnp.where(spread(row, 4) == names, one, none) for row in own]
    right = [jnp.where(spread(row, 4) == names, spread(value, 4), none) for row, value in zip(partner, weight)]
    return outer_product(jnp.concatenate(left, axis=1), jnp.concatenate(right, axis=1))


def load_numbers(frag, plain, y_code):
    lane = iota((LANES, LANES), 1)
    for z in range(2):
        value = frag[z].astype(F32)
        plain[z] = value
        y_code[z] = jnp.where(lane == 0, -1.0, pltpu.roll(value, 1, 1))


def y_partner(y_low, z, has_low):
    return jnp.where(has_low, y_low[z, TILES - 1 :, :].astype(F32)[8:9], -1.0)


def count_kernel(frag, out, plain, y_code, own_hot, pair_hot):
    load_numbers(frag, plain, y_code)
    one = jnp.ones((F, LANES), BF)
    none = jnp.zeros((F, LANES), BF)

    def body(t, total):
        hot_before = None
        first = jnp.where(t > 0, 0.0, -128.0)
        for j in range(32):
            spot = slice(LANES * j, LANES * (j + 1))
            hot, x_hot, y_hot = line_partners(plain, y_code, 32 * t + j, first, hot_before)
            hot_before = hot
            for z in range(2):
                own_hot[z, :, spot] = jnp.where(hot[z], one, none).astype(F8)
                pairs = jnp.where(x_hot[z], one, none) + jnp.where(y_hot[z], one, none)
                if z == 1:
                    pairs = pairs + jnp.where(hot[0], one, none)
                pair_hot[z, :, spot] = pairs.astype(F8)
        for z in range(2):
            total = total + outer_product(own_hot[z], pair_hot[z])
        return total

    out[...] = lax.fori_loop(0, 4, body, jnp.zeros((F, F), F32))


def slots_kernel(cells, owner, recv, rank_hot, column_hot, group, name_hot, place):
    slots = owner.shape[1]
    devices = group.shape[0]
    capacity = recv.shape[1] // devices
    hot = iota((devices, slots), 0) == owner[...]
    before = iota((slots, slots), 0) < iota((slots, slots), 1)
    earlier = jnp.dot(
        jnp.where(hot, 1.0, 0.0).astype(BF), jnp.where(before, 1.0, 0.0).astype(BF), preferred_element_type=F32
    )
    rank = jnp.sum(jnp.where(hot, earlier, 0.0), axis=0, keepdims=True).astype(jnp.int32)
    lanes = iota((LANES, slots), 0)
    rank_hot[0] = jnp.where(lanes == rank, 1.0, 0.0).astype(BF)
    rank_hot[1] = jnp.where(lanes == rank + F, 1.0, 0.0).astype(BF)
    code = jnp.concatenate([cells[0:1, :], cells[1:2, :]], axis=1)
    column_hot[...] = jnp.where(iota((4 * F, 2 * slots), 0) == (code & (4 * F - 1)), 1.0, 0.0).astype(BF)
    place[...] = jnp.full(place.shape, -4 * LANES, jnp.int32)
    for p in range(devices):
        piece = recv[:, capacity * p : capacity * (p + 1)]
        place[p : p + 1, 0:capacity] = piece
        place[p : p + 1, F : F + capacity] = piece
    group[...] = place[...] >> 7
    names = iota((LANES, LANES), 0)

    def body(p, _):
        spot = pl.ds(pl.multiple_of(p * LANES, LANES), LANES)
        name_hot[:, spot] = jnp.where((place[pl.ds(p, 1), :] & (LANES - 1)) == names, 1.0, 0.0).astype(BF)
        return 0

    lax.fori_loop(0, devices, body, 0, unroll=8)


def ahead_kernel(
    cells,
    owner,
    recv,
    frag,
    low,
    high,
    rank_hot,
    column_hot,
    group,
    name_hot,
    counts,
    plain,
    y_code,
    edge,
    first_col,
    place,
    own_hot,
    pair_hot,
    rows,
):
    line_kernel(low, high, frag, edge, first_col, rows)
    count_kernel(frag, counts, plain, y_code, own_hot, pair_hot)
    slots_kernel(cells, owner, recv, rank_hot, column_hot, group, name_hot, place)


def head_rows(head_weight):
    line, spot = iota((8, 256), 0), iota((8, 256), 1)
    head = []
    for d in range(3):
        weights = jnp.concatenate([head_weight[d : d + 1, :].astype(F32)] * 8, axis=1)
        for z in range(2):
            match = (spot // LANES == z) & ((spot // 32) % 4 == line % 4)
            head.append(jnp.where(match, jnp.broadcast_to(weights, (8, 256)), 0.0))
    return jnp.concatenate(head, axis=0).astype(BF)


def stack_affinity(groups, tile, acc, add, planes, outer, lines, head, head_bias, scr, kept, kept_at):
    for i in range(2):
        left = jnp.concatenate(
            [
                planes[i, :, (tile + g) * LANES : (tile + g + 2) * LANES]
                for g in range(STACK)
            ],
            axis=0,
        )
        part = jnp.dot(left, outer[i], preferred_element_type=F32)
        ends = [lines[side, i, groups, :] for side in range(2)]
        for g in range(STACK):
            o = STEP * g
            scr[i, o + 8 : o + STEP, :] = part[LANES * g : LANES * (g + 1)]
            scr[i, o + 7 : o + 8, 0:LANES] = ends[0][g : g + 1]
            scr[i, o + STEP : o + STEP + 1, 2 * LANES :] = ends[1][g : g + 1]
    hidden = []
    for g in range(STACK):
        o = STEP * g
        outside = [
            scr[i, o + 7 : o + 135, 0:LANES]
            + scr[i, o + 8 : o + 136, LANES : 2 * LANES]
            + scr[i, o + 9 : o + 137, 2 * LANES :]
            for i in range(2)
        ]
        total = acc(g) + jnp.concatenate(outside, axis=1)
        if add[g] is not None:
            total = total + add[g]
        hidden.append(jnp.maximum(total, 0.0).astype(BF))
    logits = outer_product(head, jnp.concatenate(hidden, axis=0))
    top_half = iota((8, LANES), 0) < 4
    for i in range(6):
        for pair in range(STACK // 2):
            at = 2 * LANES * pair
            both = logits[8 * i : 8 * i + 8]
            value = jnp.where(top_half, both[:, at : at + LANES], both[:, at + LANES : at + 2 * LANES])
            value = jax.nn.sigmoid(value + head_bias[i // 2]).astype(BF).astype(F32)
            kept[i, kept_at + 8 * pair : kept_at + 8 * pair + 8, :] = value


def table_pieces(x0, kept_at, plain, y_code, z_code, kept, lines):
    names, one, none = numbers(F), jnp.ones((F, LANES), BF), jnp.zeros((F, LANES), BF)
    low, high = jnp.zeros((3 * F, F), F32), jnp.zeros((2 * F, F), F32)
    def one_hot(row):
        return jnp.where(spread(row, 4) == names, one, none)

    before = None
    for t in range(lines // PART):
        own_rows, pair_rows = [[], []], [[], []]
        for j in range(PART):
            at = PART * t + j
            x = x0 + at
            line = slice(x, x + 1)
            weight = [spread(kept[i, kept_at + at : kept_at + at + 1, :], 4) for i in range(6)]
            hot = [one_hot(plain[z, line, :]) for z in range(2)]
            if before is None:
                before = [one_hot(plain[z, x - 1 : x, :]) if x > 0 else none for z in range(2)]
            z_hot = one_hot(z_code[line, :])
            for z in range(2):
                own_rows[z].append(hot[z])
                pair = [before[z] * weight[2 + z] + one_hot(y_code[z, line, :]) * weight[4 + z]]
                pair += [hot[0] * weight[1]] if z else [z_hot * weight[0], z_hot]
                pair_rows[z].append(jnp.concatenate(pair, axis=0))
            before = hot
        parts = [
            outer_product(jnp.concatenate(pair_rows[z], axis=1), jnp.concatenate(own_rows[z], axis=1))
            for z in range(2)
        ]
        low, high = low + parts[0], high + parts[1]
    return low.T, high.T


def first_kernel(
    acc,
    plane_one,
    plane_two,
    ring_one,
    ring_two,
    inner_lines,
    inner_ends,
    outer,
    head_weight,
    plain,
    y_code,
    x_code,
    head_bias,
    flags,
    affinity,
    kept_y,
    low_out,
    high_out,
    x_outer,
    lines,
    z_code,
    carry,
    planes,
    scr,
    kept,
):
    odd = flags[Z_ODD]
    below = jnp.where(odd > 0, ring_one[RING:, :], ring_two[RING:, :])
    z_code[...] = jnp.where(flags[Z_LOW] > 0, below.astype(F32), -1.0)
    lane = iota((LANES, LANES), 1)
    for plane, ring, i in ((plane_one, ring_one, 1 - odd), (plane_two, ring_two, odd)):
        live = jnp.where(i > 0, flags[Z_HIGH], flags[Z_LOW]) > 0
        around = jnp.where(live, ring[:RING, :], jnp.zeros((RING, LANES), BF))
        face = around[:LANES, :]
        planes[i, :, LANES:] = plane[:, LANES:HEAD]
        planes[i, :, :LANES] = jnp.where(lane < 32, face, plane[:, :LANES])
        carry[i] = plane[:, HEAD - LANES : HEAD]
        carry[2 + i] = face
        for side, dy in ((0, 0), (1, 2)):
            chunks = around[LANES + EDGE * side : LANES + EDGE * (side + 1), :]
            lines[side, i] = jnp.dot(
                line_windows(chunks), outer[i, :, LANES * dy : LANES * (dy + 1)], preferred_element_type=F32
            )
    for i in range(2):
        for side in range(2):
            lines[side, i] = lines[side, i] + inner_lines[side, :, LANES * i : LANES * (i + 1)]
    head = head_rows(head_weight)

    def affinities(s):
        base, x0 = STACK * s, 4 * STACK * s
        add = [None] * STACK
        if s == 0:
            add[0] = inner_ends[0]
        stack_affinity(
            slice(base, base + STACK), base, lambda g: acc[base + g], add, planes, outer, lines, head, head_bias, scr.at[s % 2], kept, x0
        )
        all_lines = slice(x0, x0 + 4 * STACK)
        for i in range(6):
            affinity[i // 2, i % 2, all_lines, :] = kept[i, all_lines, :].astype(BF)

    for s in range(HEAD_STACKS):
        affinities(s)
    low, high = table_pieces(0, 0, plain, y_code, z_code, kept, HEAD_LINES)
    low_out[...] = low
    high_out[...] = high
    kept_y[...] = kept[4:6]
    x_outer[...] = faces_product(
        [plain[z, 0:1, :] for z in range(2)],
        [x_code[z] for z in range(2)],
        [kept[2 + z, 0:1, :] for z in range(2)],
    )


def second_kernel(
    acc,
    plane_one,
    plane_two,
    inner_ends,
    outer,
    head_weight,
    plain,
    y_code,
    y_low,
    first_col,
    counts,
    affinity_head,
    kept_y,
    low_head,
    high_head,
    x_outer,
    lines,
    z_code,
    carry,
    cells,
    owner,
    rank_hot,
    column_hot,
    head_bias,
    flags,
    affinity,
    outgoing,
    planes,
    scr,
    kept,
):
    odd = flags[Z_ODD]
    lane = iota((LANES, LANES), 1)
    wide = WIDE - HEAD
    for i in range(2):
        planes[i, :, :LANES] = carry[i]
    for plane, i in ((plane_one, 1 - odd), (plane_two, odd)):
        planes[i, :, LANES:wide] = plane[:, : wide - LANES]
        planes[i, :, wide:] = jnp.where((lane >= 32) & (lane < 64), carry[2 + i], plane[:, wide - LANES :])
    add = [None] * STACK
    add[-1] = inner_ends[1]
    groups = pl.ds(HEAD_GROUPS, STACK)
    stack_affinity(
        groups, 0, lambda g: acc[HEAD_GROUPS + g], add, planes, outer, lines, head_rows(head_weight), head_bias, scr.at[0], kept, 0
    )
    for i in range(6):
        affinity[i // 2, i % 2, :HEAD_LINES, :] = affinity_head[i // 2, i % 2]
        affinity[i // 2, i % 2, HEAD_LINES:, :] = kept[i].astype(BF)
    low, high = table_pieces(
        HEAD_LINES, 0, plain, y_code, z_code, kept, LANES - HEAD_LINES
    )
    low, high = low_head[...] + low, high_head[...] + high
    own = low[:, :F] + high[:, :F] + high[:, F:]
    y_outer = faces_product(
        [first_col[z : z + 1, :] for z in range(2)],
        [y_partner(y_low, z, flags[Y_LOW] > 0) for z in range(2)],
        [jnp.concatenate([kept_y[z], kept[4 + z]], axis=0).T[0:1, :] for z in range(2)],
    )
    sums = jnp.concatenate([own, low[:, F : 2 * F], x_outer[...], y_outer], axis=1)
    tally = counts[...] + jnp.concatenate(
        [jnp.zeros((F, F), F32), low[:, 2 * F :], jnp.zeros((F, 2 * F), F32)], axis=1
    )
    slots = cells.shape[1]
    picked = jnp.dot(
        jnp.concatenate(halves(sums) + halves(tally), axis=0), column_hot[...], preferred_element_type=F32
    )
    code = jnp.concatenate([cells[0:1, :], cells[1:2, :]], axis=1)
    line_hot = iota((F, 2 * slots), 0) == (code >> 8)
    alive = iota((1, slots), 1) < flags[LIVE]

    def part_of(value):
        total = jnp.sum(jnp.where(line_hot, value, 0.0), axis=0, keepdims=True)
        return jnp.where(alive, total[:, :slots] + total[:, slots:], 0.0)

    part_sum = part_of(picked[:F] + picked[F : 2 * F])
    part_count = part_of(picked[2 * F : 3 * F] + picked[3 * F :])
    to_owner = iota((outgoing.shape[0], slots), 0) == owner[...]
    left = [
        jnp.where(to_owner, piece.astype(F32), 0.0).astype(BF) for piece in halves(part_sum) + halves(part_count)
    ]
    sent = outer_product(
        jnp.concatenate(left, axis=1),
        jnp.concatenate([rank_hot[0], rank_hot[0], rank_hot[1], rank_hot[1]], axis=1),
    )
    outgoing[...] = sent.reshape(outgoing.shape)


def settle_kernel(received, group_of, name_hot, out, left):
    devices = received.shape[0]
    groups = out.shape[1] // LANES
    row, lane = iota((16, LANES), 0), iota((16, LANES), 1)
    of_count = row >= 2 * groups
    inner = jnp.where(of_count, row - 2 * groups, row)
    is_low = inner >= groups
    group = jnp.where(is_low, inner - groups, inner)
    group = jnp.where((lane >= F) == of_count, group, -1)
    group = jnp.where(row < 4 * groups, group, -1)

    def body(p, _):
        spot = pl.ds(pl.multiple_of(p * LANES, LANES), LANES)
        value = received[p]
        high = value.astype(BF).astype(F32)
        piece = jnp.where(is_low, value - high, high)
        left[:, spot] = jnp.where(group_of[pl.ds(p, 1), :] == group, piece, 0.0).astype(BF)
        return 0

    lax.fori_loop(0, devices, body, 0, unroll=8)
    total = outer_product(left[...], name_hot[...])
    for g in range(groups):
        total_sum = total[g : g + 1] + total[groups + g : groups + g + 1]
        total_count = total[2 * groups + g : 2 * groups + g + 1] + total[3 * groups + g : 3 * groups + g + 1]
        out[:, LANES * g : LANES * (g + 1)] = total_sum / jnp.maximum(total_count, 1.0)


def swap(one, two, axis, closed):
    n = lax.axis_size(axis)
    if n == 1:
        return jnp.zeros_like(one), jnp.zeros_like(two)
    rounds = [[(i, i + 1) for i in range(start, n - 1, 2)] for start in range(2)]
    if n == 2:
        got = lax.ppermute(one, axis, [(0, 1), (1, 0)])
        return got, got
    if closed and n % 2 == 0:
        rounds[1].append((0, n - 1))
    return tuple(
        lax.ppermute(value, axis, [pair for a, b in pairs for pair in ((a, b), (b, a))])
        for value, pairs in zip((one, two), rounds)
    )


def shards(
    features,
    conv_weight,
    conv_bias,
    head_weight,
    head_bias,
    fragments,
    edge_cells,
    edge_owner,
    edge_count,
    recv_slot,
):
    axes = ("gx", "gy", "gz")
    size = {axis: lax.axis_size(axis) for axis in axes}
    at = {axis: lax.axis_index(axis) for axis in axes}
    devices = size["gx"] * size["gy"] * size["gz"]
    capacity = recv_slot.shape[1] // devices
    slots = edge_cells.shape[1]
    own_slots = devices * capacity // 4
    flags = []
    for axis in axes:
        flags += [at[axis], size[axis] - 1 - at[axis], at[axis] % 2]
    flags = jnp.stack(flags + [edge_count[0]]).astype(jnp.int32)

    xt_low, xt_high, z_one, z_two, end_one, end_two = pl.pallas_call(
        layout_kernel,
        out_shape=(shape((LANES, WIDE), BF),) * 2
        + (shape((LANES, HEAD), BF),) * 2
        + (shape((LANES, WIDE - HEAD), BF),) * 2,
        in_specs=[SMEM, pl.BlockSpec(memory_space=pltpu.HBM)],
        out_specs=(VMEM,) * 6,
        scratch_shapes=[pltpu.VMEM(features.shape, BF), pltpu.SemaphoreType.DMA((8,))],
        compiler_params=pltpu.CompilerParams(vmem_limit_bytes=28 << 20),
        cost_estimate=pl.CostEstimate(flops=1_000_000, bytes_accessed=1 << 17, transcendentals=0),
        name="layout",
    )(flags, pltpu.with_memory_space_constraint(features, pltpu.HBM))
    plane_one, plane_two = swap(z_one, z_two, "gz", False)
    acc, inner, outer = call(
        own_kernel,
        "own_planes",
        (shape((GROUPS, LANES, 256), F32), shape((3, 512, 256), BF), shape((2, 256, 3 * LANES), BF)),
        (xt_low, xt_high, conv_weight, conv_bias.reshape(1, -1)),
        0,
        [pltpu.VMEM((27, 32, LANES), BF), pltpu.VMEM((STEP * STACK + 8, 768), F32)],
        flops=300_000_000,
    )
    x_one, x_two = call(
        face_kernel,
        "faces",
        (
            shape((2 * LANES + 16, LANES), BF),
            shape((2 * LANES + 16, LANES), BF),
        ),
        (xt_low, xt_high, fragments, flags),
        1,
    )
    x_got = swap(x_one, x_two, "gx", True)

    owner = edge_owner.reshape(1, slots)
    rank_hot, column_hot, group, name_hot, own_counts, plain, y_code, edge, first_col = call(
        ahead_kernel,
        "ahead",
        (
            shape((2, LANES, slots), BF),
            shape((4 * F, 2 * slots), BF),
            shape((devices, LANES), jnp.int32),
            shape((LANES, devices * LANES), BF),
            shape((F, F), F32),
            shape((2, LANES, LANES), F32),
            shape((2, LANES, LANES), F32),
            shape((4, EDGE, LANES), BF),
            shape((2, LANES), F32),
        ),
        (edge_cells, owner, recv_slot, fragments, xt_low, xt_high),
        0,
        [
            pltpu.VMEM((devices, LANES), jnp.int32),
            pltpu.VMEM((2, F, 4096), F8),
            pltpu.VMEM((2, F, 4096), F8),
            pltpu.VMEM((4, EDGE, LANES), F32),
        ],
        flops=75_000_000,
    )
    *x_got, group = lax.optimization_barrier((*x_got, group))
    face, x_code, y_one, y_two = call(
        x_face_kernel,
        "x_face",
        (
            shape((2, LANES, LANES), BF),
            shape((2, 1, LANES), F32),
            shape((2, EDGE, LANES), BF),
            shape((2, EDGE, LANES), BF),
        ),
        (*x_got, edge, flags),
        1,
    )
    *y_got, outer = lax.optimization_barrier((*swap(y_one, y_two, "gy", True), outer))
    y_low, y_high, ring_one, ring_two = call(
        ring_kernel,
        "ring",
        (shape((2, EDGE, LANES), BF),) * 2 + (shape((RING + LANES, LANES), BF),) * 2,
        (face, *y_got, fragments, flags),
        1,
    )
    ring_one, ring_two = swap(ring_one, ring_two, "gz", False)

    lines, ends, counts = call(
        edge_kernel,
        "edges",
        (shape((2, GROUPS, 256), F32), shape((2, LANES, 256), F32), shape((F, 4 * F), F32)),
        (face, y_low, y_high, inner, plain, x_code, first_col, own_counts, flags),
        1,
        flops=50_000_000,
    )

    end_one, end_two, counts = lax.optimization_barrier((end_one, end_two, counts))
    end_one, end_two = swap(end_one, end_two, "gz", False)

    def stack_scratch(tiles, kept_lines):
        return [
            pltpu.VMEM((2, LANES, tiles * LANES), BF),
            pltpu.VMEM((min(2, kept_lines // 32), 2, STEP * STACK + 8, 3 * LANES), F32),
            pltpu.VMEM((6, kept_lines, LANES), F32),
        ]

    done = call(
        first_kernel,
        "first_lines",
        (
            shape((3, 2, HEAD_LINES, LANES), BF),
            shape((2, HEAD_LINES, LANES), F32),
            shape((F, 3 * F), F32),
            shape((F, 2 * F), F32),
            shape((F, F), F32),
            shape((2, 2, GROUPS, LANES), F32),
            shape((LANES, LANES), F32),
            shape((4, LANES, LANES), BF),
        ),
        (
            acc,
            plane_one,
            plane_two,
            ring_one,
            ring_two,
            lines,
            ends,
            outer,
            head_weight,
            plain,
            y_code,
            x_code,
            head_bias,
            flags,
        ),
        2,
        stack_scratch(HEAD_GROUPS + 1, HEAD_LINES),
        flops=6_000_000_000,
    )
    affinity, outgoing = call(
        second_kernel,
        "last_lines",
        (shape((3, 2, LANES, LANES), BF), shape((devices, 1, LANES), F32)),
        (
            acc,
            end_one,
            end_two,
            ends,
            outer,
            head_weight,
            plain,
            y_code,
            y_low,
            first_col,
            counts,
            *done,
            edge_cells,
            owner,
            rank_hot,
            column_hot,
            head_bias,
            flags,
        ),
        2,
        stack_scratch(TILES - HEAD_GROUPS, LANES - HEAD_LINES),
        flops=3_000_000_000,
    )
    received = lax.all_to_all(outgoing, axes, split_axis=0, concat_axis=0, tiled=True)
    edge_mean = call(
        settle_kernel,
        "settle",
        shape((1, own_slots), F32),
        (received, group, name_hot),
        0,
        [pltpu.VMEM((16, devices * LANES), BF)],
    )
    return affinity, edge_mean


def solution(mesh):
    in_specs = (
        P(None, "gz", "gx", "gy"),
        P(),
        P(),
        P(),
        P(),
        P("gz", "gx", "gy"),
        P(None, ("gx", "gy", "gz")),
        P(("gx", "gy", "gz"), None),
        P(("gx", "gy", "gz")),
        P(("gx", "gy", "gz"), None),
    )
    out_specs = (P(None, "gz", "gx", "gy"), P(("gx", "gy", "gz"), None))
    return jax.shard_map(shards, mesh=mesh, in_specs=in_specs, out_specs=out_specs, check_vma=False)
```

```python
import jax
import jax.numpy as jnp
from jax import lax
from jax.experimental import pallas as pl
from jax.experimental.pallas import tpu as pltpu
from jax.sharding import PartitionSpec as P

F = 64
LANES = 128
GROUPS = 32
TILES = GROUPS + 1
WIDE = TILES * LANES
STACK = 8
STEP = LANES + 8
EDGE = 48
HALF = LANES // 2
RING = HALF + 2 * EDGE
PART = 8
HEAD_STACKS = 3
HEAD_GROUPS = HEAD_STACKS * STACK
HEAD = (HEAD_GROUPS + 1) * LANES
HEAD_LINES = 4 * HEAD_GROUPS
BF = jnp.bfloat16
F32 = jnp.float32
F8 = jnp.float8_e4m3fn
VMEM = pl.BlockSpec(memory_space=pltpu.VMEM)
SMEM = pl.BlockSpec(memory_space=pltpu.SMEM)


def call(kernel, name, out_shape, args, smem, scratch=(), flops=1_000_000):
    return pl.pallas_call(
        kernel,
        out_shape=out_shape,
        in_specs=[VMEM] * (len(args) - smem) + [SMEM] * smem,
        out_specs=jax.tree.map(lambda _: VMEM, out_shape),
        scratch_shapes=list(scratch),
        compiler_params=pltpu.CompilerParams(vmem_limit_bytes=28 << 20),
        cost_estimate=pl.CostEstimate(flops=flops, bytes_accessed=1 << 17, transcendentals=0),
        name=name,
    )(*args)


def shape(dims, dtype):
    return jax.ShapeDtypeStruct(dims, dtype)


def iota(dims, axis):
    return lax.broadcasted_iota(jnp.int32, dims, axis)


X_LOW, X_HIGH, X_ODD, Y_LOW, Y_HIGH, Y_ODD, Z_LOW, Z_HIGH, Z_ODD, LIVE = range(10)


def outer_product(left, right):
    return lax.dot_general(left, right, (((1,), (1,)), ((), ())), preferred_element_type=F32)


def halves(value):
    high = value.astype(BF)
    return high, (value - high.astype(F32)).astype(BF)


def layout_kernel(flags, feat_hbm, low, high, z_one, z_two, end_one, end_two, feat, sems):
    copies = []
    for t in range(8):
        lines = slice(16 * t, 16 * t + 16)
        copies.append(pltpu.make_async_copy(feat_hbm.at[:, :, lines, :], feat.at[:, :, lines, :], sems.at[t]))
        copies[-1].start()
    odd = flags[Z_ODD] > 0
    zero = jnp.zeros((32, LANES), BF)
    last = [zero, zero]
    for t in range(9):
        if t < 8:
            copies[t].wait()
        both = []
        for z, plane in ((0, low), (1, high)):
            if t < 8:
                block = jnp.swapaxes(feat[:, z, 16 * t : 16 * t + 16, :], 0, 1).reshape(512, LANES)
                turned = jnp.concatenate([last[z], block[:480]], axis=0).T
                last[z] = block[480:]
            else:
                turned = jnp.concatenate([last[z], zero, zero, zero], axis=0).T
            wide = turned.shape[1]
            plane[:, 512 * t : 512 * t + wide] = turned
            both.append(turned)
        for head, end, value in (
            (z_one, end_one, jnp.where(odd, both[0], both[1])),
            (z_two, end_two, jnp.where(odd, both[1], both[0])),
        ):
            cut = min(max(HEAD - 512 * t, 0), wide)
            if cut > 0:
                head[:, 512 * t : 512 * t + cut] = value[:, :cut]
            if cut < wide:
                end[:, 512 * t + cut - HEAD : 512 * t + wide - HEAD] = value[:, cut:]


def face_kernel(low, high, frag, flags, *outs):
    odd = flags[X_ODD] > 0
    for z, plane in ((0, low), (1, high)):
        lines = slice(LANES * z, LANES * (z + 1))
        start, end = plane[:, :LANES], plane[:, WIDE - LANES :]
        for out, pair in zip(outs, ((start, end), (end, start))):
            out[lines, :] = jnp.where(odd, *pair)
    lines = [jnp.broadcast_to(frag[z, 127:128, :], (8, LANES)).astype(F32) for z in range(2)]
    lines = jnp.concatenate(lines, axis=0).astype(BF)
    for out in outs:
        out[2 * LANES :, :] = lines


def line_kernel(low, high, frag, edge, first_col, rows):
    for z, plane in ((0, low), (1, high)):
        turned = frag[z].astype(F32).T
        first_col[z : z + 1, :] = turned[0:1]
        for side, line in ((0, plane[112:128, :].astype(F32)[15:16]), (1, plane[0:16, :].astype(F32)[0:1])):
            for q in range(TILES):
                rows[2 * side + z, q : q + 1, :] = line[:, LANES * q : LANES * (q + 1)]
            rows[2 * side + z, TILES:EDGE, :] = jnp.broadcast_to(turned[127:128], (EDGE - TILES, LANES))
            edge[2 * side + z] = rows[2 * side + z].astype(BF)


def x_face_kernel(got_one, got_two, edge, flags, face, x_code, y_one, y_two):
    has_low, has_high, odd = flags[X_LOW] > 0, flags[X_HIGH] > 0, flags[X_ODD] > 0
    y_odd = flags[Y_ODD] > 0
    lane = iota((LANES, LANES), 1)
    is_low = (lane < 32) & has_low
    is_high = (lane >= 32) & (lane < 64) & has_high
    none = jnp.zeros((LANES, LANES), BF)
    row, place = iota((EDGE, LANES), 0), iota((EDGE, LANES), 1)
    ends = ((row == 0) & (place < 32)) | ((row == TILES - 1) & (place >= 32) & (place < 64))
    other = jnp.where(odd, got_one[2 * LANES :, :], got_two[2 * LANES :, :]).astype(F32)
    for z in range(2):
        lines = slice(LANES * z, LANES * (z + 1))
        low = jnp.where(odd, got_one[lines, :], got_two[lines, :])
        high = jnp.where(odd, got_two[lines, :], got_one[lines, :])
        tile = jnp.where(is_low, low, jnp.where(is_high, high, none))
        face[z] = tile
        patched = []
        for side in range(2):
            near = (tile[112:128].astype(F32)[15:16], tile[0:16].astype(F32)[0:1])[side]
            line = edge[2 * side + z].astype(F32)
            patched.append(jnp.where(ends, jnp.broadcast_to(near, (EDGE, LANES)), line).astype(BF))
        y_one[z] = jnp.where(y_odd, patched[1], patched[0])
        y_two[z] = jnp.where(y_odd, patched[0], patched[1])
        x_code[z] = jnp.where(has_low, other[8 * z : 8 * z + 1], -1.0)


def ring_kernel(face, got_one, got_two, frag, flags, y_low, y_high, z_one, z_two):
    odd, z_odd = flags[Y_ODD] > 0, flags[Z_ODD] > 0
    none = jnp.zeros((EDGE, LANES), BF)
    rings = []
    for z in range(2):
        low = jnp.where(flags[Y_LOW] > 0, jnp.where(odd, got_one[z], got_two[z]), none)
        high = jnp.where(flags[Y_HIGH] > 0, jnp.where(odd, got_two[z], got_one[z]), none)
        y_low[z] = low
        y_high[z] = high
        tile = face[z]
        folded = jnp.where(iota((HALF, LANES), 1) < HALF, tile[:HALF], pltpu.roll(tile[HALF:], HALF, 1))
        rings.append(jnp.concatenate([folded, low, high], axis=0))
    z_one[:RING, :] = jnp.where(z_odd, rings[0], rings[1])
    z_two[:RING, :] = jnp.where(z_odd, rings[1], rings[0])
    top = frag[1].astype(F32).astype(BF)
    for out in (z_one, z_two):
        out[RING:, :] = top


def banded(weight, z_off, dy, slot, quarter):
    tile = jnp.zeros((32, LANES), BF)
    if abs(z_off) <= 1:
        for q in range(4):
            dx = slot - 1 - q
            if abs(dx) <= 1:
                tile = jnp.where(quarter == q, weight[9 * (z_off + 1) + 3 * (dx + 1) + dy], tile)
    return tile


def own_kernel(low, high, conv_weight, conv_bias, acc, inner, outer, weight, scr):
    quarter = iota((32, LANES), 1) // 32
    for k in range(27):
        one = conv_weight[k].astype(F32).T.astype(BF)
        weight[k] = jnp.concatenate([one] * 4, axis=1)
    for dy in range(3):
        for slot in range(8):
            for z in range(2):
                line = slice(256 * z + 32 * slot, 256 * z + 32 * slot + 32)
                for zo in range(2):
                    inner[dy, line, LANES * zo : LANES * (zo + 1)] = banded(weight, z - zo, dy, slot, quarter)
                outer[z, 32 * slot : 32 * slot + 32, LANES * dy : LANES * (dy + 1)] = banded(
                    weight, 2 * z - 1, dy, slot, quarter
                )
    bias = jnp.concatenate([conv_bias[...]] * 8, axis=1)
    for g in range(STACK):
        scr[STEP * g + 7 : STEP * g + 8, :] = jnp.zeros((1, 768), F32)
        scr[STEP * g + STEP : STEP * g + STEP + 1, :] = jnp.zeros((1, 768), F32)

    def body(s, _):
        base = s * STACK
        left = jnp.concatenate(
            [
                jnp.concatenate(
                    [plane[:, pl.ds(pl.multiple_of((base + g) * LANES, LANES), 2 * LANES)] for g in range(STACK)],
                    axis=0,
                )
                for plane in (low, high)
            ],
            axis=1,
        )
        for dy in range(3):
            part = jnp.dot(left, inner[dy], preferred_element_type=F32)
            for g in range(STACK):
                scr[STEP * g + 8 : STEP * g + STEP, 256 * dy : 256 * dy + 256] = part[LANES * g : LANES * (g + 1)]
        for g in range(STACK):
            o = STEP * g
            acc[base + g] = (
                scr[o + 7 : o + 135, 0:256] + scr[o + 8 : o + 136, 256:512] + scr[o + 9 : o + 137, 512:768] + bias
            )
        return 0

    lax.fori_loop(0, GROUPS // STACK, body, 0)


def line_windows(chunks):
    wide = chunks.astype(F32)
    return jnp.concatenate([wide[:GROUPS], wide[1:TILES]], axis=1).astype(BF)


def edge_kernel(
    face, y_low, y_high, inner, plain, x_code, first_col, own_counts, flags, lines, ends, counts
):
    for side, (dy, source) in enumerate(((0, y_low), (2, y_high))):
        left = jnp.concatenate([line_windows(source[z]) for z in range(2)], axis=1)
        lines[side] = jnp.dot(left, inner[dy], preferred_element_type=F32)
    row = iota((LANES, 256), 0)
    lane = iota((LANES, LANES), 1)
    none = jnp.zeros((LANES, LANES), BF)
    for end in range(2):
        keep = lane < 32 if end == 0 else lane >= 32
        tiles = [jnp.where(keep, face[z], none) for z in range(2)]
        parts = []
        for dy in range(3):
            right = [inner[dy, 256 * z + LANES * end : 256 * z + LANES * end + LANES, :] for z in range(2)]
            parts.append(
                jnp.dot(
                    jnp.concatenate(tiles, axis=1), jnp.concatenate(right, axis=0), preferred_element_type=F32
                )
            )
        ends[end] = (
            jnp.where(row == 0, 0.0, pltpu.roll(parts[0], 1, 0))
            + parts[1]
            + jnp.where(row == LANES - 1, 0.0, pltpu.roll(parts[2], LANES - 1, 0))
        )
    ones = [jnp.ones((1, LANES), F32)] * 2
    x_outer = faces_product([plain[z, 0:1, :] for z in range(2)], [x_code[z] for z in range(2)], ones)
    y_outer = faces_product(
        [first_col[z : z + 1, :] for z in range(2)], [y_partner(y_low, z, flags[Y_LOW] > 0) for z in range(2)], ones
    )
    counts[...] = jnp.concatenate([own_counts[...], jnp.zeros((F, F), F32), x_outer, y_outer], axis=1)


def spread(row, copies):
    one = jnp.broadcast_to(row, (16, LANES)).astype(BF)
    return jnp.concatenate([one] * copies, axis=0)


def numbers(rows):
    return iota((rows, LANES), 0).astype(F32).astype(BF)


def line_partners(frag, y_code, x, first, hot_before):
    names = numbers(F)
    line = pl.ds(x, 1)
    hot = [spread(frag[z, line, :], 4) == names for z in range(2)]
    if hot_before is None:
        before = [frag[z, pl.ds(jnp.maximum(x - 1, 0), 1), :] + first for z in range(2)]
        hot_before = [spread(row, 4) == names for row in before]
    y_hot = [spread(y_code[z, line, :], 4) == names for z in range(2)]
    return hot, hot_before, y_hot


def faces_product(own, partner, weight):
    names = numbers(F)
    one, none = jnp.ones((F, LANES), BF), jnp.zeros((F, LANES), BF)
    left = [jnp.where(spread(row, 4) == names, one, none) for row in own]
    right = [jnp.where(spread(row, 4) == names, spread(value, 4), none) for row, value in zip(partner, weight)]
    return outer_product(jnp.concatenate(left, axis=1), jnp.concatenate(right, axis=1))


def load_numbers(frag, plain, y_code):
    lane = iota((LANES, LANES), 1)
    for z in range(2):
        value = frag[z].astype(F32)
        plain[z] = value
        y_code[z] = jnp.where(lane == 0, -1.0, pltpu.roll(value, 1, 1))


def y_partner(y_low, z, has_low):
    return jnp.where(has_low, y_low[z, TILES - 1 :, :].astype(F32)[8:9], -1.0)


def count_kernel(frag, out, plain, y_code, own_hot, pair_hot):
    load_numbers(frag, plain, y_code)
    one = jnp.ones((F, LANES), BF)
    none = jnp.zeros((F, LANES), BF)

    def body(t, total):
        hot_before = None
        first = jnp.where(t > 0, 0.0, -128.0)
        for j in range(32):
            spot = slice(LANES * j, LANES * (j + 1))
            hot, x_hot, y_hot = line_partners(plain, y_code, 32 * t + j, first, hot_before)
            hot_before = hot
            for z in range(2):
                own_hot[z, :, spot] = jnp.where(hot[z], one, none).astype(F8)
                pairs = jnp.where(x_hot[z], one, none) + jnp.where(y_hot[z], one, none)
                if z == 1:
                    pairs = pairs + jnp.where(hot[0], one, none)
                pair_hot[z, :, spot] = pairs.astype(F8)
        for z in range(2):
            total = total + outer_product(own_hot[z], pair_hot[z])
        return total

    out[...] = lax.fori_loop(0, 4, body, jnp.zeros((F, F), F32))


def slots_kernel(cells, owner, recv, rank_hot, column_hot, group, name_hot, place):
    slots = owner.shape[1]
    devices = group.shape[0]
    capacity = recv.shape[1] // devices
    hot = iota((devices, slots), 0) == owner[...]
    before = iota((slots, slots), 0) < iota((slots, slots), 1)
    earlier = jnp.dot(
        jnp.where(hot, 1.0, 0.0).astype(BF), jnp.where(before, 1.0, 0.0).astype(BF), preferred_element_type=F32
    )
    rank = jnp.sum(jnp.where(hot, earlier, 0.0), axis=0, keepdims=True).astype(jnp.int32)
    lanes = iota((LANES, slots), 0)
    rank_hot[0] = jnp.where(lanes == rank, 1.0, 0.0).astype(BF)
    rank_hot[1] = jnp.where(lanes == rank + F, 1.0, 0.0).astype(BF)
    code = jnp.concatenate([cells[0:1, :], cells[1:2, :]], axis=1)
    column_hot[...] = jnp.where(iota((4 * F, 2 * slots), 0) == (code & (4 * F - 1)), 1.0, 0.0).astype(BF)
    place[...] = jnp.full(place.shape, -4 * LANES, jnp.int32)
    for p in range(devices):
        piece = recv[:, capacity * p : capacity * (p + 1)]
        place[p : p + 1, 0:capacity] = piece
        place[p : p + 1, F : F + capacity] = piece
    group[...] = place[...] >> 7
    names = iota((LANES, LANES), 0)

    def body(p, _):
        spot = pl.ds(pl.multiple_of(p * LANES, LANES), LANES)
        name_hot[:, spot] = jnp.where((place[pl.ds(p, 1), :] & (LANES - 1)) == names, 1.0, 0.0).astype(BF)
        return 0

    lax.fori_loop(0, devices, body, 0, unroll=8)


def ahead_kernel(
    cells,
    owner,
    recv,
    frag,
    low,
    high,
    rank_hot,
    column_hot,
    group,
    name_hot,
    counts,
    plain,
    y_code,
    edge,
    first_col,
    place,
    own_hot,
    pair_hot,
    rows,
):
    line_kernel(low, high, frag, edge, first_col, rows)
    count_kernel(frag, counts, plain, y_code, own_hot, pair_hot)
    slots_kernel(cells, owner, recv, rank_hot, column_hot, group, name_hot, place)


def head_rows(head_weight):
    line, spot = iota((8, 256), 0), iota((8, 256), 1)
    head = []
    for d in range(3):
        weights = jnp.concatenate([head_weight[d : d + 1, :].astype(F32)] * 8, axis=1)
        for z in range(2):
            match = (spot // LANES == z) & ((spot // 32) % 4 == line % 4)
            head.append(jnp.where(match, jnp.broadcast_to(weights, (8, 256)), 0.0))
    return jnp.concatenate(head, axis=0).astype(BF)


def stack_affinity(groups, tile, acc, add, planes, outer, lines, head, head_bias, scr, kept, kept_at):
    for i in range(2):
        left = jnp.concatenate(
            [
                planes[i, :, (tile + g) * LANES : (tile + g + 2) * LANES]
                for g in range(STACK)
            ],
            axis=0,
        )
        part = jnp.dot(left, outer[i], preferred_element_type=F32)
        ends = [lines[side, i, groups, :] for side in range(2)]
        for g in range(STACK):
            o = STEP * g
            scr[i, o + 8 : o + STEP, :] = part[LANES * g : LANES * (g + 1)]
            scr[i, o + 7 : o + 8, 0:LANES] = ends[0][g : g + 1]
            scr[i, o + STEP : o + STEP + 1, 2 * LANES :] = ends[1][g : g + 1]
    hidden = []
    for g in range(STACK):
        o = STEP * g
        outside = [
            scr[i, o + 7 : o + 135, 0:LANES]
            + scr[i, o + 8 : o + 136, LANES : 2 * LANES]
            + scr[i, o + 9 : o + 137, 2 * LANES :]
            for i in range(2)
        ]
        total = acc(g) + jnp.concatenate(outside, axis=1)
        if add[g] is not None:
            total = total + add[g]
        hidden.append(jnp.maximum(total, 0.0).astype(BF))
    logits = outer_product(head, jnp.concatenate(hidden, axis=0))
    top_half = iota((8, LANES), 0) < 4
    for i in range(6):
        for pair in range(STACK // 2):
            at = 2 * LANES * pair
            both = logits[8 * i : 8 * i + 8]
            value = jnp.where(top_half, both[:, at : at + LANES], both[:, at + LANES : at + 2 * LANES])
            value = jax.nn.sigmoid(value + head_bias[i // 2]).astype(BF).astype(F32)
            kept[i, kept_at + 8 * pair : kept_at + 8 * pair + 8, :] = value


def table_pieces(x0, kept_at, plain, y_code, z_code, kept, lines):
    names, one, none = numbers(F), jnp.ones((F, LANES), BF), jnp.zeros((F, LANES), BF)
    low, high = jnp.zeros((3 * F, F), F32), jnp.zeros((2 * F, F), F32)
    def one_hot(row):
        return jnp.where(spread(row, 4) == names, one, none)

    before = None
    for t in range(lines // PART):
        own_rows, pair_rows = [[], []], [[], []]
        for j in range(PART):
            at = PART * t + j
            x = x0 + at
            line = slice(x, x + 1)
            weight = [spread(kept[i, kept_at + at : kept_at + at + 1, :], 4) for i in range(6)]
            hot = [one_hot(plain[z, line, :]) for z in range(2)]
            if before is None:
                before = [one_hot(plain[z, x - 1 : x, :]) if x > 0 else none for z in range(2)]
            z_hot = one_hot(z_code[line, :])
            for z in range(2):
                own_rows[z].append(hot[z])
                pair = [before[z] * weight[2 + z] + one_hot(y_code[z, line, :]) * weight[4 + z]]
                pair += [hot[0] * weight[1]] if z else [z_hot * weight[0], z_hot]
                pair_rows[z].append(jnp.concatenate(pair, axis=0))
            before = hot
        parts = [
            outer_product(jnp.concatenate(pair_rows[z], axis=1), jnp.concatenate(own_rows[z], axis=1))
            for z in range(2)
        ]
        low, high = low + parts[0], high + parts[1]
    return low.T, high.T


def first_kernel(
    acc,
    plane_one,
    plane_two,
    ring_one,
    ring_two,
    inner_lines,
    inner_ends,
    outer,
    head_weight,
    plain,
    y_code,
    x_code,
    head_bias,
    flags,
    affinity,
    kept_y,
    low_out,
    high_out,
    x_outer,
    lines,
    z_code,
    carry,
    planes,
    scr,
    kept,
):
    odd = flags[Z_ODD]
    below = jnp.where(odd > 0, ring_one[RING:, :], ring_two[RING:, :])
    z_code[...] = jnp.where(flags[Z_LOW] > 0, below.astype(F32), -1.0)
    lane = iota((LANES, LANES), 1)
    for plane, ring, i in ((plane_one, ring_one, 1 - odd), (plane_two, ring_two, odd)):
        live = jnp.where(i > 0, flags[Z_HIGH], flags[Z_LOW]) > 0
        around = jnp.where(live, ring[:RING, :], jnp.zeros((RING, LANES), BF))
        face = jnp.concatenate([around[:HALF], pltpu.roll(around[:HALF], HALF, 1)], axis=0)
        planes[i, :, LANES:] = plane[:, LANES:HEAD]
        planes[i, :, :LANES] = jnp.where(lane < 32, face, plane[:, :LANES])
        carry[i] = plane[:, HEAD - LANES : HEAD]
        carry[2 + i] = face
        for side, dy in ((0, 0), (1, 2)):
            chunks = around[HALF + EDGE * side : HALF + EDGE * (side + 1), :]
            lines[side, i] = jnp.dot(
                line_windows(chunks), outer[i, :, LANES * dy : LANES * (dy + 1)], preferred_element_type=F32
            )
    for i in range(2):
        for side in range(2):
            lines[side, i] = lines[side, i] + inner_lines[side, :, LANES * i : LANES * (i + 1)]
    head = head_rows(head_weight)

    def affinities(s):
        base, x0 = STACK * s, 4 * STACK * s
        add = [None] * STACK
        if s == 0:
            add[0] = inner_ends[0]
        stack_affinity(
            slice(base, base + STACK), base, lambda g: acc[base + g], add, planes, outer, lines, head, head_bias, scr.at[s % 2], kept, x0
        )
        all_lines = slice(x0, x0 + 4 * STACK)
        for i in range(6):
            affinity[i // 2, i % 2, all_lines, :] = kept[i, all_lines, :].astype(BF)

    for s in range(HEAD_STACKS):
        affinities(s)
    low, high = table_pieces(0, 0, plain, y_code, z_code, kept, HEAD_LINES)
    low_out[...] = low
    high_out[...] = high
    kept_y[...] = kept[4:6]
    x_outer[...] = faces_product(
        [plain[z, 0:1, :] for z in range(2)],
        [x_code[z] for z in range(2)],
        [kept[2 + z, 0:1, :] for z in range(2)],
    )


def second_kernel(
    acc,
    plane_one,
    plane_two,
    inner_ends,
    outer,
    head_weight,
    plain,
    y_code,
    y_low,
    first_col,
    counts,
    affinity_head,
    kept_y,
    low_head,
    high_head,
    x_outer,
    lines,
    z_code,
    carry,
    cells,
    owner,
    rank_hot,
    column_hot,
    head_bias,
    flags,
    affinity,
    outgoing,
    planes,
    scr,
    kept,
):
    odd = flags[Z_ODD]
    lane = iota((LANES, LANES), 1)
    wide = WIDE - HEAD
    for i in range(2):
        planes[i, :, :LANES] = carry[i]
    for plane, i in ((plane_one, 1 - odd), (plane_two, odd)):
        planes[i, :, LANES:wide] = plane[:, : wide - LANES]
        planes[i, :, wide:] = jnp.where((lane >= 32) & (lane < 64), carry[2 + i], plane[:, wide - LANES :])
    add = [None] * STACK
    add[-1] = inner_ends[1]
    groups = pl.ds(HEAD_GROUPS, STACK)
    stack_affinity(
        groups, 0, lambda g: acc[HEAD_GROUPS + g], add, planes, outer, lines, head_rows(head_weight), head_bias, scr.at[0], kept, 0
    )
    for i in range(6):
        affinity[i // 2, i % 2, :HEAD_LINES, :] = affinity_head[i // 2, i % 2]
        affinity[i // 2, i % 2, HEAD_LINES:, :] = kept[i].astype(BF)
    low, high = table_pieces(
        HEAD_LINES, 0, plain, y_code, z_code, kept, LANES - HEAD_LINES
    )
    low, high = low_head[...] + low, high_head[...] + high
    own = low[:, :F] + high[:, :F] + high[:, F:]
    y_outer = faces_product(
        [first_col[z : z + 1, :] for z in range(2)],
        [y_partner(y_low, z, flags[Y_LOW] > 0) for z in range(2)],
        [jnp.concatenate([kept_y[z], kept[4 + z]], axis=0).T[0:1, :] for z in range(2)],
    )
    sums = jnp.concatenate([own, low[:, F : 2 * F], x_outer[...], y_outer], axis=1)
    tally = counts[...] + jnp.concatenate(
        [jnp.zeros((F, F), F32), low[:, 2 * F :], jnp.zeros((F, 2 * F), F32)], axis=1
    )
    slots = cells.shape[1]
    picked = jnp.dot(
        jnp.concatenate(halves(sums) + halves(tally), axis=0), column_hot[...], preferred_element_type=F32
    )
    code = jnp.concatenate([cells[0:1, :], cells[1:2, :]], axis=1)
    line_hot = iota((F, 2 * slots), 0) == (code >> 8)
    alive = iota((1, slots), 1) < flags[LIVE]

    def part_of(value):
        total = jnp.sum(jnp.where(line_hot, value, 0.0), axis=0, keepdims=True)
        return jnp.where(alive, total[:, :slots] + total[:, slots:], 0.0)

    part_sum = part_of(picked[:F] + picked[F : 2 * F])
    part_count = part_of(picked[2 * F : 3 * F] + picked[3 * F :])
    to_owner = iota((outgoing.shape[0], slots), 0) == owner[...]
    left = [
        jnp.where(to_owner, piece.astype(F32), 0.0).astype(BF) for piece in halves(part_sum) + halves(part_count)
    ]
    sent = outer_product(
        jnp.concatenate(left, axis=1),
        jnp.concatenate([rank_hot[0], rank_hot[0], rank_hot[1], rank_hot[1]], axis=1),
    )
    outgoing[...] = sent.reshape(outgoing.shape)


def settle_kernel(received, group_of, name_hot, out, left):
    devices = received.shape[0]
    groups = out.shape[1] // LANES
    row, lane = iota((16, LANES), 0), iota((16, LANES), 1)
    of_count = row >= 2 * groups
    inner = jnp.where(of_count, row - 2 * groups, row)
    is_low = inner >= groups
    group = jnp.where(is_low, inner - groups, inner)
    group = jnp.where((lane >= F) == of_count, group, -1)
    group = jnp.where(row < 4 * groups, group, -1)

    def body(p, _):
        spot = pl.ds(pl.multiple_of(p * LANES, LANES), LANES)
        value = received[p]
        high = value.astype(BF).astype(F32)
        piece = jnp.where(is_low, value - high, high)
        left[:, spot] = jnp.where(group_of[pl.ds(p, 1), :] == group, piece, 0.0).astype(BF)
        return 0

    lax.fori_loop(0, devices, body, 0, unroll=8)
    total = outer_product(left[...], name_hot[...])
    for g in range(groups):
        total_sum = total[g : g + 1] + total[groups + g : groups + g + 1]
        total_count = total[2 * groups + g : 2 * groups + g + 1] + total[3 * groups + g : 3 * groups + g + 1]
        out[:, LANES * g : LANES * (g + 1)] = total_sum / jnp.maximum(total_count, 1.0)


def swap(one, two, axis, closed):
    n = lax.axis_size(axis)
    if n == 1:
        return jnp.zeros_like(one), jnp.zeros_like(two)
    rounds = [[(i, i + 1) for i in range(start, n - 1, 2)] for start in range(2)]
    if n == 2:
        got = lax.ppermute(one, axis, [(0, 1), (1, 0)])
        return got, got
    if closed and n % 2 == 0:
        rounds[1].append((0, n - 1))
    return tuple(
        lax.ppermute(value, axis, [pair for a, b in pairs for pair in ((a, b), (b, a))])
        for value, pairs in zip((one, two), rounds)
    )


def shards(
    features,
    conv_weight,
    conv_bias,
    head_weight,
    head_bias,
    fragments,
    edge_cells,
    edge_owner,
    edge_count,
    recv_slot,
):
    axes = ("gx", "gy", "gz")
    size = {axis: lax.axis_size(axis) for axis in axes}
    at = {axis: lax.axis_index(axis) for axis in axes}
    devices = size["gx"] * size["gy"] * size["gz"]
    capacity = recv_slot.shape[1] // devices
    slots = edge_cells.shape[1]
    own_slots = devices * capacity // 4
    flags = []
    for axis in axes:
        flags += [at[axis], size[axis] - 1 - at[axis], at[axis] % 2]
    flags = jnp.stack(flags + [edge_count[0]]).astype(jnp.int32)

    xt_low, xt_high, z_one, z_two, end_one, end_two = pl.pallas_call(
        layout_kernel,
        out_shape=(shape((LANES, WIDE), BF),) * 2
        + (shape((LANES, HEAD), BF),) * 2
        + (shape((LANES, WIDE - HEAD), BF),) * 2,
        in_specs=[SMEM, pl.BlockSpec(memory_space=pltpu.HBM)],
        out_specs=(VMEM,) * 6,
        scratch_shapes=[pltpu.VMEM(features.shape, BF), pltpu.SemaphoreType.DMA((8,))],
        compiler_params=pltpu.CompilerParams(vmem_limit_bytes=28 << 20),
        cost_estimate=pl.CostEstimate(flops=1_000_000, bytes_accessed=1 << 17, transcendentals=0),
        name="layout",
    )(flags, pltpu.with_memory_space_constraint(features, pltpu.HBM))
    plane_one, plane_two = swap(z_one, z_two, "gz", False)
    acc, inner, outer = call(
        own_kernel,
        "own_planes",
        (shape((GROUPS, LANES, 256), F32), shape((3, 512, 256), BF), shape((2, 256, 3 * LANES), BF)),
        (xt_low, xt_high, conv_weight, conv_bias.reshape(1, -1)),
        0,
        [pltpu.VMEM((27, 32, LANES), BF), pltpu.VMEM((STEP * STACK + 8, 768), F32)],
        flops=300_000_000,
    )
    x_sent = call(
        face_kernel,
        "faces",
        (shape((2 * LANES + 16, LANES), BF),) * (1 if size["gx"] == 2 else 2),
        (xt_low, xt_high, fragments, flags),
        1,
    )
    x_got = swap(x_sent[0], x_sent[-1], "gx", True)

    owner = edge_owner.reshape(1, slots)
    rank_hot, column_hot, group, name_hot, own_counts, plain, y_code, edge, first_col = call(
        ahead_kernel,
        "ahead",
        (
            shape((2, LANES, slots), BF),
            shape((4 * F, 2 * slots), BF),
            shape((devices, LANES), jnp.int32),
            shape((LANES, devices * LANES), BF),
            shape((F, F), F32),
            shape((2, LANES, LANES), F32),
            shape((2, LANES, LANES), F32),
            shape((4, EDGE, LANES), BF),
            shape((2, LANES), F32),
        ),
        (edge_cells, owner, recv_slot, fragments, xt_low, xt_high),
        0,
        [
            pltpu.VMEM((devices, LANES), jnp.int32),
            pltpu.VMEM((2, F, 4096), F8),
            pltpu.VMEM((2, F, 4096), F8),
            pltpu.VMEM((4, EDGE, LANES), F32),
        ],
        flops=75_000_000,
    )
    *x_got, group = lax.optimization_barrier((*x_got, group))
    face, x_code, y_one, y_two = call(
        x_face_kernel,
        "x_face",
        (
            shape((2, LANES, LANES), BF),
            shape((2, 1, LANES), F32),
            shape((2, EDGE, LANES), BF),
            shape((2, EDGE, LANES), BF),
        ),
        (*x_got, edge, flags),
        1,
    )
    *y_got, outer = lax.optimization_barrier((*swap(y_one, y_two, "gy", True), outer))
    y_low, y_high, ring_one, ring_two = call(
        ring_kernel,
        "ring",
        (shape((2, EDGE, LANES), BF),) * 2 + (shape((RING + LANES, LANES), BF),) * 2,
        (face, *y_got, fragments, flags),
        1,
    )
    ring_one, ring_two = swap(ring_one, ring_two, "gz", False)

    lines, ends, counts = call(
        edge_kernel,
        "edges",
        (shape((2, GROUPS, 256), F32), shape((2, LANES, 256), F32), shape((F, 4 * F), F32)),
        (face, y_low, y_high, inner, plain, x_code, first_col, own_counts, flags),
        1,
        flops=50_000_000,
    )

    end_one, end_two, counts = lax.optimization_barrier((end_one, end_two, counts))
    end_one, end_two = swap(end_one, end_two, "gz", False)

    def stack_scratch(tiles, kept_lines):
        return [
            pltpu.VMEM((2, LANES, tiles * LANES), BF),
            pltpu.VMEM((min(2, kept_lines // 32), 2, STEP * STACK + 8, 3 * LANES), F32),
            pltpu.VMEM((6, kept_lines, LANES), F32),
        ]

    done = call(
        first_kernel,
        "first_lines",
        (
            shape((3, 2, HEAD_LINES, LANES), BF),
            shape((2, HEAD_LINES, LANES), F32),
            shape((F, 3 * F), F32),
            shape((F, 2 * F), F32),
            shape((F, F), F32),
            shape((2, 2, GROUPS, LANES), F32),
            shape((LANES, LANES), F32),
            shape((4, LANES, LANES), BF),
        ),
        (
            acc,
            plane_one,
            plane_two,
            ring_one,
            ring_two,
            lines,
            ends,
            outer,
            head_weight,
            plain,
            y_code,
            x_code,
            head_bias,
            flags,
        ),
        2,
        stack_scratch(HEAD_GROUPS + 1, HEAD_LINES),
        flops=6_000_000_000,
    )
    affinity, outgoing = call(
        second_kernel,
        "last_lines",
        (shape((3, 2, LANES, LANES), BF), shape((devices, 1, LANES), F32)),
        (
            acc,
            end_one,
            end_two,
            ends,
            outer,
            head_weight,
            plain,
            y_code,
            y_low,
            first_col,
            counts,
            *done,
            edge_cells,
            owner,
            rank_hot,
            column_hot,
            head_bias,
            flags,
        ),
        2,
        stack_scratch(TILES - HEAD_GROUPS, LANES - HEAD_LINES),
        flops=3_000_000_000,
    )
    received = lax.all_to_all(outgoing, axes, split_axis=0, concat_axis=0, tiled=True)
    edge_mean = call(
        settle_kernel,
        "settle",
        shape((1, own_slots), F32),
        (received, group, name_hot),
        0,
        [pltpu.VMEM((16, devices * LANES), BF)],
    )
    return affinity, edge_mean


def solution(mesh):
    in_specs = (
        P(None, "gz", "gx", "gy"),
        P(),
        P(),
        P(),
        P(),
        P("gz", "gx", "gy"),
        P(None, ("gx", "gy", "gz")),
        P(("gx", "gy", "gz"), None),
        P(("gx", "gy", "gz")),
        P(("gx", "gy", "gz"), None),
    )
    out_specs = (P(None, "gz", "gx", "gy"), P(("gx", "gy", "gz"), None))
    return jax.shard_map(shards, mesh=mesh, in_specs=in_specs, out_specs=out_specs, check_vma=False)
```

```python
import jax
import jax.numpy as jnp
from jax import lax
from jax.experimental import pallas as pl
from jax.experimental.pallas import tpu as pltpu
from jax.sharding import PartitionSpec as P

F = 64
LANES = 128
GROUPS = 32
TILES = GROUPS + 1
WIDE = TILES * LANES
STACK = 8
STEP = LANES + 8
EDGE = 48
HALF = LANES // 2
RING = HALF + 2 * EDGE
PART = 16
HEAD_STACKS = 3
HEAD_GROUPS = HEAD_STACKS * STACK
HEAD = (HEAD_GROUPS + 1) * LANES
HEAD_LINES = 4 * HEAD_GROUPS
BF = jnp.bfloat16
F32 = jnp.float32
F8 = jnp.float8_e4m3fn
VMEM = pl.BlockSpec(memory_space=pltpu.VMEM)
SMEM = pl.BlockSpec(memory_space=pltpu.SMEM)


def call(kernel, name, out_shape, args, smem, scratch=(), flops=1_000_000):
    return pl.pallas_call(
        kernel,
        out_shape=out_shape,
        in_specs=[VMEM] * (len(args) - smem) + [SMEM] * smem,
        out_specs=jax.tree.map(lambda _: VMEM, out_shape),
        scratch_shapes=list(scratch),
        compiler_params=pltpu.CompilerParams(vmem_limit_bytes=28 << 20),
        cost_estimate=pl.CostEstimate(flops=flops, bytes_accessed=1 << 17, transcendentals=0),
        name=name,
    )(*args)


def shape(dims, dtype):
    return jax.ShapeDtypeStruct(dims, dtype)


def iota(dims, axis):
    return lax.broadcasted_iota(jnp.int32, dims, axis)


X_LOW, X_HIGH, X_ODD, Y_LOW, Y_HIGH, Y_ODD, Z_LOW, Z_HIGH, Z_ODD, LIVE = range(10)


def outer_product(left, right):
    return lax.dot_general(left, right, (((1,), (1,)), ((), ())), preferred_element_type=F32)


def halves(value):
    high = value.astype(BF)
    return high, (value - high.astype(F32)).astype(BF)


def layout_kernel(flags, feat_hbm, low, high, z_one, z_two, end_one, end_two, feat, sems):
    copies = []
    for t in range(8):
        lines = slice(16 * t, 16 * t + 16)
        copies.append(pltpu.make_async_copy(feat_hbm.at[:, :, lines, :], feat.at[:, :, lines, :], sems.at[t]))
        copies[-1].start()
    odd = flags[Z_ODD] > 0
    zero = jnp.zeros((32, LANES), BF)
    last = [zero, zero]
    for t in range(9):
        if t < 8:
            copies[t].wait()
        both = []
        for z, plane in ((0, low), (1, high)):
            if t < 8:
                block = jnp.swapaxes(feat[:, z, 16 * t : 16 * t + 16, :], 0, 1).reshape(512, LANES)
                turned = jnp.concatenate([last[z], block[:480]], axis=0).T
                last[z] = block[480:]
            else:
                turned = jnp.concatenate([last[z], zero, zero, zero], axis=0).T
            wide = turned.shape[1]
            plane[:, 512 * t : 512 * t + wide] = turned
            both.append(turned)
        for head, end, value in (
            (z_one, end_one, jnp.where(odd, both[0], both[1])),
            (z_two, end_two, jnp.where(odd, both[1], both[0])),
        ):
            cut = min(max(HEAD - 512 * t, 0), wide)
            if cut > 0:
                head[:, 512 * t : 512 * t + cut] = value[:, :cut]
            if cut < wide:
                end[:, 512 * t + cut - HEAD : 512 * t + wide - HEAD] = value[:, cut:]


def face_kernel(low, high, frag, flags, *outs):
    odd = flags[X_ODD] > 0
    for z, plane in ((0, low), (1, high)):
        lines = slice(LANES * z, LANES * (z + 1))
        start, end = plane[:, :LANES], plane[:, WIDE - LANES :]
        for out, pair in zip(outs, ((start, end), (end, start))):
            out[lines, :] = jnp.where(odd, *pair)
    lines = [jnp.broadcast_to(frag[z, 127:128, :], (8, LANES)).astype(F32) for z in range(2)]
    lines = jnp.concatenate(lines, axis=0).astype(BF)
    for out in outs:
        out[2 * LANES :, :] = lines


def line_kernel(low, high, frag, edge, first_col, rows):
    for z, plane in ((0, low), (1, high)):
        turned = frag[z].astype(F32).T
        first_col[z : z + 1, :] = turned[0:1]
        for side, line in ((0, plane[112:128, :].astype(F32)[15:16]), (1, plane[0:16, :].astype(F32)[0:1])):
            for q in range(TILES):
                rows[2 * side + z, q : q + 1, :] = line[:, LANES * q : LANES * (q + 1)]
            rows[2 * side + z, TILES:EDGE, :] = jnp.broadcast_to(turned[127:128], (EDGE - TILES, LANES))
            edge[2 * side + z] = rows[2 * side + z].astype(BF)


def x_face_kernel(got_one, got_two, edge, flags, face, x_code, y_one, y_two):
    has_low, has_high, odd = flags[X_LOW] > 0, flags[X_HIGH] > 0, flags[X_ODD] > 0
    y_odd = flags[Y_ODD] > 0
    lane = iota((LANES, LANES), 1)
    is_low = (lane < 32) & has_low
    is_high = (lane >= 32) & (lane < 64) & has_high
    none = jnp.zeros((LANES, LANES), BF)
    row, place = iota((EDGE, LANES), 0), iota((EDGE, LANES), 1)
    ends = ((row == 0) & (place < 32)) | ((row == TILES - 1) & (place >= 32) & (place < 64))
    other = jnp.where(odd, got_one[2 * LANES :, :], got_two[2 * LANES :, :]).astype(F32)
    for z in range(2):
        lines = slice(LANES * z, LANES * (z + 1))
        low = jnp.where(odd, got_one[lines, :], got_two[lines, :])
        high = jnp.where(odd, got_two[lines, :], got_one[lines, :])
        tile = jnp.where(is_low, low, jnp.where(is_high, high, none))
        face[z] = tile
        patched = []
        for side in range(2):
            near = (tile[112:128].astype(F32)[15:16], tile[0:16].astype(F32)[0:1])[side]
            line = edge[2 * side + z].astype(F32)
            patched.append(jnp.where(ends, jnp.broadcast_to(near, (EDGE, LANES)), line).astype(BF))
        y_one[z] = jnp.where(y_odd, patched[1], patched[0])
        y_two[z] = jnp.where(y_odd, patched[0], patched[1])
        x_code[z] = jnp.where(has_low, other[8 * z : 8 * z + 1], -1.0)


def ring_kernel(face, got_one, got_two, frag, flags, y_low, y_high, z_one, z_two):
    odd, z_odd = flags[Y_ODD] > 0, flags[Z_ODD] > 0
    none = jnp.zeros((EDGE, LANES), BF)
    rings = []
    for z in range(2):
        low = jnp.where(flags[Y_LOW] > 0, jnp.where(odd, got_one[z], got_two[z]), none)
        high = jnp.where(flags[Y_HIGH] > 0, jnp.where(odd, got_two[z], got_one[z]), none)
        y_low[z] = low
        y_high[z] = high
        tile = face[z]
        folded = jnp.where(iota((HALF, LANES), 1) < HALF, tile[:HALF], pltpu.roll(tile[HALF:], HALF, 1))
        rings.append(jnp.concatenate([folded, low, high], axis=0))
    z_one[:RING, :] = jnp.where(z_odd, rings[0], rings[1])
    z_two[:RING, :] = jnp.where(z_odd, rings[1], rings[0])
    top = frag[1].astype(F32).astype(BF)
    for out in (z_one, z_two):
        out[RING:, :] = top


def banded(weight, z_off, dy, slot, quarter):
    tile = jnp.zeros((32, LANES), BF)
    if abs(z_off) <= 1:
        for q in range(4):
            dx = slot - 1 - q
            if abs(dx) <= 1:
                tile = jnp.where(quarter == q, weight[9 * (z_off + 1) + 3 * (dx + 1) + dy], tile)
    return tile


def own_kernel(low, high, conv_weight, conv_bias, acc, inner, outer, weight, scr):
    quarter = iota((32, LANES), 1) // 32
    for k in range(27):
        one = conv_weight[k].astype(F32).T.astype(BF)
        weight[k] = jnp.concatenate([one] * 4, axis=1)
    for dy in range(3):
        for slot in range(8):
            for z in range(2):
                line = slice(256 * z + 32 * slot, 256 * z + 32 * slot + 32)
                for zo in range(2):
                    inner[dy, line, LANES * zo : LANES * (zo + 1)] = banded(weight, z - zo, dy, slot, quarter)
                outer[z, 32 * slot : 32 * slot + 32, LANES * dy : LANES * (dy + 1)] = banded(
                    weight, 2 * z - 1, dy, slot, quarter
                )
    bias = jnp.concatenate([conv_bias[...]] * 8, axis=1)
    for g in range(STACK):
        scr[STEP * g + 7 : STEP * g + 8, :] = jnp.zeros((1, 768), F32)
        scr[STEP * g + STEP : STEP * g + STEP + 1, :] = jnp.zeros((1, 768), F32)

    def body(s, _):
        base = s * STACK
        left = jnp.concatenate(
            [
                jnp.concatenate(
                    [plane[:, pl.ds(pl.multiple_of((base + g) * LANES, LANES), 2 * LANES)] for g in range(STACK)],
                    axis=0,
                )
                for plane in (low, high)
            ],
            axis=1,
        )
        for dy in range(3):
            part = jnp.dot(left, inner[dy], preferred_element_type=F32)
            for g in range(STACK):
                scr[STEP * g + 8 : STEP * g + STEP, 256 * dy : 256 * dy + 256] = part[LANES * g : LANES * (g + 1)]
        for g in range(STACK):
            o = STEP * g
            acc[base + g] = (
                scr[o + 7 : o + 135, 0:256] + scr[o + 8 : o + 136, 256:512] + scr[o + 9 : o + 137, 512:768] + bias
            )
        return 0

    lax.fori_loop(0, GROUPS // STACK, body, 0)


def line_windows(chunks):
    wide = chunks.astype(F32)
    return jnp.concatenate([wide[:GROUPS], wide[1:TILES]], axis=1).astype(BF)


def edge_kernel(
    face, y_low, y_high, inner, plain, x_code, first_col, own_counts, flags, lines, ends, counts
):
    for side, (dy, source) in enumerate(((0, y_low), (2, y_high))):
        left = jnp.concatenate([line_windows(source[z]) for z in range(2)], axis=1)
        lines[side] = jnp.dot(left, inner[dy], preferred_element_type=F32)
    row = iota((LANES, 256), 0)
    lane = iota((LANES, LANES), 1)
    none = jnp.zeros((LANES, LANES), BF)
    for end in range(2):
        keep = lane < 32 if end == 0 else lane >= 32
        tiles = [jnp.where(keep, face[z], none) for z in range(2)]
        parts = []
        for dy in range(3):
            right = [inner[dy, 256 * z + LANES * end : 256 * z + LANES * end + LANES, :] for z in range(2)]
            parts.append(
                jnp.dot(
                    jnp.concatenate(tiles, axis=1), jnp.concatenate(right, axis=0), preferred_element_type=F32
                )
            )
        ends[end] = (
            jnp.where(row == 0, 0.0, pltpu.roll(parts[0], 1, 0))
            + parts[1]
            + jnp.where(row == LANES - 1, 0.0, pltpu.roll(parts[2], LANES - 1, 0))
        )
    ones = [jnp.ones((1, LANES), F32)] * 2
    x_outer = faces_product([plain[z, 0:1, :] for z in range(2)], [x_code[z] for z in range(2)], ones)
    y_outer = faces_product(
        [first_col[z : z + 1, :] for z in range(2)], [y_partner(y_low, z, flags[Y_LOW] > 0) for z in range(2)], ones
    )
    counts[...] = jnp.concatenate([own_counts[...], jnp.zeros((F, F), F32), x_outer, y_outer], axis=1)


def spread(row, copies):
    one = jnp.broadcast_to(row, (16, LANES)).astype(BF)
    return jnp.concatenate([one] * copies, axis=0)


def numbers(rows):
    return iota((rows, LANES), 0).astype(F32).astype(BF)


def line_partners(frag, y_code, x, first, hot_before):
    names = numbers(F)
    line = pl.ds(x, 1)
    hot = [spread(frag[z, line, :], 4) == names for z in range(2)]
    if hot_before is None:
        before = [frag[z, pl.ds(jnp.maximum(x - 1, 0), 1), :] + first for z in range(2)]
        hot_before = [spread(row, 4) == names for row in before]
    y_hot = [spread(y_code[z, line, :], 4) == names for z in range(2)]
    return hot, hot_before, y_hot


def faces_product(own, partner, weight):
    names = numbers(F)
    one, none = jnp.ones((F, LANES), BF), jnp.zeros((F, LANES), BF)
    left = [jnp.where(spread(row, 4) == names, one, none) for row in own]
    right = [jnp.where(spread(row, 4) == names, spread(value, 4), none) for row, value in zip(partner, weight)]
    return outer_product(jnp.concatenate(left, axis=1), jnp.concatenate(right, axis=1))


def load_numbers(frag, plain, y_code):
    lane = iota((LANES, LANES), 1)
    for z in range(2):
        value = frag[z].astype(F32)
        plain[z] = value
        y_code[z] = jnp.where(lane == 0, -1.0, pltpu.roll(value, 1, 1))


def y_partner(y_low, z, has_low):
    return jnp.where(has_low, y_low[z, TILES - 1 :, :].astype(F32)[8:9], -1.0)


def count_kernel(frag, out, plain, y_code, own_hot, pair_hot):
    load_numbers(frag, plain, y_code)
    one = jnp.ones((F, LANES), BF)
    none = jnp.zeros((F, LANES), BF)

    def body(t, total):
        hot_before = None
        first = jnp.where(t > 0, 0.0, -128.0)
        for j in range(32):
            spot = slice(LANES * j, LANES * (j + 1))
            hot, x_hot, y_hot = line_partners(plain, y_code, 32 * t + j, first, hot_before)
            hot_before = hot
            for z in range(2):
                own_hot[z, :, spot] = jnp.where(hot[z], one, none).astype(F8)
                pairs = jnp.where(x_hot[z], one, none) + jnp.where(y_hot[z], one, none)
                if z == 1:
                    pairs = pairs + jnp.where(hot[0], one, none)
                pair_hot[z, :, spot] = pairs.astype(F8)
        for z in range(2):
            total = total + outer_product(own_hot[z], pair_hot[z])
        return total

    out[...] = lax.fori_loop(0, 4, body, jnp.zeros((F, F), F32))


def slots_kernel(cells, owner, recv, rank_hot, column_hot, group, name_hot, place):
    slots = owner.shape[1]
    devices = group.shape[0]
    capacity = recv.shape[1] // devices
    hot = iota((devices, slots), 0) == owner[...]
    before = iota((slots, slots), 0) < iota((slots, slots), 1)
    earlier = jnp.dot(
        jnp.where(hot, 1.0, 0.0).astype(BF), jnp.where(before, 1.0, 0.0).astype(BF), preferred_element_type=F32
    )
    rank = jnp.sum(jnp.where(hot, earlier, 0.0), axis=0, keepdims=True).astype(jnp.int32)
    lanes = iota((LANES, slots), 0)
    rank_hot[0] = jnp.where(lanes == rank, 1.0, 0.0).astype(BF)
    rank_hot[1] = jnp.where(lanes == rank + F, 1.0, 0.0).astype(BF)
    code = jnp.concatenate([cells[0:1, :], cells[1:2, :]], axis=1)
    column_hot[...] = jnp.where(iota((4 * F, 2 * slots), 0) == (code & (4 * F - 1)), 1.0, 0.0).astype(BF)
    place[...] = jnp.full(place.shape, -4 * LANES, jnp.int32)
    for p in range(devices):
        piece = recv[:, capacity * p : capacity * (p + 1)]
        place[p : p + 1, 0:capacity] = piece
        place[p : p + 1, F : F + capacity] = piece
    group[...] = place[...] >> 7
    names = iota((LANES, LANES), 0)

    def body(p, _):
        spot = pl.ds(pl.multiple_of(p * LANES, LANES), LANES)
        name_hot[:, spot] = jnp.where((place[pl.ds(p, 1), :] & (LANES - 1)) == names, 1.0, 0.0).astype(BF)
        return 0

    lax.fori_loop(0, devices, body, 0, unroll=8)


def ahead_kernel(
    cells,
    owner,
    recv,
    frag,
    low,
    high,
    rank_hot,
    column_hot,
    group,
    name_hot,
    counts,
    plain,
    y_code,
    edge,
    first_col,
    place,
    own_hot,
    pair_hot,
    rows,
):
    line_kernel(low, high, frag, edge, first_col, rows)
    count_kernel(frag, counts, plain, y_code, own_hot, pair_hot)
    slots_kernel(cells, owner, recv, rank_hot, column_hot, group, name_hot, place)


def head_rows(head_weight):
    line, spot = iota((8, 256), 0), iota((8, 256), 1)
    head = []
    for d in range(3):
        weights = jnp.concatenate([head_weight[d : d + 1, :].astype(F32)] * 8, axis=1)
        for z in range(2):
            match = (spot // LANES == z) & ((spot // 32) % 4 == line % 4)
            head.append(jnp.where(match, jnp.broadcast_to(weights, (8, 256)), 0.0))
    return jnp.concatenate(head, axis=0).astype(BF)


def stack_affinity(groups, tile, acc, add, planes, outer, lines, head, head_bias, scr, kept, kept_at):
    for i in range(2):
        left = jnp.concatenate(
            [
                planes[i, :, (tile + g) * LANES : (tile + g + 2) * LANES]
                for g in range(STACK)
            ],
            axis=0,
        )
        part = jnp.dot(left, outer[i], preferred_element_type=F32)
        ends = [lines[side, i, groups, :] for side in range(2)]
        for g in range(STACK):
            o = STEP * g
            scr[i, o + 8 : o + STEP, :] = part[LANES * g : LANES * (g + 1)]
            scr[i, o + 7 : o + 8, 0:LANES] = ends[0][g : g + 1]
            scr[i, o + STEP : o + STEP + 1, 2 * LANES :] = ends[1][g : g + 1]
    hidden = []
    for g in range(STACK):
        o = STEP * g
        outside = [
            scr[i, o + 7 : o + 135, 0:LANES]
            + scr[i, o + 8 : o + 136, LANES : 2 * LANES]
            + scr[i, o + 9 : o + 137, 2 * LANES :]
            for i in range(2)
        ]
        total = acc(g) + jnp.concatenate(outside, axis=1)
        if add[g] is not None:
            total = total + add[g]
        hidden.append(jnp.maximum(total, 0.0).astype(BF))
    logits = outer_product(head, jnp.concatenate(hidden, axis=0))
    top_half = iota((8, LANES), 0) < 4
    for i in range(6):
        for pair in range(STACK // 2):
            at = 2 * LANES * pair
            both = logits[8 * i : 8 * i + 8]
            value = jnp.where(top_half, both[:, at : at + LANES], both[:, at + LANES : at + 2 * LANES])
            value = jax.nn.sigmoid(value + head_bias[i // 2]).astype(BF).astype(F32)
            kept[i, kept_at + 8 * pair : kept_at + 8 * pair + 8, :] = value


def table_pieces(x0, kept_at, plain, y_code, z_code, kept, lines):
    names, one, none = numbers(F), jnp.ones((F, LANES), BF), jnp.zeros((F, LANES), BF)
    low, high = jnp.zeros((3 * F, F), F32), jnp.zeros((2 * F, F), F32)
    def one_hot(row):
        return jnp.where(spread(row, 4) == names, one, none)

    before = None
    for t in range(lines // PART):
        own_rows, pair_rows = [[], []], [[], []]
        for j in range(PART):
            at = PART * t + j
            x = x0 + at
            line = slice(x, x + 1)
            weight = [spread(kept[i, kept_at + at : kept_at + at + 1, :], 4) for i in range(6)]
            hot = [one_hot(plain[z, line, :]) for z in range(2)]
            if before is None:
                before = [one_hot(plain[z, x - 1 : x, :]) if x > 0 else none for z in range(2)]
            z_hot = one_hot(z_code[line, :])
            for z in range(2):
                own_rows[z].append(hot[z])
                pair = [before[z] * weight[2 + z] + one_hot(y_code[z, line, :]) * weight[4 + z]]
                pair += [hot[0] * weight[1]] if z else [z_hot * weight[0], z_hot]
                pair_rows[z].append(jnp.concatenate(pair, axis=0))
            before = hot
        parts = [
            outer_product(jnp.concatenate(pair_rows[z], axis=1), jnp.concatenate(own_rows[z], axis=1))
            for z in range(2)
        ]
        low, high = low + parts[0], high + parts[1]
    return low.T, high.T


def first_kernel(
    acc,
    plane_one,
    plane_two,
    ring_one,
    ring_two,
    inner_lines,
    inner_ends,
    outer,
    head_weight,
    plain,
    y_code,
    x_code,
    head_bias,
    flags,
    affinity,
    kept_y,
    low_out,
    high_out,
    x_outer,
    lines,
    z_code,
    carry,
    planes,
    scr,
    kept,
):
    odd = flags[Z_ODD]
    below = jnp.where(odd > 0, ring_one[RING:, :], ring_two[RING:, :])
    z_code[...] = jnp.where(flags[Z_LOW] > 0, below.astype(F32), -1.0)
    lane = iota((LANES, LANES), 1)
    for plane, ring, i in ((plane_one, ring_one, 1 - odd), (plane_two, ring_two, odd)):
        live = jnp.where(i > 0, flags[Z_HIGH], flags[Z_LOW]) > 0
        around = jnp.where(live, ring[:RING, :], jnp.zeros((RING, LANES), BF))
        face = jnp.concatenate([around[:HALF], pltpu.roll(around[:HALF], HALF, 1)], axis=0)
        planes[i, :, LANES:] = plane[:, LANES:HEAD]
        planes[i, :, :LANES] = jnp.where(lane < 32, face, plane[:, :LANES])
        carry[i] = plane[:, HEAD - LANES : HEAD]
        carry[2 + i] = face
        for side, dy in ((0, 0), (1, 2)):
            chunks = around[HALF + EDGE * side : HALF + EDGE * (side + 1), :]
            lines[side, i] = jnp.dot(
                line_windows(chunks), outer[i, :, LANES * dy : LANES * (dy + 1)], preferred_element_type=F32
            )
    for i in range(2):
        for side in range(2):
            lines[side, i] = lines[side, i] + inner_lines[side, :, LANES * i : LANES * (i + 1)]
    head = head_rows(head_weight)

    def affinities(s):
        base, x0 = STACK * s, 4 * STACK * s
        add = [None] * STACK
        if s == 0:
            add[0] = inner_ends[0]
        stack_affinity(
            slice(base, base + STACK), base, lambda g: acc[base + g], add, planes, outer, lines, head, head_bias, scr.at[s % 2], kept, x0
        )
        all_lines = slice(x0, x0 + 4 * STACK)
        for i in range(6):
            affinity[i // 2, i % 2, all_lines, :] = kept[i, all_lines, :].astype(BF)

    affinities(0)
    low, high = jnp.zeros((F, 3 * F), F32), jnp.zeros((F, 2 * F), F32)
    for s in range(HEAD_STACKS):
        if s + 1 < HEAD_STACKS:
            affinities(s + 1)
        x0 = 4 * STACK * s
        more = table_pieces(x0, x0, plain, y_code, z_code, kept, 4 * STACK)
        low, high = low + more[0], high + more[1]
    low_out[...] = low
    high_out[...] = high
    kept_y[...] = kept[4:6]
    x_outer[...] = faces_product(
        [plain[z, 0:1, :] for z in range(2)],
        [x_code[z] for z in range(2)],
        [kept[2 + z, 0:1, :] for z in range(2)],
    )


def second_kernel(
    acc,
    plane_one,
    plane_two,
    inner_ends,
    outer,
    head_weight,
    plain,
    y_code,
    y_low,
    first_col,
    counts,
    affinity_head,
    kept_y,
    low_head,
    high_head,
    x_outer,
    lines,
    z_code,
    carry,
    cells,
    owner,
    rank_hot,
    column_hot,
    head_bias,
    flags,
    affinity,
    outgoing,
    planes,
    scr,
    kept,
):
    odd = flags[Z_ODD]
    lane = iota((LANES, LANES), 1)
    wide = WIDE - HEAD
    for i in range(2):
        planes[i, :, :LANES] = carry[i]
    for plane, i in ((plane_one, 1 - odd), (plane_two, odd)):
        planes[i, :, LANES:wide] = plane[:, : wide - LANES]
        planes[i, :, wide:] = jnp.where((lane >= 32) & (lane < 64), carry[2 + i], plane[:, wide - LANES :])
    add = [None] * STACK
    add[-1] = inner_ends[1]
    groups = pl.ds(HEAD_GROUPS, STACK)
    stack_affinity(
        groups, 0, lambda g: acc[HEAD_GROUPS + g], add, planes, outer, lines, head_rows(head_weight), head_bias, scr.at[0], kept, 0
    )
    for i in range(6):
        affinity[i // 2, i % 2, :HEAD_LINES, :] = affinity_head[i // 2, i % 2]
        affinity[i // 2, i % 2, HEAD_LINES:, :] = kept[i].astype(BF)
    low, high = table_pieces(
        HEAD_LINES, 0, plain, y_code, z_code, kept, LANES - HEAD_LINES
    )
    low, high = low_head[...] + low, high_head[...] + high
    own = low[:, :F] + high[:, :F] + high[:, F:]
    y_outer = faces_product(
        [first_col[z : z + 1, :] for z in range(2)],
        [y_partner(y_low, z, flags[Y_LOW] > 0) for z in range(2)],
        [jnp.concatenate([kept_y[z], kept[4 + z]], axis=0).T[0:1, :] for z in range(2)],
    )
    sums = jnp.concatenate([own, low[:, F : 2 * F], x_outer[...], y_outer], axis=1)
    tally = counts[...] + jnp.concatenate(
        [jnp.zeros((F, F), F32), low[:, 2 * F :], jnp.zeros((F, 2 * F), F32)], axis=1
    )
    slots = cells.shape[1]
    picked = jnp.dot(
        jnp.concatenate(halves(sums) + halves(tally), axis=0), column_hot[...], preferred_element_type=F32
    )
    code = jnp.concatenate([cells[0:1, :], cells[1:2, :]], axis=1)
    line_hot = iota((F, 2 * slots), 0) == (code >> 8)
    alive = iota((1, slots), 1) < flags[LIVE]

    def part_of(value):
        total = jnp.sum(jnp.where(line_hot, value, 0.0), axis=0, keepdims=True)
        return jnp.where(alive, total[:, :slots] + total[:, slots:], 0.0)

    part_sum = part_of(picked[:F] + picked[F : 2 * F])
    part_count = part_of(picked[2 * F : 3 * F] + picked[3 * F :])
    to_owner = iota((outgoing.shape[0], slots), 0) == owner[...]
    left = [
        jnp.where(to_owner, piece.astype(F32), 0.0).astype(BF) for piece in halves(part_sum) + halves(part_count)
    ]
    sent = outer_product(
        jnp.concatenate(left, axis=1),
        jnp.concatenate([rank_hot[0], rank_hot[0], rank_hot[1], rank_hot[1]], axis=1),
    )
    outgoing[...] = sent.reshape(outgoing.shape)


def settle_kernel(received, group_of, name_hot, out, left):
    devices = received.shape[0]
    groups = out.shape[1] // LANES
    row, lane = iota((16, LANES), 0), iota((16, LANES), 1)
    of_count = row >= 2 * groups
    inner = jnp.where(of_count, row - 2 * groups, row)
    is_low = inner >= groups
    group = jnp.where(is_low, inner - groups, inner)
    group = jnp.where((lane >= F) == of_count, group, -1)
    group = jnp.where(row < 4 * groups, group, -1)

    def body(p, _):
        spot = pl.ds(pl.multiple_of(p * LANES, LANES), LANES)
        value = received[p]
        high = value.astype(BF).astype(F32)
        piece = jnp.where(is_low, value - high, high)
        left[:, spot] = jnp.where(group_of[pl.ds(p, 1), :] == group, piece, 0.0).astype(BF)
        return 0

    lax.fori_loop(0, devices, body, 0, unroll=8)
    total = outer_product(left[...], name_hot[...])
    for g in range(groups):
        total_sum = total[g : g + 1] + total[groups + g : groups + g + 1]
        total_count = total[2 * groups + g : 2 * groups + g + 1] + total[3 * groups + g : 3 * groups + g + 1]
        out[:, LANES * g : LANES * (g + 1)] = total_sum / jnp.maximum(total_count, 1.0)


def swap(one, two, axis, closed):
    n = lax.axis_size(axis)
    if n == 1:
        return jnp.zeros_like(one), jnp.zeros_like(two)
    rounds = [[(i, i + 1) for i in range(start, n - 1, 2)] for start in range(2)]
    if n == 2:
        got = lax.ppermute(one, axis, [(0, 1), (1, 0)])
        return got, got
    if closed and n % 2 == 0:
        rounds[1].append((0, n - 1))
    return tuple(
        lax.ppermute(value, axis, [pair for a, b in pairs for pair in ((a, b), (b, a))])
        for value, pairs in zip((one, two), rounds)
    )


def shards(
    features,
    conv_weight,
    conv_bias,
    head_weight,
    head_bias,
    fragments,
    edge_cells,
    edge_owner,
    edge_count,
    recv_slot,
):
    axes = ("gx", "gy", "gz")
    size = {axis: lax.axis_size(axis) for axis in axes}
    at = {axis: lax.axis_index(axis) for axis in axes}
    devices = size["gx"] * size["gy"] * size["gz"]
    capacity = recv_slot.shape[1] // devices
    slots = edge_cells.shape[1]
    own_slots = devices * capacity // 4
    flags = []
    for axis in axes:
        flags += [at[axis], size[axis] - 1 - at[axis], at[axis] % 2]
    flags = jnp.stack(flags + [edge_count[0]]).astype(jnp.int32)

    xt_low, xt_high, z_one, z_two, end_one, end_two = pl.pallas_call(
        layout_kernel,
        out_shape=(shape((LANES, WIDE), BF),) * 2
        + (shape((LANES, HEAD), BF),) * 2
        + (shape((LANES, WIDE - HEAD), BF),) * 2,
        in_specs=[SMEM, pl.BlockSpec(memory_space=pltpu.HBM)],
        out_specs=(VMEM,) * 6,
        scratch_shapes=[pltpu.VMEM(features.shape, BF), pltpu.SemaphoreType.DMA((8,))],
        compiler_params=pltpu.CompilerParams(vmem_limit_bytes=28 << 20),
        cost_estimate=pl.CostEstimate(flops=1_000_000, bytes_accessed=1 << 17, transcendentals=0),
        name="layout",
    )(flags, pltpu.with_memory_space_constraint(features, pltpu.HBM))
    plane_one, plane_two = swap(z_one, z_two, "gz", False)
    acc, inner, outer = call(
        own_kernel,
        "own_planes",
        (shape((GROUPS, LANES, 256), F32), shape((3, 512, 256), BF), shape((2, 256, 3 * LANES), BF)),
        (xt_low, xt_high, conv_weight, conv_bias.reshape(1, -1)),
        0,
        [pltpu.VMEM((27, 32, LANES), BF), pltpu.VMEM((STEP * STACK + 8, 768), F32)],
        flops=300_000_000,
    )
    x_sent = call(
        face_kernel,
        "faces",
        (shape((2 * LANES + 16, LANES), BF),) * (1 if size["gx"] == 2 else 2),
        (xt_low, xt_high, fragments, flags),
        1,
    )
    x_got = swap(x_sent[0], x_sent[-1], "gx", True)

    owner = edge_owner.reshape(1, slots)
    rank_hot, column_hot, group, name_hot, own_counts, plain, y_code, edge, first_col = call(
        ahead_kernel,
        "ahead",
        (
            shape((2, LANES, slots), BF),
            shape((4 * F, 2 * slots), BF),
            shape((devices, LANES), jnp.int32),
            shape((LANES, devices * LANES), BF),
            shape((F, F), F32),
            shape((2, LANES, LANES), F32),
            shape((2, LANES, LANES), F32),
            shape((4, EDGE, LANES), BF),
            shape((2, LANES), F32),
        ),
        (edge_cells, owner, recv_slot, fragments, xt_low, xt_high),
        0,
        [
            pltpu.VMEM((devices, LANES), jnp.int32),
            pltpu.VMEM((2, F, 4096), F8),
            pltpu.VMEM((2, F, 4096), F8),
            pltpu.VMEM((4, EDGE, LANES), F32),
        ],
        flops=75_000_000,
    )
    *x_got, group = lax.optimization_barrier((*x_got, group))
    face, x_code, y_one, y_two = call(
        x_face_kernel,
        "x_face",
        (
            shape((2, LANES, LANES), BF),
            shape((2, 1, LANES), F32),
            shape((2, EDGE, LANES), BF),
            shape((2, EDGE, LANES), BF),
        ),
        (*x_got, edge, flags),
        1,
    )
    *y_got, outer = lax.optimization_barrier((*swap(y_one, y_two, "gy", True), outer))
    y_low, y_high, ring_one, ring_two = call(
        ring_kernel,
        "ring",
        (shape((2, EDGE, LANES), BF),) * 2 + (shape((RING + LANES, LANES), BF),) * 2,
        (face, *y_got, fragments, flags),
        1,
    )
    ring_one, ring_two = swap(ring_one, ring_two, "gz", False)

    lines, ends, counts = call(
        edge_kernel,
        "edges",
        (shape((2, GROUPS, 256), F32), shape((2, LANES, 256), F32), shape((F, 4 * F), F32)),
        (face, y_low, y_high, inner, plain, x_code, first_col, own_counts, flags),
        1,
        flops=50_000_000,
    )

    end_one, end_two, counts = lax.optimization_barrier((end_one, end_two, counts))
    end_two, plane_one = lax.optimization_barrier((end_two, plane_one))
    end_one, end_two = swap(end_one, end_two, "gz", False)

    def stack_scratch(tiles, kept_lines):
        return [
            pltpu.VMEM((2, LANES, tiles * LANES), BF),
            pltpu.VMEM((min(2, kept_lines // 32), 2, STEP * STACK + 8, 3 * LANES), F32),
            pltpu.VMEM((6, kept_lines, LANES), F32),
        ]

    done = call(
        first_kernel,
        "first_lines",
        (
            shape((3, 2, HEAD_LINES, LANES), BF),
            shape((2, HEAD_LINES, LANES), F32),
            shape((F, 3 * F), F32),
            shape((F, 2 * F), F32),
            shape((F, F), F32),
            shape((2, 2, GROUPS, LANES), F32),
            shape((LANES, LANES), F32),
            shape((4, LANES, LANES), BF),
        ),
        (
            acc,
            plane_one,
            plane_two,
            ring_one,
            ring_two,
            lines,
            ends,
            outer,
            head_weight,
            plain,
            y_code,
            x_code,
            head_bias,
            flags,
        ),
        2,
        stack_scratch(HEAD_GROUPS + 1, HEAD_LINES),
        flops=6_000_000_000,
    )
    affinity, outgoing = call(
        second_kernel,
        "last_lines",
        (shape((3, 2, LANES, LANES), BF), shape((devices, 1, LANES), F32)),
        (
            acc,
            end_one,
            end_two,
            ends,
            outer,
            head_weight,
            plain,
            y_code,
            y_low,
            first_col,
            counts,
            *done,
            edge_cells,
            owner,
            rank_hot,
            column_hot,
            head_bias,
            flags,
        ),
        2,
        stack_scratch(TILES - HEAD_GROUPS, LANES - HEAD_LINES),
        flops=3_000_000_000,
    )
    received = lax.all_to_all(outgoing, axes, split_axis=0, concat_axis=0, tiled=True)
    edge_mean = call(
        settle_kernel,
        "settle",
        shape((1, own_slots), F32),
        (received, group, name_hot),
        0,
        [pltpu.VMEM((16, devices * LANES), BF)],
    )
    return affinity, edge_mean


def solution(mesh):
    in_specs = (
        P(None, "gz", "gx", "gy"),
        P(),
        P(),
        P(),
        P(),
        P("gz", "gx", "gy"),
        P(None, ("gx", "gy", "gz")),
        P(("gx", "gy", "gz"), None),
        P(("gx", "gy", "gz")),
        P(("gx", "gy", "gz"), None),
    )
    out_specs = (P(None, "gz", "gx", "gy"), P(("gx", "gy", "gz"), None))
    return jax.shard_map(shards, mesh=mesh, in_specs=in_specs, out_specs=out_specs, check_vma=False)
```

```python
import jax
import jax.numpy as jnp
from jax import lax
from jax.experimental import pallas as pl
from jax.experimental.pallas import tpu as pltpu
from jax.sharding import PartitionSpec as P

F = 64
LANES = 128
GROUPS = 32
TILES = GROUPS + 1
WIDE = TILES * LANES
STACK = 8
STEP = LANES + 8
EDGE = 48
HALF = LANES // 2
RING = HALF + 2 * EDGE
PART = 32
HEAD_STACKS = 3
HEAD_GROUPS = HEAD_STACKS * STACK
HEAD = (HEAD_GROUPS + 1) * LANES
HEAD_LINES = 4 * HEAD_GROUPS
BF = jnp.bfloat16
F32 = jnp.float32
F8 = jnp.float8_e4m3fn
VMEM = pl.BlockSpec(memory_space=pltpu.VMEM)
SMEM = pl.BlockSpec(memory_space=pltpu.SMEM)


def call(kernel, name, out_shape, args, smem, scratch=(), flops=1_000_000):
    return pl.pallas_call(
        kernel,
        out_shape=out_shape,
        in_specs=[VMEM] * (len(args) - smem) + [SMEM] * smem,
        out_specs=jax.tree.map(lambda _: VMEM, out_shape),
        scratch_shapes=list(scratch),
        compiler_params=pltpu.CompilerParams(vmem_limit_bytes=28 << 20),
        cost_estimate=pl.CostEstimate(flops=flops, bytes_accessed=1 << 17, transcendentals=0),
        name=name,
    )(*args)


def shape(dims, dtype):
    return jax.ShapeDtypeStruct(dims, dtype)


def iota(dims, axis):
    return lax.broadcasted_iota(jnp.int32, dims, axis)


X_LOW, X_HIGH, X_ODD, Y_LOW, Y_HIGH, Y_ODD, Z_LOW, Z_HIGH, Z_ODD, LIVE = range(10)


def outer_product(left, right):
    return lax.dot_general(left, right, (((1,), (1,)), ((), ())), preferred_element_type=F32)


def halves(value):
    high = value.astype(BF)
    return high, (value - high.astype(F32)).astype(BF)


def layout_kernel(flags, feat_hbm, low, high, z_one, z_two, end_one, end_two, feat, sems):
    copies = []
    for t in range(8):
        lines = slice(16 * t, 16 * t + 16)
        copies.append(pltpu.make_async_copy(feat_hbm.at[:, :, lines, :], feat.at[:, :, lines, :], sems.at[t]))
        copies[-1].start()
    odd = flags[Z_ODD] > 0
    zero = jnp.zeros((32, LANES), BF)
    last = [zero, zero]
    for t in range(9):
        if t < 8:
            copies[t].wait()
        both = []
        for z, plane in ((0, low), (1, high)):
            if t < 8:
                block = jnp.swapaxes(feat[:, z, 16 * t : 16 * t + 16, :], 0, 1).reshape(512, LANES)
                turned = jnp.concatenate([last[z], block[:480]], axis=0).T
                last[z] = block[480:]
            else:
                turned = jnp.concatenate([last[z], zero, zero, zero], axis=0).T
            wide = turned.shape[1]
            plane[:, 512 * t : 512 * t + wide] = turned
            both.append(turned)
        for head, end, value in (
            (z_one, end_one, jnp.where(odd, both[0], both[1])),
            (z_two, end_two, jnp.where(odd, both[1], both[0])),
        ):
            cut = min(max(HEAD - 512 * t, 0), wide)
            if cut > 0:
                head[:, 512 * t : 512 * t + cut] = value[:, :cut]
            if cut < wide:
                end[:, 512 * t + cut - HEAD : 512 * t + wide - HEAD] = value[:, cut:]


def face_kernel(low, high, frag, flags, *outs):
    odd = flags[X_ODD] > 0
    for z, plane in ((0, low), (1, high)):
        lines = slice(LANES * z, LANES * (z + 1))
        start, end = plane[:, :LANES], plane[:, WIDE - LANES :]
        for out, pair in zip(outs, ((start, end), (end, start))):
            out[lines, :] = jnp.where(odd, *pair)
    lines = [jnp.broadcast_to(frag[z, 127:128, :], (8, LANES)).astype(F32) for z in range(2)]
    lines = jnp.concatenate(lines, axis=0).astype(BF)
    for out in outs:
        out[2 * LANES :, :] = lines


def line_kernel(low, high, frag, edge, first_col, rows):
    for z, plane in ((0, low), (1, high)):
        turned = frag[z].astype(F32).T
        first_col[z : z + 1, :] = turned[0:1]
        for side, line in ((0, plane[112:128, :].astype(F32)[15:16]), (1, plane[0:16, :].astype(F32)[0:1])):
            for q in range(TILES):
                rows[2 * side + z, q : q + 1, :] = line[:, LANES * q : LANES * (q + 1)]
            rows[2 * side + z, TILES:EDGE, :] = jnp.broadcast_to(turned[127:128], (EDGE - TILES, LANES))
            edge[2 * side + z] = rows[2 * side + z].astype(BF)


def x_face_kernel(got_one, got_two, edge, flags, face, x_code, y_one, y_two):
    has_low, has_high, odd = flags[X_LOW] > 0, flags[X_HIGH] > 0, flags[X_ODD] > 0
    y_odd = flags[Y_ODD] > 0
    lane = iota((LANES, LANES), 1)
    is_low = (lane < 32) & has_low
    is_high = (lane >= 32) & (lane < 64) & has_high
    none = jnp.zeros((LANES, LANES), BF)
    row, place = iota((EDGE, LANES), 0), iota((EDGE, LANES), 1)
    ends = ((row == 0) & (place < 32)) | ((row == TILES - 1) & (place >= 32) & (place < 64))
    other = jnp.where(odd, got_one[2 * LANES :, :], got_two[2 * LANES :, :]).astype(F32)
    for z in range(2):
        lines = slice(LANES * z, LANES * (z + 1))
        low = jnp.where(odd, got_one[lines, :], got_two[lines, :])
        high = jnp.where(odd, got_two[lines, :], got_one[lines, :])
        tile = jnp.where(is_low, low, jnp.where(is_high, high, none))
        face[z] = tile
        patched = []
        for side in range(2):
            near = (tile[112:128].astype(F32)[15:16], tile[0:16].astype(F32)[0:1])[side]
            line = edge[2 * side + z].astype(F32)
            patched.append(jnp.where(ends, jnp.broadcast_to(near, (EDGE, LANES)), line).astype(BF))
        y_one[z] = jnp.where(y_odd, patched[1], patched[0])
        y_two[z] = jnp.where(y_odd, patched[0], patched[1])
        x_code[z] = jnp.where(has_low, other[8 * z : 8 * z + 1], -1.0)


def ring_kernel(face, got_one, got_two, frag, flags, y_low, y_high, z_one, z_two):
    odd, z_odd = flags[Y_ODD] > 0, flags[Z_ODD] > 0
    none = jnp.zeros((EDGE, LANES), BF)
    rings = []
    for z in range(2):
        low = jnp.where(flags[Y_LOW] > 0, jnp.where(odd, got_one[z], got_two[z]), none)
        high = jnp.where(flags[Y_HIGH] > 0, jnp.where(odd, got_two[z], got_one[z]), none)
        y_low[z] = low
        y_high[z] = high
        tile = face[z]
        folded = jnp.where(iota((HALF, LANES), 1) < HALF, tile[:HALF], pltpu.roll(tile[HALF:], HALF, 1))
        rings.append(jnp.concatenate([folded, low, high], axis=0))
    z_one[:RING, :] = jnp.where(z_odd, rings[0], rings[1])
    z_two[:RING, :] = jnp.where(z_odd, rings[1], rings[0])
    top = frag[1].astype(F32).astype(BF)
    for out in (z_one, z_two):
        out[RING:, :] = top


def banded(weight, z_off, dy, slot, quarter):
    tile = jnp.zeros((32, LANES), BF)
    if abs(z_off) <= 1:
        for q in range(4):
            dx = slot - 1 - q
            if abs(dx) <= 1:
                tile = jnp.where(quarter == q, weight[9 * (z_off + 1) + 3 * (dx + 1) + dy], tile)
    return tile


def own_kernel(low, high, conv_weight, conv_bias, acc, inner, outer, weight, scr):
    quarter = iota((32, LANES), 1) // 32
    for k in range(27):
        one = conv_weight[k].astype(F32).T.astype(BF)
        weight[k] = jnp.concatenate([one] * 4, axis=1)
    for dy in range(3):
        for slot in range(8):
            for z in range(2):
                line = slice(256 * z + 32 * slot, 256 * z + 32 * slot + 32)
                for zo in range(2):
                    inner[dy, line, LANES * zo : LANES * (zo + 1)] = banded(weight, z - zo, dy, slot, quarter)
                outer[z, 32 * slot : 32 * slot + 32, LANES * dy : LANES * (dy + 1)] = banded(
                    weight, 2 * z - 1, dy, slot, quarter
                )
    bias = jnp.concatenate([conv_bias[...]] * 8, axis=1)
    for g in range(STACK):
        scr[STEP * g + 7 : STEP * g + 8, :] = jnp.zeros((1, 768), F32)
        scr[STEP * g + STEP : STEP * g + STEP + 1, :] = jnp.zeros((1, 768), F32)

    def body(s, _):
        base = s * STACK
        left = jnp.concatenate(
            [
                jnp.concatenate(
                    [plane[:, pl.ds(pl.multiple_of((base + g) * LANES, LANES), 2 * LANES)] for g in range(STACK)],
                    axis=0,
                )
                for plane in (low, high)
            ],
            axis=1,
        )
        for dy in range(3):
            part = jnp.dot(left, inner[dy], preferred_element_type=F32)
            for g in range(STACK):
                scr[STEP * g + 8 : STEP * g + STEP, 256 * dy : 256 * dy + 256] = part[LANES * g : LANES * (g + 1)]
        for g in range(STACK):
            o = STEP * g
            acc[base + g] = (
                scr[o + 7 : o + 135, 0:256] + scr[o + 8 : o + 136, 256:512] + scr[o + 9 : o + 137, 512:768] + bias
            )
        return 0

    lax.fori_loop(0, GROUPS // STACK, body, 0)


def line_windows(chunks):
    wide = chunks.astype(F32)
    return jnp.concatenate([wide[:GROUPS], wide[1:TILES]], axis=1).astype(BF)


def edge_kernel(
    face, y_low, y_high, inner, plain, x_code, first_col, own_counts, flags, lines, ends, counts
):
    for side, (dy, source) in enumerate(((0, y_low), (2, y_high))):
        left = jnp.concatenate([line_windows(source[z]) for z in range(2)], axis=1)
        lines[side] = jnp.dot(left, inner[dy], preferred_element_type=F32)
    row = iota((LANES, 256), 0)
    lane = iota((LANES, LANES), 1)
    none = jnp.zeros((LANES, LANES), BF)
    for end in range(2):
        keep = lane < 32 if end == 0 else lane >= 32
        tiles = [jnp.where(keep, face[z], none) for z in range(2)]
        parts = []
        for dy in range(3):
            right = [inner[dy, 256 * z + LANES * end : 256 * z + LANES * end + LANES, :] for z in range(2)]
            parts.append(
                jnp.dot(
                    jnp.concatenate(tiles, axis=1), jnp.concatenate(right, axis=0), preferred_element_type=F32
                )
            )
        ends[end] = (
            jnp.where(row == 0, 0.0, pltpu.roll(parts[0], 1, 0))
            + parts[1]
            + jnp.where(row == LANES - 1, 0.0, pltpu.roll(parts[2], LANES - 1, 0))
        )
    ones = [jnp.ones((1, LANES), F32)] * 2
    x_outer = faces_product([plain[z, 0:1, :] for z in range(2)], [x_code[z] for z in range(2)], ones)
    y_outer = faces_product(
        [first_col[z : z + 1, :] for z in range(2)], [y_partner(y_low, z, flags[Y_LOW] > 0) for z in range(2)], ones
    )
    counts[...] = jnp.concatenate([own_counts[...], jnp.zeros((F, F), F32), x_outer, y_outer], axis=1)


def spread(row, copies):
    one = jnp.broadcast_to(row, (16, LANES)).astype(BF)
    return jnp.concatenate([one] * copies, axis=0)


def numbers(rows):
    return iota((rows, LANES), 0).astype(F32).astype(BF)


def line_partners(frag, y_code, x, first, hot_before):
    names = numbers(F)
    line = pl.ds(x, 1)
    hot = [spread(frag[z, line, :], 4) == names for z in range(2)]
    if hot_before is None:
        before = [frag[z, pl.ds(jnp.maximum(x - 1, 0), 1), :] + first for z in range(2)]
        hot_before = [spread(row, 4) == names for row in before]
    y_hot = [spread(y_code[z, line, :], 4) == names for z in range(2)]
    return hot, hot_before, y_hot


def faces_product(own, partner, weight):
    names = numbers(F)
    one, none = jnp.ones((F, LANES), BF), jnp.zeros((F, LANES), BF)
    left = [jnp.where(spread(row, 4) == names, one, none) for row in own]
    right = [jnp.where(spread(row, 4) == names, spread(value, 4), none) for row, value in zip(partner, weight)]
    return outer_product(jnp.concatenate(left, axis=1), jnp.concatenate(right, axis=1))


def load_numbers(frag, plain, y_code):
    lane = iota((LANES, LANES), 1)
    for z in range(2):
        value = frag[z].astype(F32)
        plain[z] = value
        y_code[z] = jnp.where(lane == 0, -1.0, pltpu.roll(value, 1, 1))


def y_partner(y_low, z, has_low):
    return jnp.where(has_low, y_low[z, TILES - 1 :, :].astype(F32)[8:9], -1.0)


def count_kernel(frag, out, plain, y_code, own_hot, pair_hot):
    load_numbers(frag, plain, y_code)
    one = jnp.ones((F, LANES), BF)
    none = jnp.zeros((F, LANES), BF)

    def body(t, total):
        hot_before = None
        first = jnp.where(t > 0, 0.0, -128.0)
        for j in range(32):
            spot = slice(LANES * j, LANES * (j + 1))
            hot, x_hot, y_hot = line_partners(plain, y_code, 32 * t + j, first, hot_before)
            hot_before = hot
            for z in range(2):
                own_hot[z, :, spot] = jnp.where(hot[z], one, none).astype(F8)
                pairs = jnp.where(x_hot[z], one, none) + jnp.where(y_hot[z], one, none)
                if z == 1:
                    pairs = pairs + jnp.where(hot[0], one, none)
                pair_hot[z, :, spot] = pairs.astype(F8)
        for z in range(2):
            total = total + outer_product(own_hot[z], pair_hot[z])
        return total

    out[...] = lax.fori_loop(0, 4, body, jnp.zeros((F, F), F32))


def slots_kernel(cells, owner, recv, rank_hot, column_hot, group, name_hot, place):
    slots = owner.shape[1]
    devices = group.shape[0]
    capacity = recv.shape[1] // devices
    hot = iota((devices, slots), 0) == owner[...]
    before = iota((slots, slots), 0) < iota((slots, slots), 1)
    earlier = jnp.dot(
        jnp.where(hot, 1.0, 0.0).astype(BF), jnp.where(before, 1.0, 0.0).astype(BF), preferred_element_type=F32
    )
    rank = jnp.sum(jnp.where(hot, earlier, 0.0), axis=0, keepdims=True).astype(jnp.int32)
    lanes = iota((LANES, slots), 0)
    rank_hot[0] = jnp.where(lanes == rank, 1.0, 0.0).astype(BF)
    rank_hot[1] = jnp.where(lanes == rank + F, 1.0, 0.0).astype(BF)
    code = jnp.concatenate([cells[0:1, :], cells[1:2, :]], axis=1)
    column_hot[...] = jnp.where(iota((4 * F, 2 * slots), 0) == (code & (4 * F - 1)), 1.0, 0.0).astype(BF)
    place[...] = jnp.full(place.shape, -4 * LANES, jnp.int32)
    for p in range(devices):
        piece = recv[:, capacity * p : capacity * (p + 1)]
        place[p : p + 1, 0:capacity] = piece
        place[p : p + 1, F : F + capacity] = piece
    group[...] = place[...] >> 7
    names = iota((LANES, LANES), 0)

    def body(p, _):
        spot = pl.ds(pl.multiple_of(p * LANES, LANES), LANES)
        name_hot[:, spot] = jnp.where((place[pl.ds(p, 1), :] & (LANES - 1)) == names, 1.0, 0.0).astype(BF)
        return 0

    lax.fori_loop(0, devices, body, 0, unroll=8)


def ahead_kernel(
    cells,
    owner,
    recv,
    frag,
    low,
    high,
    rank_hot,
    column_hot,
    group,
    name_hot,
    counts,
    plain,
    y_code,
    edge,
    first_col,
    place,
    own_hot,
    pair_hot,
    rows,
):
    line_kernel(low, high, frag, edge, first_col, rows)
    count_kernel(frag, counts, plain, y_code, own_hot, pair_hot)
    slots_kernel(cells, owner, recv, rank_hot, column_hot, group, name_hot, place)


def head_rows(head_weight):
    line, spot = iota((8, 256), 0), iota((8, 256), 1)
    head = []
    for d in range(3):
        weights = jnp.concatenate([head_weight[d : d + 1, :].astype(F32)] * 8, axis=1)
        for z in range(2):
            match = (spot // LANES == z) & ((spot // 32) % 4 == line % 4)
            head.append(jnp.where(match, jnp.broadcast_to(weights, (8, 256)), 0.0))
    return jnp.concatenate(head, axis=0).astype(BF)


def stack_affinity(groups, tile, acc, add, planes, outer, lines, head, head_bias, scr, kept, kept_at):
    for i in range(2):
        left = jnp.concatenate(
            [
                planes[i, :, (tile + g) * LANES : (tile + g + 2) * LANES]
                for g in range(STACK)
            ],
            axis=0,
        )
        part = jnp.dot(left, outer[i], preferred_element_type=F32)
        ends = [lines[side, i, groups, :] for side in range(2)]
        for g in range(STACK):
            o = STEP * g
            scr[i, o + 8 : o + STEP, :] = part[LANES * g : LANES * (g + 1)]
            scr[i, o + 7 : o + 8, 0:LANES] = ends[0][g : g + 1]
            scr[i, o + STEP : o + STEP + 1, 2 * LANES :] = ends[1][g : g + 1]
    hidden = []
    for g in range(STACK):
        o = STEP * g
        outside = [
            scr[i, o + 7 : o + 135, 0:LANES]
            + scr[i, o + 8 : o + 136, LANES : 2 * LANES]
            + scr[i, o + 9 : o + 137, 2 * LANES :]
            for i in range(2)
        ]
        total = acc(g) + jnp.concatenate(outside, axis=1)
        if add[g] is not None:
            total = total + add[g]
        hidden.append(jnp.maximum(total, 0.0).astype(BF))
    logits = outer_product(head, jnp.concatenate(hidden, axis=0))
    top_half = iota((8, LANES), 0) < 4
    for i in range(6):
        for pair in range(STACK // 2):
            at = 2 * LANES * pair
            both = logits[8 * i : 8 * i + 8]
            value = jnp.where(top_half, both[:, at : at + LANES], both[:, at + LANES : at + 2 * LANES])
            value = jax.nn.sigmoid(value + head_bias[i // 2]).astype(BF).astype(F32)
            kept[i, kept_at + 8 * pair : kept_at + 8 * pair + 8, :] = value


def table_pieces(x0, kept_at, plain, y_code, z_code, kept, lines):
    names, one, none = numbers(F), jnp.ones((F, LANES), BF), jnp.zeros((F, LANES), BF)
    low, high = jnp.zeros((3 * F, F), F32), jnp.zeros((2 * F, F), F32)
    def one_hot(row):
        return jnp.where(spread(row, 4) == names, one, none)

    before = None
    for t in range(lines // PART):
        own_rows, pair_rows = [[], []], [[], []]
        for j in range(PART):
            at = PART * t + j
            x = x0 + at
            line = slice(x, x + 1)
            weight = [spread(kept[i, kept_at + at : kept_at + at + 1, :], 4) for i in range(6)]
            hot = [one_hot(plain[z, line, :]) for z in range(2)]
            if before is None:
                before = [one_hot(plain[z, x - 1 : x, :]) if x > 0 else none for z in range(2)]
            z_hot = one_hot(z_code[line, :])
            for z in range(2):
                own_rows[z].append(hot[z])
                pair = [before[z] * weight[2 + z] + one_hot(y_code[z, line, :]) * weight[4 + z]]
                pair += [hot[0] * weight[1]] if z else [z_hot * weight[0], z_hot]
                pair_rows[z].append(jnp.concatenate(pair, axis=0))
            before = hot
        parts = [
            outer_product(jnp.concatenate(pair_rows[z], axis=1), jnp.concatenate(own_rows[z], axis=1))
            for z in range(2)
        ]
        low, high = low + parts[0], high + parts[1]
    return low.T, high.T


def first_kernel(
    acc,
    plane_one,
    plane_two,
    ring_one,
    ring_two,
    inner_lines,
    inner_ends,
    outer,
    head_weight,
    plain,
    y_code,
    x_code,
    head_bias,
    flags,
    affinity,
    kept_y,
    low_out,
    high_out,
    x_outer,
    lines,
    z_code,
    carry,
    planes,
    scr,
    kept,
):
    odd = flags[Z_ODD]
    below = jnp.where(odd > 0, ring_one[RING:, :], ring_two[RING:, :])
    z_code[...] = jnp.where(flags[Z_LOW] > 0, below.astype(F32), -1.0)
    lane = iota((LANES, LANES), 1)
    for plane, ring, i in ((plane_one, ring_one, 1 - odd), (plane_two, ring_two, odd)):
        live = jnp.where(i > 0, flags[Z_HIGH], flags[Z_LOW]) > 0
        around = jnp.where(live, ring[:RING, :], jnp.zeros((RING, LANES), BF))
        face = jnp.concatenate([around[:HALF], pltpu.roll(around[:HALF], HALF, 1)], axis=0)
        planes[i, :, LANES:] = plane[:, LANES:HEAD]
        planes[i, :, :LANES] = jnp.where(lane < 32, face, plane[:, :LANES])
        carry[i] = plane[:, HEAD - LANES : HEAD]
        carry[2 + i] = face
        for side, dy in ((0, 0), (1, 2)):
            chunks = around[HALF + EDGE * side : HALF + EDGE * (side + 1), :]
            lines[side, i] = jnp.dot(
                line_windows(chunks), outer[i, :, LANES * dy : LANES * (dy + 1)], preferred_element_type=F32
            )
    for i in range(2):
        for side in range(2):
            lines[side, i] = lines[side, i] + inner_lines[side, :, LANES * i : LANES * (i + 1)]
    head = head_rows(head_weight)

    def affinities(s):
        base, x0 = STACK * s, 4 * STACK * s
        add = [None] * STACK
        if s == 0:
            add[0] = inner_ends[0]
        stack_affinity(
            slice(base, base + STACK), base, lambda g: acc[base + g], add, planes, outer, lines, head, head_bias, scr.at[s % 2], kept, x0
        )
        all_lines = slice(x0, x0 + 4 * STACK)
        for i in range(6):
            affinity[i // 2, i % 2, all_lines, :] = kept[i, all_lines, :].astype(BF)

    affinities(0)
    low, high = jnp.zeros((F, 3 * F), F32), jnp.zeros((F, 2 * F), F32)
    for s in range(HEAD_STACKS):
        if s + 1 < HEAD_STACKS:
            affinities(s + 1)
        x0 = 4 * STACK * s
        more = table_pieces(x0, x0, plain, y_code, z_code, kept, 4 * STACK)
        low, high = low + more[0], high + more[1]
    low_out[...] = low
    high_out[...] = high
    kept_y[...] = kept[4:6]
    x_outer[...] = faces_product(
        [plain[z, 0:1, :] for z in range(2)],
        [x_code[z] for z in range(2)],
        [kept[2 + z, 0:1, :] for z in range(2)],
    )


def second_kernel(
    acc,
    plane_one,
    plane_two,
    inner_ends,
    outer,
    head_weight,
    plain,
    y_code,
    y_low,
    first_col,
    counts,
    affinity_head,
    kept_y,
    low_head,
    high_head,
    x_outer,
    lines,
    z_code,
    carry,
    cells,
    owner,
    rank_hot,
    column_hot,
    head_bias,
    flags,
    affinity,
    outgoing,
    planes,
    scr,
    kept,
):
    odd = flags[Z_ODD]
    lane = iota((LANES, LANES), 1)
    wide = WIDE - HEAD
    for i in range(2):
        planes[i, :, :LANES] = carry[i]
    for plane, i in ((plane_one, 1 - odd), (plane_two, odd)):
        planes[i, :, LANES:wide] = plane[:, : wide - LANES]
        planes[i, :, wide:] = jnp.where((lane >= 32) & (lane < 64), carry[2 + i], plane[:, wide - LANES :])
    add = [None] * STACK
    add[-1] = inner_ends[1]
    groups = pl.ds(HEAD_GROUPS, STACK)
    stack_affinity(
        groups, 0, lambda g: acc[HEAD_GROUPS + g], add, planes, outer, lines, head_rows(head_weight), head_bias, scr.at[0], kept, 0
    )
    for i in range(6):
        affinity[i // 2, i % 2, :HEAD_LINES, :] = affinity_head[i // 2, i % 2]
        affinity[i // 2, i % 2, HEAD_LINES:, :] = kept[i].astype(BF)
    low, high = table_pieces(
        HEAD_LINES, 0, plain, y_code, z_code, kept, LANES - HEAD_LINES
    )
    low, high = low_head[...] + low, high_head[...] + high
    own = low[:, :F] + high[:, :F] + high[:, F:]
    y_outer = faces_product(
        [first_col[z : z + 1, :] for z in range(2)],
        [y_partner(y_low, z, flags[Y_LOW] > 0) for z in range(2)],
        [jnp.concatenate([kept_y[z], kept[4 + z]], axis=0).T[0:1, :] for z in range(2)],
    )
    sums = jnp.concatenate([own, low[:, F : 2 * F], x_outer[...], y_outer], axis=1)
    tally = counts[...] + jnp.concatenate(
        [jnp.zeros((F, F), F32), low[:, 2 * F :], jnp.zeros((F, 2 * F), F32)], axis=1
    )
    slots = cells.shape[1]
    picked = jnp.dot(
        jnp.concatenate(halves(sums) + halves(tally), axis=0), column_hot[...], preferred_element_type=F32
    )
    code = jnp.concatenate([cells[0:1, :], cells[1:2, :]], axis=1)
    line_hot = iota((F, 2 * slots), 0) == (code >> 8)
    alive = iota((1, slots), 1) < flags[LIVE]

    def part_of(value):
        total = jnp.sum(jnp.where(line_hot, value, 0.0), axis=0, keepdims=True)
        return jnp.where(alive, total[:, :slots] + total[:, slots:], 0.0)

    part_sum = part_of(picked[:F] + picked[F : 2 * F])
    part_count = part_of(picked[2 * F : 3 * F] + picked[3 * F :])
    to_owner = iota((outgoing.shape[0], slots), 0) == owner[...]
    left = [
        jnp.where(to_owner, piece.astype(F32), 0.0).astype(BF) for piece in halves(part_sum) + halves(part_count)
    ]
    sent = outer_product(
        jnp.concatenate(left, axis=1),
        jnp.concatenate([rank_hot[0], rank_hot[0], rank_hot[1], rank_hot[1]], axis=1),
    )
    outgoing[...] = sent.reshape(outgoing.shape)


def settle_kernel(received, group_of, name_hot, out, left):
    devices = received.shape[0]
    groups = out.shape[1] // LANES
    row, lane = iota((16, LANES), 0), iota((16, LANES), 1)
    of_count = row >= 2 * groups
    inner = jnp.where(of_count, row - 2 * groups, row)
    is_low = inner >= groups
    group = jnp.where(is_low, inner - groups, inner)
    group = jnp.where((lane >= F) == of_count, group, -1)
    group = jnp.where(row < 4 * groups, group, -1)

    def body(p, _):
        spot = pl.ds(pl.multiple_of(p * LANES, LANES), LANES)
        value = received[p]
        high = value.astype(BF).astype(F32)
        piece = jnp.where(is_low, value - high, high)
        left[:, spot] = jnp.where(group_of[pl.ds(p, 1), :] == group, piece, 0.0).astype(BF)
        return 0

    lax.fori_loop(0, devices, body, 0, unroll=8)
    total = outer_product(left[...], name_hot[...])
    for g in range(groups):
        total_sum = total[g : g + 1] + total[groups + g : groups + g + 1]
        total_count = total[2 * groups + g : 2 * groups + g + 1] + total[3 * groups + g : 3 * groups + g + 1]
        out[:, LANES * g : LANES * (g + 1)] = total_sum / jnp.maximum(total_count, 1.0)


def swap(one, two, axis, closed):
    n = lax.axis_size(axis)
    if n == 1:
        return jnp.zeros_like(one), jnp.zeros_like(two)
    rounds = [[(i, i + 1) for i in range(start, n - 1, 2)] for start in range(2)]
    if n == 2:
        got = lax.ppermute(one, axis, [(0, 1), (1, 0)])
        return got, got
    if closed and n % 2 == 0:
        rounds[1].append((0, n - 1))
    return tuple(
        lax.ppermute(value, axis, [pair for a, b in pairs for pair in ((a, b), (b, a))])
        for value, pairs in zip((one, two), rounds)
    )


def shards(
    features,
    conv_weight,
    conv_bias,
    head_weight,
    head_bias,
    fragments,
    edge_cells,
    edge_owner,
    edge_count,
    recv_slot,
):
    axes = ("gx", "gy", "gz")
    size = {axis: lax.axis_size(axis) for axis in axes}
    at = {axis: lax.axis_index(axis) for axis in axes}
    devices = size["gx"] * size["gy"] * size["gz"]
    capacity = recv_slot.shape[1] // devices
    slots = edge_cells.shape[1]
    own_slots = devices * capacity // 4
    flags = []
    for axis in axes:
        flags += [at[axis], size[axis] - 1 - at[axis], at[axis] % 2]
    flags = jnp.stack(flags + [edge_count[0]]).astype(jnp.int32)

    xt_low, xt_high, z_one, z_two, end_one, end_two = pl.pallas_call(
        layout_kernel,
        out_shape=(shape((LANES, WIDE), BF),) * 2
        + (shape((LANES, HEAD), BF),) * 2
        + (shape((LANES, WIDE - HEAD), BF),) * 2,
        in_specs=[SMEM, pl.BlockSpec(memory_space=pltpu.HBM)],
        out_specs=(VMEM,) * 6,
        scratch_shapes=[pltpu.VMEM(features.shape, BF), pltpu.SemaphoreType.DMA((8,))],
        compiler_params=pltpu.CompilerParams(vmem_limit_bytes=28 << 20),
        cost_estimate=pl.CostEstimate(flops=1_000_000, bytes_accessed=1 << 17, transcendentals=0),
        name="layout",
    )(flags, pltpu.with_memory_space_constraint(features, pltpu.HBM))
    plane_one, plane_two = swap(z_one, z_two, "gz", False)
    acc, inner, outer = call(
        own_kernel,
        "own_planes",
        (shape((GROUPS, LANES, 256), F32), shape((3, 512, 256), BF), shape((2, 256, 3 * LANES), BF)),
        (xt_low, xt_high, conv_weight, conv_bias.reshape(1, -1)),
        0,
        [pltpu.VMEM((27, 32, LANES), BF), pltpu.VMEM((STEP * STACK + 8, 768), F32)],
        flops=300_000_000,
    )
    x_sent = call(
        face_kernel,
        "faces",
        (shape((2 * LANES + 16, LANES), BF),) * (1 if size["gx"] == 2 else 2),
        (xt_low, xt_high, fragments, flags),
        1,
    )
    x_got = swap(x_sent[0], x_sent[-1], "gx", True)

    owner = edge_owner.reshape(1, slots)
    rank_hot, column_hot, group, name_hot, own_counts, plain, y_code, edge, first_col = call(
        ahead_kernel,
        "ahead",
        (
            shape((2, LANES, slots), BF),
            shape((4 * F, 2 * slots), BF),
            shape((devices, LANES), jnp.int32),
            shape((LANES, devices * LANES), BF),
            shape((F, F), F32),
            shape((2, LANES, LANES), F32),
            shape((2, LANES, LANES), F32),
            shape((4, EDGE, LANES), BF),
            shape((2, LANES), F32),
        ),
        (edge_cells, owner, recv_slot, fragments, xt_low, xt_high),
        0,
        [
            pltpu.VMEM((devices, LANES), jnp.int32),
            pltpu.VMEM((2, F, 4096), F8),
            pltpu.VMEM((2, F, 4096), F8),
            pltpu.VMEM((4, EDGE, LANES), F32),
        ],
        flops=75_000_000,
    )
    *x_got, group = lax.optimization_barrier((*x_got, group))
    face, x_code, y_one, y_two = call(
        x_face_kernel,
        "x_face",
        (
            shape((2, LANES, LANES), BF),
            shape((2, 1, LANES), F32),
            shape((2, EDGE, LANES), BF),
            shape((2, EDGE, LANES), BF),
        ),
        (*x_got, edge, flags),
        1,
    )
    *y_got, outer = lax.optimization_barrier((*swap(y_one, y_two, "gy", True), outer))
    y_low, y_high, ring_one, ring_two = call(
        ring_kernel,
        "ring",
        (shape((2, EDGE, LANES), BF),) * 2 + (shape((RING + LANES, LANES), BF),) * 2,
        (face, *y_got, fragments, flags),
        1,
    )
    ring_one, ring_two = swap(ring_one, ring_two, "gz", False)

    lines, ends, counts = call(
        edge_kernel,
        "edges",
        (shape((2, GROUPS, 256), F32), shape((2, LANES, 256), F32), shape((F, 4 * F), F32)),
        (face, y_low, y_high, inner, plain, x_code, first_col, own_counts, flags),
        1,
        flops=50_000_000,
    )

    end_one, end_two, counts = lax.optimization_barrier((end_one, end_two, counts))
    end_two, plane_one = lax.optimization_barrier((end_two, plane_one))
    end_one, end_two = swap(end_one, end_two, "gz", False)

    def stack_scratch(tiles, kept_lines):
        return [
            pltpu.VMEM((2, LANES, tiles * LANES), BF),
            pltpu.VMEM((min(2, kept_lines // 32), 2, STEP * STACK + 8, 3 * LANES), F32),
            pltpu.VMEM((6, kept_lines, LANES), F32),
        ]

    done = call(
        first_kernel,
        "first_lines",
        (
            shape((3, 2, HEAD_LINES, LANES), BF),
            shape((2, HEAD_LINES, LANES), F32),
            shape((F, 3 * F), F32),
            shape((F, 2 * F), F32),
            shape((F, F), F32),
            shape((2, 2, GROUPS, LANES), F32),
            shape((LANES, LANES), F32),
            shape((4, LANES, LANES), BF),
        ),
        (
            acc,
            plane_one,
            plane_two,
            ring_one,
            ring_two,
            lines,
            ends,
            outer,
            head_weight,
            plain,
            y_code,
            x_code,
            head_bias,
            flags,
        ),
        2,
        stack_scratch(HEAD_GROUPS + 1, HEAD_LINES),
        flops=6_000_000_000,
    )
    affinity, outgoing = call(
        second_kernel,
        "last_lines",
        (shape((3, 2, LANES, LANES), BF), shape((devices, 1, LANES), F32)),
        (
            acc,
            end_one,
            end_two,
            ends,
            outer,
            head_weight,
            plain,
            y_code,
            y_low,
            first_col,
            counts,
            *done,
            edge_cells,
            owner,
            rank_hot,
            column_hot,
            head_bias,
            flags,
        ),
        2,
        stack_scratch(TILES - HEAD_GROUPS, LANES - HEAD_LINES),
        flops=3_000_000_000,
    )
    received = lax.all_to_all(outgoing, axes, split_axis=0, concat_axis=0, tiled=True)
    edge_mean = call(
        settle_kernel,
        "settle",
        shape((1, own_slots), F32),
        (received, group, name_hot),
        0,
        [pltpu.VMEM((16, devices * LANES), BF)],
    )
    return affinity, edge_mean


def solution(mesh):
    in_specs = (
        P(None, "gz", "gx", "gy"),
        P(),
        P(),
        P(),
        P(),
        P("gz", "gx", "gy"),
        P(None, ("gx", "gy", "gz")),
        P(("gx", "gy", "gz"), None),
        P(("gx", "gy", "gz")),
        P(("gx", "gy", "gz"), None),
    )
    out_specs = (P(None, "gz", "gx", "gy"), P(("gx", "gy", "gz"), None))
    return jax.shard_map(shards, mesh=mesh, in_specs=in_specs, out_specs=out_specs, check_vma=False)
```
